512 devices in a mesh: ctx: 64 (over x, y, core), kvh: 8 (over z).
Axes of the slice: x: 4, y: 8, z: 8, core: 2. Of those that a mesh axis runs over, the one named last changes fastest.
Arguments:
- queries: bfloat16 [8192, 8, 2, 128], P('ctx', 'kvh'), may hold values from -48 to 48
- keys: bfloat16 [8192, 8, 128], P('ctx', 'kvh'), may hold values from -6 to 6
- values: bfloat16 [8192, 8, 128], P('ctx', 'kvh'), may hold values from -6 to 6
- w_query: float32 [128, 128], replicated, may hold values from -0.5 to 0.5
- w_key: float32 [128, 128], replicated, may hold values from -0.5 to 0.5
Outputs:
- student_out: bfloat16 [8192, 8, 2, 128], P('ctx', 'kvh')
- grad_query: float32 [128, 128], replicated
- grad_key: float32 [128, 128], replicated
- loss: float32 [], replicated
The draws below stay inside these ranges and needn't reach their ends.
All inputs are finite; a program needn't handle non-finite values.
Results may differ from the reference program's by a relative error of at most 0.0035.
Values may be sent and summed in bfloat16 or wider, within the bound.
No kernel may reach another device: no remote copies, remote signals or barrier semaphores. Data moves between devices by JAX's collectives and lax.ppermute only.
A program may use at most 64 MiB of HBM per device.

```python
import jax
import jax.numpy as jnp
from jax import lax

HEAD = 128
FEAT = 256
QPG = 2
TOK_DEV = 128
TOKENS = 8192
KVH = 8


def shared_keys(key):
    normal_part = jax.random.normal(jax.random.fold_in(key, 101), (TOKENS, KVH, HEAD), jnp.float32)
    return normal_part


def draw_keys(key, part):
    normal_part = shared_keys(key)
    base = jnp.clip(normal_part, -6.0, 6.0)
    return base.astype(jnp.bfloat16)


def draw_queries(key, part):
    key = jax.random.fold_in(key, 5)
    shape = (TOKENS, KVH, QPG, HEAD)
    base = jnp.clip(2.0 * jax.random.normal(key, shape, jnp.float32), -12.0, 12.0)
    return base.astype(jnp.bfloat16)


def shard_levels(key, shape, shards, least, largest):
    factor_of = 1.0
    for dim, blocks in shards:
        draws = jax.random.uniform(jax.random.fold_in(jax.random.fold_in(key, 6), dim), (blocks,), jnp.float32, least / len(shards), largest / len(shards))
        factor_of = factor_of * jnp.repeat(jnp.exp(draws), shape[dim] // blocks).reshape((-1,) + (1,) * (len(shape) - 1 - dim))
    return factor_of


def scatter_about(stream_key, dims, deviation, bound, pieces=(), kind=jnp.bfloat16):
    entries = deviation * jax.random.normal(stream_key, dims, jnp.float32)
    if pieces:
        entries = entries * shard_levels(stream_key, dims, pieces, -0.22, 0.18)
    return jnp.clip(entries, -bound, bound).astype(kind)


def setup_inputs(seed: int = 0) -> dict:
    seeds = jax.random.split(jax.random.key(seed), 6)
    queries = draw_queries(jax.random.fold_in(seeds[5], 71), 0)
    keys = draw_keys(jax.random.fold_in(seeds[5], 71), 0)
    values = scatter_about(seeds[2], (TOKENS, KVH, HEAD), 1.0, 6.0, ((0, 64), (1, 8)))
    w_query = scatter_about(seeds[3], (HEAD, FEAT // 2), HEAD ** -0.5, 0.5, (), jnp.float32)
    w_key = scatter_about(seeds[4], (HEAD, FEAT // 2), HEAD ** -0.5, 0.5, (), jnp.float32)
    return dict(queries=queries, keys=keys, values=values, w_query=w_query, w_key=w_key)


HIGH = lax.Precision.HIGHEST

def features(rows, weight):
    pre = jnp.einsum('...h,he->...e', rows.astype(jnp.float32), weight, precision=HIGH)
    return jnp.concatenate([jax.nn.softplus(pre), jax.nn.softplus(-pre)], -1)

def teacher(queries, keys, values):
    length = queries.shape[0]
    block = min(512, length)
    scale = HEAD ** (-0.5)
    heads = []
    for group in range(KVH):
        key_rows = keys[:, group].astype(jnp.float32)
        val_rows = values[:, group].astype(jnp.float32)
        per_head = []
        for head in range(QPG):
            query_rows = queries[:, group, head].astype(jnp.float32).reshape(length // block, block, HEAD)
            starts = (jnp.arange(length // block) * block).astype(jnp.int32)

            def rows_out(item):
                qblock, begin = item
                scores = jnp.dot(qblock, key_rows.T, precision=HIGH) * scale
                allowed = jnp.arange(length)[None, :] <= (begin + jnp.arange(block))[:, None]
                scores = jnp.where(allowed, scores, -1e+30)
                best = scores.max(-1, keepdims=True)
                weights = jnp.where(allowed, jnp.exp(scores - best), 0.0).astype(jnp.bfloat16).astype(jnp.float32)
                return jnp.dot(weights, val_rows, precision=HIGH) / weights.sum(-1, keepdims=True)
            per_head.append(lax.map(rows_out, (query_rows, starts)).reshape(length, HEAD))
        heads.append(jnp.stack(per_head, 1))
    return jnp.stack(heads, 1).astype(jnp.bfloat16)

def student(w_query, w_key, queries, keys, values, targets):
    length = queries.shape[0]
    blocks = length // TOK_DEV
    fq = features(queries, w_query).reshape(blocks, TOK_DEV, KVH, QPG, FEAT)
    fk = features(keys, w_key).reshape(blocks, TOK_DEV, KVH, FEAT)
    vf = values.astype(jnp.float32).reshape(blocks, TOK_DEV, KVH, HEAD)
    causal = (jnp.arange(TOK_DEV)[:, None] >= jnp.arange(TOK_DEV)[None, :])[:, None, None, :]

    def step(carry, item):
        summed, normer = carry
        qf, kf, vb = item
        attn = jnp.where(causal, jnp.einsum('tgpf,ngf->tgpn', qf, kf, precision=HIGH), 0.0)
        num = jnp.einsum('tgpn,ngh->tgph', attn, vb, precision=HIGH) + jnp.einsum('tgpf,gfh->tgph', qf, summed, precision=HIGH)
        den = attn.sum(-1) + jnp.einsum('tgpf,gf->tgp', qf, normer, precision=HIGH)
        summed = summed + jnp.einsum('ngf,ngh->gfh', kf, vb, precision=HIGH)
        normer = normer + kf.sum(0)
        return ((summed, normer), num / den[..., None])
    init = (jnp.zeros((KVH, FEAT, HEAD), jnp.float32), jnp.zeros((KVH, FEAT), jnp.float32))
    _, outs = lax.scan(step, init, (fq, fk, vf))
    outs = outs.reshape(length, KVH, QPG, HEAD)
    diff = outs - targets.astype(jnp.float32)
    loss = jnp.sum(diff * diff) / (length * KVH * QPG)
    return (loss, outs)

def reference(queries, keys, values, w_query, w_key):
    targets = teacher(queries, keys, values)
    (loss, outs), grads = jax.value_and_grad(student, argnums=(0, 1), has_aux=True)(w_query, w_key, queries, keys, values, targets)
    return (outs.astype(jnp.bfloat16), grads[0], grads[1], loss)
```

```python
import functools

import jax
import jax.numpy as jnp
from jax import lax
from jax.experimental import pallas as pl
from jax.experimental.pallas import tpu as pltpu
from jax.sharding import PartitionSpec as P

F32, BF16 = jnp.float32, jnp.bfloat16
NN = (((1,), (0,)), ((), ()))
NT = (((1,), (1,)), ((), ()))
LOG2E = 1.4426950408889634
CORES = 2


def dot(a, b, dims=NN):
    return lax.dot_general(a, b, dims, preferred_element_type=F32)


def halves(a):
    high = a.astype(BF16)
    return high, (a - high.astype(F32)).astype(BF16)


def dot3(a, b, dims=NN):
    ah, al = halves(a)
    bh, bl = halves(b)
    return dot(ah, bh, dims) + (dot(ah, bl, dims) + dot(al, bh, dims))


def dot2(a, b, dims=NN):
    ah, al = halves(a)
    return dot(ah, b, dims) + dot(al, b, dims)


def log1p(e):
    return jnp.where(e < 1e-3, e * (1.0 - e * (0.5 - e * (1.0 / 3.0))), jnp.log(1.0 + e))


def feature_parts(pre):
    e = jnp.exp(-jnp.abs(pre))
    t = log1p(e)
    r = 1.0 / (1.0 + e)
    return jnp.maximum(pre, 0.0) + t, jnp.maximum(-pre, 0.0) + t, jnp.where(pre >= 0.0, r, e * r)


def pair(a):
    return jnp.concatenate([a, a], 1)


def with_ones(v):
    return jnp.concatenate([v, jnp.ones_like(v)], 1)


def fold(q, keys, vals, w2, mrow, accl, state, sig, scale, allowed, full):
    scores = dot(q, keys, NT)
    if allowed is not None:
        scores = jnp.where(allowed, scores, -1e30)
    old = mrow[...]
    new = jnp.maximum(old, scores.max(-1, keepdims=True))
    mrow[...] = new
    c = scale * LOG2E
    weights = jnp.exp2((scores - new) * c).astype(BF16)
    values1 = with_ones(vals)
    accl[...] = accl[...] * jnp.exp2((old - new) * c) + dot(weights, values1)
    pre = dot(w2, pair(keys), NT)
    sp, sm, sig[...] = feature_parts(pre)
    feats = jnp.concatenate([sp, sm], 0)
    if full is not None:
        feats = jnp.where(full, feats, 0.0)
    state[...] += dot2(feats, values1)


def flat(ref, which):
    blocks, rows, head = ref.shape[0], ref.shape[2], ref.shape[3]
    return ref[:, which].reshape(blocks * rows, head)


def place(ny):
    me = lax.axis_index("ctx")
    return me // (ny * CORES), (me // CORES) % ny, me % CORES


def own_plane(ny, scale, q_ref, same_ref, other_ref, wk_ref, m_ref, accl_ref, state_ref, sig_ref):
    _, y, core = place(ny)
    rows = same_ref.shape[2]
    keys_n = ny * rows
    q = q_ref[...]
    w2 = jnp.concatenate(halves(wk_ref[...].T), 1)
    m_ref[...] = jnp.full(m_ref.shape, -1e30, F32)
    accl_ref[...] = jnp.zeros_like(accl_ref)
    state_ref[...] = jnp.zeros_like(state_ref)
    per = q.shape[0] // rows
    col = lax.broadcasted_iota(jnp.int32, (q.shape[0], keys_n), 1)
    row = lax.broadcasted_iota(jnp.int32, (q.shape[0], keys_n), 0) // per
    key = lax.broadcasted_iota(jnp.int32, (1, keys_n), 1)
    fold(
        q, flat(same_ref, 0), flat(same_ref, 1), w2, m_ref, accl_ref, state_ref, sig_ref.at[0], scale,
        col <= row + y * rows, key < y * rows,
    )
    fold(
        q, flat(other_ref, 0), flat(other_ref, 1), w2, m_ref, accl_ref, state_ref, sig_ref.at[1], scale,
        col < (y + core) * rows, key < (y + core) * rows,
    )


def finish(
    ny, shifts, scale, count,
    q_ref, same_ref, other_ref, *rest,
):
    got = rest[: 2 * shifts]
    (wq_ref, wk_ref, m_in, accl_in, state_in, sig_own, out_ref, grad_ref, m_ref, accl_ref, state_ref, sig_ref) = rest[2 * shifts :]
    x, y, core = place(ny)
    rows, head = same_ref.shape[2], same_ref.shape[3]
    keys_n = ny * rows
    q = q_ref[...]
    per = q.shape[0] // rows
    w2 = jnp.concatenate(halves(wk_ref[...].T), 1)
    m_ref[...] = m_in[...]
    accl_ref[...] = accl_in[...]
    state_ref[...] = state_in[...]
    for s in range(1, shifts + 1):

        @pl.when(x >= s)
        def _(s=s):
            for half in range(2):
                ref = got[2 * (s - 1) + half]
                fold(
                    q, flat(ref, 0), flat(ref, 1), w2, m_ref, accl_ref, state_ref,
                    sig_ref.at[2 * (s - 1) + half], scale, None, None,
                )

    accl = accl_ref[...]
    targets = (accl[:, :head] / accl[:, head:]).astype(BF16).astype(F32)
    wq = wq_ref[...]
    wqh, wql = halves(wq)
    sp, sm, _ = feature_parts(dot(q, wqh) + dot(q, wql))
    fq = jnp.concatenate([sp, sm], 1)
    wqt = jnp.concatenate(halves(wq.T), 1)
    sp, sm, sig_q = feature_parts(dot(wqt, pair(q), NT))
    fq_t = jnp.concatenate([sp, sm], 0)
    kd, vd = same_ref[y, 0], same_ref[y, 1]
    sp, sm, sig_d = feature_parts(dot(w2, pair(kd), NT))
    fk_t = jnp.concatenate([sp, sm], 0)
    causal = lax.broadcasted_iota(jnp.int32, (q.shape[0], rows), 1) <= (
        lax.broadcasted_iota(jnp.int32, (q.shape[0], rows), 0) // per
    )
    attn = jnp.where(causal, dot3(fq, fk_t), 0.0)
    state = state_ref[...]
    numden = dot3(fq, state) + dot2(attn, with_ones(vd))
    den = numden[:, head:]
    outs = numden[:, :head] / den
    out_ref[...] = outs.astype(BF16)
    diff = outs - targets
    loss = jnp.sum(diff * diff) / count
    grad_out = diff * (2.0 / count)
    d_num = grad_out / den
    d_den = -jnp.sum(grad_out * outs, -1, keepdims=True) / den
    back = dot3(fq_t, jnp.concatenate([d_num, d_den], 1))
    d_attn = jnp.where(causal, dot2(d_num, vd, NT) + d_den[:, :rows], 0.0)
    lane = lax.broadcasted_iota(jnp.int32, d_den.shape, 1)
    d_aug = jnp.concatenate([d_num, jnp.where(lane == 0, d_den, 0.0)], 1)
    d_fq = dot3(state, d_aug, NT) + dot3(fk_t, d_attn, NT)
    d_pre = d_fq[:head] * sig_q - d_fq[head:] * (1.0 - sig_q)
    grad_q = dot2(d_pre, q)
    d_fk = dot3(fq_t, d_attn)
    d_pre = d_fk[:head] * sig_d - d_fk[head:] * (1.0 - sig_d)
    grad_k = dot2(d_pre, kd)
    both = jnp.concatenate([back[:head, :head] + back[head:, :head], back[head:, :head]], 0)
    both_n = back[:head, head : head + 1] + back[head:, head : head + 1]
    low_n = back[head:, head : head + 1]
    both2 = jnp.concatenate(halves(both), 1)

    def key_grad(keys, vals, sig, full):
        z = dot(both2, pair(vals), NT)
        d_pre = sig * (z[:head] + both_n) - (z[head:] + low_n)
        if full is not None:
            d_pre = jnp.where(full, d_pre, 0.0)
        return dot2(d_pre, keys)

    key = lax.broadcasted_iota(jnp.int32, (1, keys_n), 1)
    grad_k += key_grad(flat(same_ref, 0), flat(same_ref, 1), sig_own[0], key < y * rows)
    grad_k += key_grad(flat(other_ref, 0), flat(other_ref, 1), sig_own[1], key < (y + core) * rows)
    state_ref[:, :head] = jnp.concatenate([grad_q, grad_k], 0)
    for s in range(1, shifts + 1):

        @pl.when(x >= s)
        def _(s=s):
            for half in range(2):
                ref = got[2 * (s - 1) + half]
                state_ref[head:, :head] += key_grad(
                    flat(ref, 0), flat(ref, 1), sig_ref[2 * (s - 1) + half], None
                )

    n = grad_ref.shape[0]
    grads = jnp.concatenate([state_ref[:head, :head].T, state_ref[head:, :head].T], 0)
    parts = 2 * head // n
    for r in range(parts):
        grad_ref[:, r, :] = grads[r * n : (r + 1) * n]
    grad_ref[:, parts, :] = jnp.full((n, head), loss, F32)
    for r in range(parts + 1, grad_ref.shape[1]):
        grad_ref[:, r, :] = jnp.zeros((n, head), F32)


VMEM = pl.BlockSpec(memory_space=pltpu.VMEM)
PARAMS = pltpu.CompilerParams(vmem_limit_bytes=56 * 1024 * 1024)


def spread(a, axis, groups=None, ways=None):
    ways = ways or lax.axis_size(axis)
    copies = jnp.broadcast_to(a[None], (ways, *a.shape))
    return lax.all_to_all(copies, axis, 0, 0, tiled=True, axis_index_groups=groups)


def shards(nx, ny, queries, keys, values, w_query, w_key):
    rows, groups, per, head = queries.shape
    n_ctx, n_kvh = lax.axis_size("ctx"), lax.axis_size("kvh")
    scale = head**-0.5
    count = float(rows * n_ctx * groups * n_kvh * per)
    at = lambda x, y, c: (x * ny + y) * CORES + c
    every = [(x, y, c) for x in range(nx) for y in range(ny) for c in range(CORES)]
    y_groups = [[at(x, y, c) for y in range(ny)] for x in range(nx) for c in range(CORES)]
    swap = [(at(x, y, c), at(x, y, 1 - c)) for x, y, c in every]
    q = queries.reshape(rows * per, head)
    kv = jnp.stack([keys.reshape(rows, head), values.reshape(rows, head)])
    same = spread(kv, "ctx", y_groups, ny)
    got = [
        lax.ppermute(same, "ctx", [(at(x, y, c), at(x + s, y, c)) for x, y, c in every if x + s < nx])
        for s in range(1, nx)
    ]
    other = lax.ppermute(same, "ctx", swap)
    keys_n = ny * rows
    carry = (
        jax.ShapeDtypeStruct((rows * per, 1), F32),
        jax.ShapeDtypeStruct((rows * per, 2 * head), F32),
        jax.ShapeDtypeStruct((2 * head, 2 * head), F32),
        jax.ShapeDtypeStruct((2, head, keys_n), F32),
    )
    carried = pl.pallas_call(
        functools.partial(own_plane, ny, scale),
        out_shape=carry,
        in_specs=[VMEM] * 4,
        out_specs=[VMEM] * 4,
        compiler_params=PARAMS,
        cost_estimate=pl.CostEstimate(flops=3_000_000_000, bytes_accessed=3_000_000, transcendentals=1_000_000),
        name="own_plane",
    )(q, same, other, w_key)
    both = []
    for a in got:
        both += [a, lax.ppermute(a, "ctx", swap)]
    out, grads = pl.pallas_call(
        functools.partial(finish, ny, nx - 1, scale, count),
        out_shape=(
            jax.ShapeDtypeStruct((rows * per, head), BF16),
            jax.ShapeDtypeStruct((n_ctx, 8, head), F32),
        ),
        in_specs=[VMEM] * (9 + len(both)),
        out_specs=[VMEM] * 2,
        scratch_shapes=[
            pltpu.VMEM((rows * per, 1), F32),
            pltpu.VMEM((rows * per, 2 * head), F32),
            pltpu.VMEM((2 * head, 2 * head), F32),
            pltpu.VMEM((2 * (nx - 1), head, keys_n), F32),
        ],
        compiler_params=PARAMS,
        cost_estimate=pl.CostEstimate(flops=9_000_000_000, bytes_accessed=6_000_000, transcendentals=3_000_000),
        name="finish",
    )(q, same, other, *both, w_query, w_key, *carried)
    mine = lax.all_to_all(grads, "ctx", 0, 0, tiled=True).sum(0)
    mine = spread(mine, "kvh").sum(0)
    summed = spread(mine, "ctx")
    parts = 2 * head // n_ctx
    g = summed[:, :parts].transpose(1, 0, 2).reshape(2, head, head)
    return out.reshape(queries.shape), g[0], g[1], summed[0, parts, 0]


def solution(mesh):
    n_ctx = mesh.shape["ctx"]
    ny = min(8, n_ctx // CORES)
    nx = n_ctx // (CORES * ny)
    placed = (P("ctx", "kvh", None, None), P("ctx", "kvh", None), P("ctx", "kvh", None), P(), P())
    return jax.shard_map(
        functools.partial(shards, nx, ny),
        mesh=mesh,
        in_specs=placed,
        out_specs=(P("ctx", "kvh", None, None), P(), P(), P()),
        check_vma=False,
    )
```

```python
import functools

import jax
import jax.numpy as jnp
from jax import lax
from jax.experimental import pallas as pl
from jax.experimental.pallas import tpu as pltpu
from jax.sharding import PartitionSpec as P

F32, BF16 = jnp.float32, jnp.bfloat16
NN = (((1,), (0,)), ((), ()))
NT = (((1,), (1,)), ((), ()))
LOG2E = 1.4426950408889634
CORES = 2


def dot(a, b, dims=NN):
    return lax.dot_general(a, b, dims, preferred_element_type=F32)


def halves(a):
    high = a.astype(BF16)
    return high, (a - high.astype(F32)).astype(BF16)


def dot3(a, b, dims=NN):
    ah, al = halves(a)
    bh, bl = halves(b)
    return dot(ah, bh, dims) + (dot(ah, bl, dims) + dot(al, bh, dims))


def dot2(a, b, dims=NN):
    ah, al = halves(a)
    return dot(ah, b, dims) + dot(al, b, dims)


def log1p(e):
    return jnp.where(e < 1e-3, e * (1.0 - e * (0.5 - e * (1.0 / 3.0))), jnp.log(1.0 + e))


def feature_parts(pre):
    e = jnp.exp(-jnp.abs(pre))
    t = log1p(e)
    r = 1.0 / (1.0 + e)
    return jnp.maximum(pre, 0.0) + t, jnp.maximum(-pre, 0.0) + t, jnp.where(pre >= 0.0, r, e * r)


def pair(a):
    return jnp.concatenate([a, a], 1)


def with_ones(v):
    return jnp.concatenate([v, jnp.ones_like(v)], 1)


def fold(q, keys, vals, w2, mrow, accl, state, sig, scale, allowed, full):
    scores = dot(q, keys, NT)
    if allowed is not None:
        scores = jnp.where(allowed, scores, -1e30)
    old = mrow[...]
    new = jnp.maximum(old, scores.max(-1, keepdims=True))
    mrow[...] = new
    c = scale * LOG2E
    weights = jnp.exp2((scores - new) * c).astype(BF16)
    values1 = with_ones(vals)
    accl[...] = accl[...] * jnp.exp2((old - new) * c) + dot(weights, values1)
    pre = dot(w2, pair(keys), NT)
    sp, sm, sig[...] = feature_parts(pre)
    feats = jnp.concatenate([sp, sm], 0)
    if full is not None:
        feats = jnp.where(full, feats, 0.0)
    state[...] += dot2(feats, values1)


def flat(ref, which):
    blocks, rows, head = ref.shape[0], ref.shape[2], ref.shape[3]
    return ref[:, which].reshape(blocks * rows, head)


def place(ny):
    me = lax.axis_index("ctx")
    return me // (ny * CORES), (me // CORES) % ny, me % CORES


def own_plane(
    ny, scale,
    q_ref, same_ref, other_ref, wq_ref, wk_ref,
    m_ref, accl_ref, state_ref, sig_ref, fq_ref, fqt_ref, sigq_ref, fkd_ref, sigd_ref, near_ref,
):
    _, y, core = place(ny)
    rows = same_ref.shape[2]
    keys_n = ny * rows
    q = q_ref[...]
    w2 = jnp.concatenate(halves(wk_ref[...].T), 1)
    m_ref[...] = jnp.full(m_ref.shape, -1e30, F32)
    accl_ref[...] = jnp.zeros_like(accl_ref)
    state_ref[...] = jnp.zeros_like(state_ref)
    per = q.shape[0] // rows
    col = lax.broadcasted_iota(jnp.int32, (q.shape[0], keys_n), 1)
    row = lax.broadcasted_iota(jnp.int32, (q.shape[0], keys_n), 0) // per
    key = lax.broadcasted_iota(jnp.int32, (1, keys_n), 1)
    fold(
        q, flat(same_ref, 0), flat(same_ref, 1), w2, m_ref, accl_ref, state_ref, sig_ref.at[0], scale,
        col <= row + y * rows, key < y * rows,
    )
    fold(
        q, flat(other_ref, 0), flat(other_ref, 1), w2, m_ref, accl_ref, state_ref, sig_ref.at[1], scale,
        col < (y + core) * rows, key < (y + core) * rows,
    )
    wq = wq_ref[...]
    wqt = jnp.concatenate(halves(wq.T), 1)
    sp, sm, sigq_ref[...] = feature_parts(dot(wqt, pair(q), NT))
    fq_t = jnp.concatenate([sp, sm], 0)
    fqt_ref[...] = fq_t
    fq = fq_t.T
    fq_ref[...] = fq
    kd, vd = same_ref[y, 0], same_ref[y, 1]
    sp, sm, sigd_ref[...] = feature_parts(dot(w2, pair(kd), NT))
    fk_t = jnp.concatenate([sp, sm], 0)
    fkd_ref[...] = fk_t
    attn = jnp.where(diagonal(q.shape[0], rows), dot3(fq, fk_t), 0.0)
    near_ref[...] = dot2(attn, with_ones(vd))


def diagonal(n, rows):
    return lax.broadcasted_iota(jnp.int32, (n, rows), 1) <= (
        lax.broadcasted_iota(jnp.int32, (n, rows), 0) // (n // rows)
    )


def finish(ny, shifts, scale, count, q_ref, same_ref, other_ref, *rest):
    got = rest[: 2 * shifts]
    (
        wk_ref, m_in, accl_in, state_in, sig_own, fq_ref, fqt_ref, sigq_ref, fkd_ref, sigd_ref, near_ref,
        out_ref, grad_ref, m_ref, accl_ref, state_ref, sig_ref, grads_ref,
    ) = rest[2 * shifts :]
    x, y, core = place(ny)
    rows, head = same_ref.shape[2], same_ref.shape[3]
    keys_n = ny * rows
    q = q_ref[...]
    w2 = jnp.concatenate(halves(wk_ref[...].T), 1)
    m_ref[...] = m_in[...]
    accl_ref[...] = accl_in[...]
    state_ref[...] = state_in[...]
    for s in range(1, shifts + 1):

        @pl.when(x >= s)
        def _(s=s):
            for half in range(2):
                ref = got[2 * (s - 1) + half]
                fold(
                    q, flat(ref, 0), flat(ref, 1), w2, m_ref, accl_ref, state_ref,
                    sig_ref.at[2 * (s - 1) + half], scale, None, None,
                )

    accl = accl_ref[...]
    targets = (accl[:, :head] / accl[:, head:]).astype(BF16).astype(F32)
    kd, vd = same_ref[y, 0], same_ref[y, 1]
    fq_t, fk_t, sig_q, sig_d = fqt_ref[...], fkd_ref[...], sigq_ref[...], sigd_ref[...]
    state = state_ref[...]
    numden = dot3(fq_ref[...], state) + near_ref[...]
    den = numden[:, head:]
    outs = numden[:, :head] / den
    out_ref[...] = outs.astype(BF16)
    diff = outs - targets
    loss = jnp.sum(diff * diff) / count
    grad_out = diff * (2.0 / count)
    d_num = grad_out / den
    d_den = -jnp.sum(grad_out * outs, -1, keepdims=True) / den
    back = dot3(fq_t, jnp.concatenate([d_num, d_den], 1))
    d_attn = jnp.where(diagonal(q.shape[0], rows), dot2(d_num, vd, NT) + d_den[:, :rows], 0.0)
    lane = lax.broadcasted_iota(jnp.int32, d_den.shape, 1)
    d_aug = jnp.concatenate([d_num, jnp.where(lane == 0, d_den, 0.0)], 1)
    d_fq = dot3(state, d_aug, NT) + dot3(fk_t, d_attn, NT)
    d_pre = d_fq[:head] * sig_q - d_fq[head:] * (1.0 - sig_q)
    grad_q = dot2(d_pre, q)
    d_fk = dot3(fq_t, d_attn)
    d_pre = d_fk[:head] * sig_d - d_fk[head:] * (1.0 - sig_d)
    grad_k = dot2(d_pre, kd)
    both = jnp.concatenate([back[:head, :head] + back[head:, :head], back[head:, :head]], 0)
    both_n = back[:head, head : head + 1] + back[head:, head : head + 1]
    low_n = back[head:, head : head + 1]
    both2 = jnp.concatenate(halves(both), 1)

    def key_grad(keys, vals, sig, full):
        z = dot(both2, pair(vals), NT)
        d_pre = sig * (z[:head] + both_n) - (z[head:] + low_n)
        if full is not None:
            d_pre = jnp.where(full, d_pre, 0.0)
        return dot2(d_pre, keys)

    key = lax.broadcasted_iota(jnp.int32, (1, keys_n), 1)
    grad_k += key_grad(flat(same_ref, 0), flat(same_ref, 1), sig_own[0], key < y * rows)
    grad_k += key_grad(flat(other_ref, 0), flat(other_ref, 1), sig_own[1], key < (y + core) * rows)
    state_ref[head:, :head] = grad_k
    for s in range(1, shifts + 1):

        @pl.when(x >= s)
        def _(s=s):
            for half in range(2):
                ref = got[2 * (s - 1) + half]
                state_ref[head:, :head] += key_grad(
                    flat(ref, 0), flat(ref, 1), sig_ref[2 * (s - 1) + half], None
                )

    grads_ref[:head] = grad_q.T
    grads_ref[head:] = state_ref[head:, :head].T
    chunks = grad_ref.shape[0] - 2 * head
    parts = 2 * head // chunks
    for r in range(parts):
        grad_ref[pl.ds(r, chunks, stride=parts + 1), :] = grads_ref[pl.ds(r, chunks, stride=parts), :]
    grad_ref[pl.ds(parts, chunks, stride=parts + 1), :] = jnp.full((chunks, head), loss, F32)


VMEM = pl.BlockSpec(memory_space=pltpu.VMEM)
PARAMS = pltpu.CompilerParams(vmem_limit_bytes=56 * 1024 * 1024)


def spread(a, axis, groups=None, ways=None):
    ways = ways or lax.axis_size(axis)
    copies = jnp.broadcast_to(a[None], (ways, *a.shape))
    return lax.all_to_all(copies, axis, 0, 0, tiled=True, axis_index_groups=groups)


def shards(nx, ny, queries, keys, values, w_query, w_key):
    rows, groups, per, head = queries.shape
    n_ctx, n_kvh = lax.axis_size("ctx"), lax.axis_size("kvh")
    scale = head**-0.5
    count = float(rows * n_ctx * groups * n_kvh * per)
    at = lambda x, y, c: (x * ny + y) * CORES + c
    every = [(x, y, c) for x in range(nx) for y in range(ny) for c in range(CORES)]
    y_groups = [[at(x, y, c) for y in range(ny)] for x in range(nx) for c in range(CORES)]
    swap = [(at(x, y, c), at(x, y, 1 - c)) for x, y, c in every]
    q = queries.reshape(rows * per, head)
    kv = jnp.stack([keys.reshape(rows, head), values.reshape(rows, head)])
    same = spread(kv, "ctx", y_groups, ny)
    got = [
        lax.ppermute(same, "ctx", [(at(x, y, c), at(x + s, y, c)) for x, y, c in every if x + s < nx])
        for s in range(1, nx)
    ]
    other = lax.ppermute(same, "ctx", swap)
    n, feats, keys_n = rows * per, 2 * head, ny * rows
    f32 = lambda *shape: jax.ShapeDtypeStruct(shape, F32)
    carried = pl.pallas_call(
        functools.partial(own_plane, ny, scale),
        out_shape=(
            f32(n, 1), f32(n, feats), f32(feats, feats), f32(2, head, keys_n),
            f32(n, feats), f32(feats, n), f32(head, n), f32(feats, rows), f32(head, rows), f32(n, feats),
        ),
        in_specs=[VMEM] * 5,
        out_specs=[VMEM] * 10,
        compiler_params=PARAMS,
        cost_estimate=pl.CostEstimate(flops=3_000_000_000, bytes_accessed=3_000_000, transcendentals=1_000_000),
        name="own_plane",
    )(q, same, other, w_query, w_key)
    got, carried = lax.optimization_barrier((got, carried))
    both = []
    for a in got:
        both += [a, lax.ppermute(a, "ctx", swap)]
    parts = feats // n_ctx
    out, grads = pl.pallas_call(
        functools.partial(finish, ny, nx - 1, scale, count),
        out_shape=(jax.ShapeDtypeStruct((n, head), BF16), f32(n_ctx * (parts + 1), head)),
        in_specs=[VMEM] * (14 + len(both)),
        out_specs=[VMEM] * 2,
        scratch_shapes=[
            pltpu.VMEM((n, 1), F32),
            pltpu.VMEM((n, feats), F32),
            pltpu.VMEM((feats, feats), F32),
            pltpu.VMEM((2 * (nx - 1), head, keys_n), F32),
            pltpu.VMEM((feats, head), F32),
        ],
        compiler_params=PARAMS,
        cost_estimate=pl.CostEstimate(flops=9_000_000_000, bytes_accessed=6_000_000, transcendentals=3_000_000),
        name="finish",
    )(q, same, other, *both, w_key, *carried)
    mine = lax.all_to_all(grads.reshape(n_ctx, 1, -1), "ctx", 0, 0, tiled=True).sum(0)
    mine = spread(mine, "kvh").sum(0)
    g = spread(mine[:, : parts * head], "ctx").reshape(2, head, head)
    return out.reshape(queries.shape), g[0], g[1], mine[0, parts * head]


def solution(mesh):
    n_ctx = mesh.shape["ctx"]
    ny = min(8, n_ctx // CORES)
    nx = n_ctx // (CORES * ny)
    placed = (P("ctx", "kvh", None, None), P("ctx", "kvh", None), P("ctx", "kvh", None), P(), P())
    return jax.shard_map(
        functools.partial(shards, nx, ny),
        mesh=mesh,
        in_specs=placed,
        out_specs=(P("ctx", "kvh", None, None), P(), P(), P()),
        check_vma=False,
    )
```

```python
import functools

import jax
import jax.numpy as jnp
from jax import lax
from jax.experimental import pallas as pl
from jax.experimental.pallas import tpu as pltpu
from jax.sharding import PartitionSpec as P

F32, BF16 = jnp.float32, jnp.bfloat16
NN = (((1,), (0,)), ((), ()))
NT = (((1,), (1,)), ((), ()))
LOG2E = 1.4426950408889634
CORES = 2


def dot(a, b, dims=NN):
    return lax.dot_general(a, b, dims, preferred_element_type=F32)


def halves(a):
    high = a.astype(BF16)
    return high, (a - high.astype(F32)).astype(BF16)


def dot3(a, b, dims=NN):
    ah, al = halves(a)
    bh, bl = halves(b)
    return dot(ah, bh, dims) + (dot(ah, bl, dims) + dot(al, bh, dims))


def dot2(a, b, dims=NN):
    ah, al = halves(a)
    return dot(ah, b, dims) + dot(al, b, dims)


def log1p(e):
    return jnp.where(e < 1e-3, e * (1.0 - e * (0.5 - e * (1.0 / 3.0))), jnp.log(1.0 + e))


def feature_parts(pre):
    e = jnp.exp(-jnp.abs(pre))
    t = log1p(e)
    r = 1.0 / (1.0 + e)
    return jnp.maximum(pre, 0.0) + t, jnp.maximum(-pre, 0.0) + t, jnp.where(pre >= 0.0, r, e * r)


def pair(a):
    return jnp.concatenate([a, a], 1)


def with_ones(v):
    return jnp.concatenate([v, jnp.ones_like(v)], 1)


def flat(ref, which):
    blocks, rows, head = ref.shape[0], ref.shape[2], ref.shape[3]
    return ref[:, which].reshape(blocks * rows, head)


def place(ny):
    me = lax.axis_index("ctx")
    return me // (ny * CORES), (me // CORES) % ny, me % CORES


def diagonal(n, rows):
    return lax.broadcasted_iota(jnp.int32, (n, rows), 1) <= (
        lax.broadcasted_iota(jnp.int32, (n, rows), 0) // (n // rows)
    )


def to_rows(columns, head):
    n = columns[0].shape[0]
    lane = lax.broadcasted_iota(jnp.int32, (n, head), 1)
    wide = jnp.zeros((n, head), F32)
    for i, c in enumerate(columns):
        wide = jnp.where(lane == i, c, wide)
    rows = wide.T[:8]
    return jnp.concatenate([rows[:, k : k + head] for k in range(0, n, head)], 0)


def to_columns(rows, head):
    top = jnp.concatenate([rows[k : k + 8] for k in range(0, rows.shape[0], 8)], 1)
    return jnp.concatenate([top] * (head // 8), 0).T


def prepare(q_ref, kv_ref, wq_ref, wk_ref, fq_ref, fqt_ref, sigq_ref, fkd_ref, sigd_ref, near_ref):
    q, kd, vd = q_ref[...], kv_ref[0], kv_ref[1]
    wqt = jnp.concatenate(halves(wq_ref[...].T), 1)
    w2 = jnp.concatenate(halves(wk_ref[...].T), 1)
    sp, sm, sigq_ref[...] = feature_parts(dot(wqt, pair(q), NT))
    fq_t = jnp.concatenate([sp, sm], 0)
    fqt_ref[...] = fq_t
    fq = fq_t.T
    fq_ref[...] = fq
    sp, sm, sigd_ref[...] = feature_parts(dot(w2, pair(kd), NT))
    fk_t = jnp.concatenate([sp, sm], 0)
    fkd_ref[...] = fk_t
    attn = jnp.where(diagonal(q.shape[0], kd.shape[0]), dot3(fq, fk_t), 0.0)
    near_ref[...] = dot2(attn, with_ones(vd))


def forward(
    nx, ny, scale,
    q_ref, *rest,
):
    later = rest[: nx - 1]
    same_ref, other_ref, wk_ref, m_ref, accl_ref, state_ref, sig_ref, pay_ref, m_s, accl_s, full_s = rest[nx - 1 :]
    x, y, core = place(ny)
    rows, head = same_ref.shape[2], same_ref.shape[3]
    n, keys_n = q_ref.shape[0], ny * rows
    c = scale * LOG2E
    w2 = jnp.concatenate(halves(wk_ref[...].T), 1)
    key = lax.broadcasted_iota(jnp.int32, (1, keys_n), 1)
    kvs = [(flat(same_ref, 0), with_ones(flat(same_ref, 1))), (flat(other_ref, 0), with_ones(flat(other_ref, 1)))]

    def rounded_max(scores):
        return scores.max(-1, keepdims=True).astype(BF16).astype(F32)

    for half, (keys, values1) in enumerate(kvs):
        sp, sm, sig_ref[half] = feature_parts(dot(w2, pair(keys), NT))
        feats = jnp.concatenate([sp, sm], 0)
        seen = jnp.where(key < (y + half * core) * rows, feats, 0.0)
        part, whole = dot2(seen, values1), dot2(feats, values1)
        if half == 0:
            state_ref[...], full_s[...] = part, whole
        else:
            state_ref[...] += part
            full_s[...] += whole

    feats_n = full_s.shape[0]

    def send(s):
        to = x + s
        total = accl_s[:, head : head + 1]
        norm = full_s[:, head : head + 1]
        th, nh = total.astype(BF16).astype(F32), norm.astype(BF16).astype(F32)
        pay_ref[to, :n] = accl_s[:, :head].astype(BF16)
        pay_ref[to, n : n + feats_n] = full_s[:, :head].astype(BF16)
        pay_ref[to, n + feats_n :] = to_rows([m_s[...], th, total - th, nh, norm - nh], head).astype(BF16)

    col = lax.broadcasted_iota(jnp.int32, (n, keys_n), 1)
    row = lax.broadcasted_iota(jnp.int32, (n, keys_n), 0) // (n // rows)
    q = q_ref[...]
    scores = jnp.where(col <= row + y * rows, dot(q, kvs[0][0], NT), -1e30)
    old = rounded_max(scores)
    first = dot(jnp.exp2((scores - old) * c).astype(BF16), kvs[0][1])
    scores = jnp.where(col < (y + core) * rows, dot(q, kvs[1][0], NT), -1e30)
    new = jnp.maximum(old, rounded_max(scores))
    m_ref[...] = new
    accl_ref[...] = first * jnp.exp2((old - new) * c) + dot(jnp.exp2((scores - new) * c).astype(BF16), kvs[1][1])
    for s in range(1, nx):

        @pl.when(x + s < nx)
        def _(s=s):
            q = later[s - 1][...]
            scores = dot(q, kvs[0][0], NT)
            old = rounded_max(scores)
            first = dot(jnp.exp2((scores - old) * c).astype(BF16), kvs[0][1])
            scores = dot(q, kvs[1][0], NT)
            new = jnp.maximum(old, rounded_max(scores))
            m_s[...] = new
            accl_s[...] = first * jnp.exp2((old - new) * c) + dot(
                jnp.exp2((scores - new) * c).astype(BF16), kvs[1][1]
            )
            send(s)

    for d in range(nx):

        @pl.when(d <= x)
        def _(d=d):
            pay_ref[d] = jnp.zeros(pay_ref.shape[1:], BF16)


def merge(
    nx, ny, scale, count,
    m_in, accl_in, state_in, got_ref, fq_ref, fqt_ref, near_ref,
    out_ref, dnum_ref, dden_ref, state_ref, back_ref, pay_ref, loss_ref, m_ref, accl_ref,
):
    x, _, _ = place(ny)
    n, feats_n = fq_ref.shape
    head = out_ref.shape[1]
    c = scale * LOG2E
    m_ref[...] = m_in[...]
    accl_ref[...] = accl_in[...]
    state_ref[...] = state_in[...]
    for s in range(1, nx):

        @pl.when(x >= s)
        def _(s=s):
            columns = to_columns(got_ref[x - s, n + feats_n :].astype(F32), head)
            theirs = columns[:, 0:1]
            total = columns[:, 1:2] + columns[:, 2:3]
            norm = columns[:, 3:4] + columns[:, 4:5]
            old = m_ref[...]
            new = jnp.maximum(old, theirs)
            m_ref[...] = new
            mine, other = jnp.exp2((old - new) * c), jnp.exp2((theirs - new) * c)
            accl_ref[:, :head] = accl_ref[:, :head] * mine + got_ref[x - s, :n].astype(F32) * other
            accl_ref[:, head:] = accl_ref[:, head:] * mine + total * other
            state_ref[:, :head] += got_ref[x - s, n : n + feats_n].astype(F32)
            state_ref[:, head:] += norm

    accl = accl_ref[...]
    targets = (accl[:, :head] / accl[:, head:]).astype(BF16).astype(F32)
    numden = dot3(fq_ref[...], state_ref[...]) + near_ref[...]
    den = numden[:, head:]
    outs = numden[:, :head] / den
    out_ref[...] = outs.astype(BF16)
    diff = outs - targets
    loss_ref[...] = jnp.full(loss_ref.shape, jnp.sum(diff * diff) / count, F32)
    grad_out = diff * (2.0 / count)
    d_num = grad_out / den
    d_den = -jnp.sum(grad_out * outs, -1, keepdims=True) / den
    dnum_ref[...] = d_num
    dden_ref[...] = d_den
    back = dot3(fqt_ref[...], jnp.concatenate([d_num, d_den], 1))
    back_ref[...] = back
    norm = back[:, head : head + 1]
    nh = norm.astype(BF16).astype(F32)
    rows = to_rows([nh, norm - nh], head).astype(BF16)
    for d in range(nx):
        pay_ref[d, :feats_n] = back[:, :head].astype(BF16)
        pay_ref[d, feats_n:] = rows


def near_grads(
    q_ref, kv_ref, dnum_ref, dden_ref, state_ref, fqt_ref, sigq_ref, fkd_ref, sigd_ref, grads_ref
):
    q, kd, vd = q_ref[...], kv_ref[0], kv_ref[1]
    head, rows = kd.shape[1], kd.shape[0]
    d_num, d_den, fq_t, fk_t = dnum_ref[...], dden_ref[...], fqt_ref[...], fkd_ref[...]
    d_attn = jnp.where(diagonal(q.shape[0], rows), dot2(d_num, vd, NT) + d_den[:, :rows], 0.0)
    lane = lax.broadcasted_iota(jnp.int32, d_den.shape, 1)
    d_aug = jnp.concatenate([d_num, jnp.where(lane == 0, d_den, 0.0)], 1)
    d_fq = dot3(state_ref[...], d_aug, NT) + dot3(fk_t, d_attn, NT)
    sig_q, sig_d = sigq_ref[...], sigd_ref[...]
    d_pre = d_fq[:head] * sig_q - d_fq[head:] * (1.0 - sig_q)
    grads_ref[:head] = dot2(d_pre, q)
    d_fk = dot3(fq_t, d_attn)
    d_pre = d_fk[:head] * sig_d - d_fk[head:] * (1.0 - sig_d)
    grads_ref[head:] = dot2(d_pre, kd)


def backward(
    nx, ny,
    same_ref, other_ref, sig_ref, back_in, got_ref, near_ref, loss_ref,
    grad_ref, after_ref, sum_ref,
):
    x, y, core = place(ny)
    rows, head = same_ref.shape[2], same_ref.shape[3]
    keys_n = ny * rows
    feats_n = back_in.shape[0]
    after_ref[...] = jnp.zeros_like(after_ref)
    for s in range(1, nx):

        @pl.when(x + s < nx)
        def _(s=s):
            columns = to_columns(got_ref[x + s, feats_n:].astype(F32), head)
            after_ref[:, :head] += got_ref[x + s, :feats_n].astype(F32)
            after_ref[:, head:] += columns[:, 0:1] + columns[:, 1:2]

    def both(state):
        joint = state[:head] + state[head:]
        mats = jnp.concatenate([joint[:, :head], state[head:, :head]], 0)
        norms = jnp.concatenate([joint[:, head : head + 1], state[head:, head : head + 1]], 0)
        return jnp.concatenate(halves(mats), 1), norms

    own2, own_n = both(back_in[...])
    after2, after_n = both(after_ref[...])
    two = jnp.concatenate([own2, after2], 0)
    key = lax.broadcasted_iota(jnp.int32, (1, keys_n), 1)
    total = near_ref[head:]
    for half, ref in enumerate((same_ref, other_ref)):
        z = dot(two, pair(flat(ref, 1)), NT)
        d = jnp.where(key < (y + half * core) * rows, z[: 2 * head] + own_n, 0.0) + (z[2 * head :] + after_n)
        total += dot2(sig_ref[half] * d[:head] - d[head:], flat(ref, 0))
    sum_ref[:head] = near_ref[:head].T
    sum_ref[head:] = total.T
    chunks = grad_ref.shape[0] - 2 * head
    parts = 2 * head // chunks
    for r in range(parts):
        grad_ref[pl.ds(r, chunks, stride=parts + 1), :] = sum_ref[pl.ds(r, chunks, stride=parts), :]
    grad_ref[pl.ds(parts, chunks, stride=parts + 1), :] = jnp.broadcast_to(loss_ref[0:1], (chunks, head))


VMEM = pl.BlockSpec(memory_space=pltpu.VMEM)
PARAMS = pltpu.CompilerParams(vmem_limit_bytes=56 * 1024 * 1024)


def spread(a, axis, groups=None, ways=None):
    ways = ways or lax.axis_size(axis)
    copies = jnp.broadcast_to(a[None], (ways, *a.shape))
    return lax.all_to_all(copies, axis, 0, 0, tiled=True, axis_index_groups=groups)


def shards(nx, ny, queries, keys, values, w_query, w_key):
    rows, groups, per, head = queries.shape
    n_ctx, n_kvh = lax.axis_size("ctx"), lax.axis_size("kvh")
    scale = head**-0.5
    count = float(rows * n_ctx * groups * n_kvh * per)
    at = lambda x, y, c: (x * ny + y) * CORES + c
    every = [(x, y, c) for x in range(nx) for y in range(ny) for c in range(CORES)]
    y_groups = [[at(x, y, c) for y in range(ny)] for x in range(nx) for c in range(CORES)]
    x_groups = [[at(x, y, c) for x in range(nx)] for y in range(ny) for c in range(CORES)]
    swap = [(at(x, y, c), at(x, y, 1 - c)) for x, y, c in every]
    n, feats, keys_n = rows * per, 2 * head, ny * rows
    f32 = lambda *shape: jax.ShapeDtypeStruct(shape, F32)
    bf16 = lambda *shape: jax.ShapeDtypeStruct(shape, BF16)

    def call(body, outs, args, scratch=(), flops=1, name=None):
        return pl.pallas_call(
            body,
            out_shape=outs,
            in_specs=[VMEM] * len(args),
            out_specs=jax.tree.map(lambda _: VMEM, outs),
            scratch_shapes=[pltpu.VMEM(shape, F32) for shape in scratch],
            compiler_params=PARAMS,
            cost_estimate=pl.CostEstimate(
                flops=flops * 1_000_000_000, bytes_accessed=2_000_000, transcendentals=flops * 300_000
            ),
            name=name,
        )(*args)

    q = queries.reshape(n, head)
    kv = jnp.stack([keys.reshape(rows, head), values.reshape(rows, head)])
    same = spread(kv, "ctx", y_groups, ny)
    later = [
        lax.ppermute(q, "ctx", [(at(x, y, c), at(x - s, y, c)) for x, y, c in every if x >= s])
        for s in range(1, nx)
    ]
    own = call(
        prepare,
        (f32(n, feats), f32(feats, n), f32(head, n), f32(feats, rows), f32(head, rows), f32(n, feats)),
        (q, kv, w_query, w_key), flops=2, name="prepare",
    )
    same, later, (fq, fqt, sigq, fkd, sigd, near) = lax.optimization_barrier((same, later, own))
    other = lax.ppermute(same, "ctx", swap)
    m, accl, state, sig, pay = call(
        functools.partial(forward, nx, ny, scale),
        (f32(n, 1), f32(n, feats), f32(feats, feats), f32(2, head, keys_n), bf16(nx, n + feats + 16, head)),
        (q, *later, same, other, w_key),
        scratch=((n, 1), (n, feats), (feats, feats)), flops=6, name="forward",
    )
    got = lax.all_to_all(pay, "ctx", 0, 0, tiled=True, axis_index_groups=x_groups)
    out, dnum, dden, state, back, pay, loss = call(
        functools.partial(merge, nx, ny, scale, count),
        (bf16(n, head), f32(n, head), f32(n, head), f32(feats, feats), f32(feats, feats), bf16(nx, feats + 16, head), f32(8, head)),
        (m, accl, state, got, fq, fqt, near),
        scratch=((n, 1), (n, feats)), flops=2, name="merge",
    )
    got = lax.all_to_all(pay, "ctx", 0, 0, tiled=True, axis_index_groups=x_groups)
    grads = call(
        near_grads, f32(feats, head), (q, kv, dnum, dden, state, fqt, sigq, fkd, sigd), flops=2, name="near_grads",
    )
    parts = feats // n_ctx
    grads = call(
        functools.partial(backward, nx, ny),
        f32(n_ctx * (parts + 1), head),
        (same, other, sig, back, got, grads, loss),
        scratch=((feats, feats), (feats, head)), flops=4, name="backward",
    )
    mine = lax.all_to_all(grads.reshape(n_ctx, 1, -1), "ctx", 0, 0, tiled=True).sum(0)
    mine = spread(mine, "kvh").sum(0)
    g = spread(mine[:, : parts * head], "ctx").reshape(2, head, head)
    return out.reshape(queries.shape), g[0], g[1], mine[0, parts * head]


def solution(mesh):
    n_ctx = mesh.shape["ctx"]
    ny = min(8, n_ctx // CORES)
    nx = n_ctx // (CORES * ny)
    placed = (P("ctx", "kvh", None, None), P("ctx", "kvh", None), P("ctx", "kvh", None), P(), P())
    return jax.shard_map(
        functools.partial(shards, nx, ny),
        mesh=mesh,
        in_specs=placed,
        out_specs=(P("ctx", "kvh", None, None), P(), P(), P()),
        check_vma=False,
    )
```

```python
import functools

import jax
import jax.numpy as jnp
from jax import lax
from jax.experimental import pallas as pl
from jax.experimental.pallas import tpu as pltpu
from jax.sharding import PartitionSpec as P

F32, BF16 = jnp.float32, jnp.bfloat16
NN = (((1,), (0,)), ((), ()))
NT = (((1,), (1,)), ((), ()))
LOG2E = 1.4426950408889634
CORES = 2


def dot(a, b, dims=NN):
    return lax.dot_general(a, b, dims, preferred_element_type=F32)


def halves(a):
    high = a.astype(BF16)
    return high, (a - high.astype(F32)).astype(BF16)


def dot3(a, b, dims=NN):
    ah, al = halves(a)
    bh, bl = halves(b)
    return dot(ah, bh, dims) + (dot(ah, bl, dims) + dot(al, bh, dims))


def dot2(a, b, dims=NN):
    ah, al = halves(a)
    return dot(ah, b, dims) + dot(al, b, dims)


def log1p(e):
    return jnp.where(e < 1e-3, e * (1.0 - e * (0.5 - e * (1.0 / 3.0))), jnp.log(1.0 + e))


def feature_parts(pre):
    e = jnp.exp(-jnp.abs(pre))
    t = log1p(e)
    r = 1.0 / (1.0 + e)
    return jnp.maximum(pre, 0.0) + t, jnp.maximum(-pre, 0.0) + t, jnp.where(pre >= 0.0, r, e * r)


def pair(a):
    return jnp.concatenate([a, a], 1)


def with_ones(v):
    return jnp.concatenate([v, jnp.ones_like(v)], 1)


def flat(ref, which):
    blocks, rows, head = ref.shape[0], ref.shape[2], ref.shape[3]
    return ref[:, which].reshape(blocks * rows, head)


def place(ny):
    me = lax.axis_index("ctx")
    return me // (ny * CORES), (me // CORES) % ny, me % CORES


def diagonal(n, rows):
    return lax.broadcasted_iota(jnp.int32, (n, rows), 1) <= (
        lax.broadcasted_iota(jnp.int32, (n, rows), 0) // (n // rows)
    )


def to_rows(columns, head):
    n = columns[0].shape[0]
    lane = lax.broadcasted_iota(jnp.int32, (n, head), 1)
    wide = jnp.zeros((n, head), F32)
    for i, c in enumerate(columns):
        wide = jnp.where(lane == i, c, wide)
    rows = wide.T[:8]
    return jnp.concatenate([rows[:, k : k + head] for k in range(0, n, head)], 0)


def to_columns(rows, head):
    top = jnp.concatenate([rows[k : k + 8] for k in range(0, rows.shape[0], 8)], 1)
    return jnp.concatenate([top] * (head // 8), 0).T


def prepare(q_ref, k_ref, v_ref, wq_ref, wk_ref, fq_ref, fqt_ref, sigq_ref, fkd_ref, sigd_ref, near_ref):
    q, kd, vd = q_ref[...], k_ref[...], v_ref[...]
    wqt = jnp.concatenate(halves(wq_ref[...].T), 1)
    w2 = jnp.concatenate(halves(wk_ref[...].T), 1)
    sp, sm, sigq_ref[...] = feature_parts(dot(wqt, pair(q), NT))
    fq_t = jnp.concatenate([sp, sm], 0)
    fqt_ref[...] = fq_t
    fq = fq_t.T
    fq_ref[...] = fq
    sp, sm, sigd_ref[...] = feature_parts(dot(w2, pair(kd), NT))
    fk_t = jnp.concatenate([sp, sm], 0)
    fkd_ref[...] = fk_t
    attn = jnp.where(diagonal(q.shape[0], kd.shape[0]), dot3(fq, fk_t), 0.0)
    near_ref[...] = dot2(attn, with_ones(vd))


def add_states(keys, vals, w2, seen, sig_ref, part, whole):
    rows = part.shape[0] // 2
    sp, sm, sig_ref[...] = feature_parts(dot(w2, pair(keys), NT))
    both = jnp.concatenate([sp, sm], 0)
    for b in range(keys.shape[0] // rows):
        high, low = halves(both[:, b * rows : (b + 1) * rows])
        values1 = with_ones(vals[b * rows : (b + 1) * rows])
        state = dot(jnp.concatenate([high, low], 1), jnp.concatenate([values1, values1], 0))
        whole += state
        part += state * (b < seen).astype(F32)
    return part, whole


def same_core(ny, same_ref, wk_ref, state_ref, full_ref, sig_ref):
    _, y, _ = place(ny)
    w2 = jnp.concatenate(halves(wk_ref[...].T), 1)
    zero = jnp.zeros(state_ref.shape, F32)
    state_ref[...], full_ref[...] = add_states(
        flat(same_ref, 0), flat(same_ref, 1), w2, y, sig_ref, zero, zero
    )


def forward(nx, ny, scale, q_ref, *rest):
    later = rest[: nx - 1]
    (
        same_ref, other_ref, wk_ref, state_in, full_in,
        m_ref, accl_ref, state_ref, sig_ref, pay_ref, m_s, accl_s,
    ) = rest[nx - 1 :]
    x, y, core = place(ny)
    rows, head = same_ref.shape[2], same_ref.shape[3]
    n, keys_n = q_ref.shape[0], ny * rows
    c = scale * LOG2E
    w2 = jnp.concatenate(halves(wk_ref[...].T), 1)
    keys0, values0 = flat(same_ref, 0), with_ones(flat(same_ref, 1))
    keys1, values1 = flat(other_ref, 0), with_ones(flat(other_ref, 1))
    state_ref[...], full = add_states(
        keys1, flat(other_ref, 1), w2, y + core, sig_ref, state_in[...], full_in[...]
    )
    feats_n = full.shape[0]
    full_high = full[:, :head].astype(BF16)
    norm = full[:, head : head + 1]
    norm_high = norm.astype(BF16).astype(F32)

    def teach(q, m_out, accl_out, masks):
        scores0, scores1 = dot(q, keys0, NT), dot(q, keys1, NT)
        if masks is not None:
            scores0 = jnp.where(masks[0], scores0, -1e30)
            scores1 = jnp.where(masks[1], scores1, -1e30)
        best = jnp.maximum(scores0.max(-1, keepdims=True), scores1.max(-1, keepdims=True))
        best = best.astype(BF16).astype(F32)
        m_out[...] = best
        accl_out[...] = dot(jnp.exp2((scores0 - best) * c).astype(BF16), values0) + dot(
            jnp.exp2((scores1 - best) * c).astype(BF16), values1
        )

    col = lax.broadcasted_iota(jnp.int32, (n, keys_n), 1)
    row = lax.broadcasted_iota(jnp.int32, (n, keys_n), 0) // (n // rows)
    teach(q_ref[...], m_ref, accl_ref, (col <= row + y * rows, col < (y + core) * rows))
    for s in range(1, nx):

        @pl.when(x + s < nx)
        def _(s=s):
            teach(later[s - 1][...], m_s, accl_s, None)
            to = x + s
            total = accl_s[:, head : head + 1]
            high = total.astype(BF16).astype(F32)
            pay_ref[to, :n] = accl_s[:, :head].astype(BF16)
            pay_ref[to, n : n + feats_n] = full_high
            pay_ref[to, n + feats_n :] = to_rows(
                [m_s[...], high, total - high, norm_high, norm - norm_high], head
            ).astype(BF16)

    for d in range(nx):

        @pl.when(d <= x)
        def _(d=d):
            pay_ref[d] = jnp.zeros(pay_ref.shape[1:], BF16)


def merge(
    nx, ny, scale, count,
    m_in, accl_in, state_in, got_ref, fq_ref, fqt_ref, near_ref,
    out_ref, dnum_ref, dden_ref, state_ref, back_ref, pay_ref, loss_ref, m_ref, accl_ref,
):
    x, _, _ = place(ny)
    n, feats_n = fq_ref.shape
    head = out_ref.shape[1]
    c = scale * LOG2E
    m_ref[...] = m_in[...]
    accl_ref[...] = accl_in[...]
    state_ref[...] = state_in[...]
    for s in range(1, nx):

        @pl.when(x >= s)
        def _(s=s):
            columns = to_columns(got_ref[x - s, n + feats_n :].astype(F32), head)
            theirs = columns[:, 0:1]
            total = columns[:, 1:2] + columns[:, 2:3]
            norm = columns[:, 3:4] + columns[:, 4:5]
            old = m_ref[...]
            new = jnp.maximum(old, theirs)
            m_ref[...] = new
            mine, other = jnp.exp2((old - new) * c), jnp.exp2((theirs - new) * c)
            accl_ref[:, :head] = accl_ref[:, :head] * mine + got_ref[x - s, :n].astype(F32) * other
            accl_ref[:, head:] = accl_ref[:, head:] * mine + total * other
            state_ref[:, :head] += got_ref[x - s, n : n + feats_n].astype(F32)
            state_ref[:, head:] += norm

    accl = accl_ref[...]
    targets = (accl[:, :head] / accl[:, head:]).astype(BF16).astype(F32)
    numden = dot3(fq_ref[...], state_ref[...]) + near_ref[...]
    den = numden[:, head:]
    outs = numden[:, :head] / den
    out_ref[...] = outs.astype(BF16)
    diff = outs - targets
    loss_ref[...] = jnp.full(loss_ref.shape, jnp.sum(diff * diff) / count, F32)
    grad_out = diff * (2.0 / count)
    d_num = grad_out / den
    d_den = -jnp.sum(grad_out * outs, -1, keepdims=True) / den
    dnum_ref[...] = d_num
    dden_ref[...] = d_den
    back = dot3(fqt_ref[...], jnp.concatenate([d_num, d_den], 1))
    back_ref[...] = back
    norm = back[:, head : head + 1]
    nh = norm.astype(BF16).astype(F32)
    rows = to_rows([nh, norm - nh], head).astype(BF16)
    for d in range(nx):
        pay_ref[d, :feats_n] = back[:, :head].astype(BF16)
        pay_ref[d, feats_n:] = rows


def near_grads(
    q_ref, k_ref, v_ref, dnum_ref, dden_ref, state_ref, fqt_ref, sigq_ref, fkd_ref, sigd_ref, grads_ref
):
    q, kd, vd = q_ref[...], k_ref[...], v_ref[...]
    head, rows = kd.shape[1], kd.shape[0]
    d_num, d_den, fq_t, fk_t = dnum_ref[...], dden_ref[...], fqt_ref[...], fkd_ref[...]
    d_attn = jnp.where(diagonal(q.shape[0], rows), dot2(d_num, vd, NT) + d_den[:, :rows], 0.0)
    lane = lax.broadcasted_iota(jnp.int32, d_den.shape, 1)
    d_aug = jnp.concatenate([d_num, jnp.where(lane == 0, d_den, 0.0)], 1)
    d_fq = dot3(state_ref[...], d_aug, NT) + dot3(fk_t, d_attn, NT)
    sig_q, sig_d = sigq_ref[...], sigd_ref[...]
    d_pre = d_fq[:head] * sig_q - d_fq[head:] * (1.0 - sig_q)
    grads_ref[:head] = dot2(d_pre, q)
    d_fk = dot3(fq_t, d_attn)
    d_pre = d_fk[:head] * sig_d - d_fk[head:] * (1.0 - sig_d)
    grads_ref[head:] = dot2(d_pre, kd)


def backward(
    nx, ny,
    same_ref, other_ref, sig0_ref, sig1_ref, back_in, got_ref, near_ref, loss_ref,
    grad_ref, after_ref, sum_ref,
):
    x, y, core = place(ny)
    rows, head = same_ref.shape[2], same_ref.shape[3]
    keys_n = ny * rows
    feats_n = back_in.shape[0]
    after_ref[...] = jnp.zeros_like(after_ref)
    for s in range(1, nx):

        @pl.when(x + s < nx)
        def _(s=s):
            columns = to_columns(got_ref[x + s, feats_n:].astype(F32), head)
            after_ref[:, :head] += got_ref[x + s, :feats_n].astype(F32)
            after_ref[:, head:] += columns[:, 0:1] + columns[:, 1:2]

    def both(state):
        joint = state[:head] + state[head:]
        mats = jnp.concatenate([joint[:, :head], state[head:, :head]], 0)
        norms = jnp.concatenate([joint[:, head : head + 1], state[head:, head : head + 1]], 0)
        return jnp.concatenate(halves(mats), 1), norms

    own2, own_n = both(back_in[...])
    after2, after_n = both(after_ref[...])
    two = jnp.concatenate([own2, after2], 0)
    key = lax.broadcasted_iota(jnp.int32, (1, keys_n), 1)
    total = near_ref[head:]
    for half, ref, sig_ref in ((0, same_ref, sig0_ref), (1, other_ref, sig1_ref)):
        z = dot(two, pair(flat(ref, 1)), NT)
        d = jnp.where(key < (y + half * core) * rows, z[: 2 * head] + own_n, 0.0) + (z[2 * head :] + after_n)
        total += dot2(sig_ref[...] * d[:head] - d[head:], flat(ref, 0))
    sum_ref[:head] = near_ref[:head].T
    sum_ref[head:] = total.T
    chunks = grad_ref.shape[0] - 2 * head
    parts = 2 * head // chunks
    for r in range(parts):
        grad_ref[pl.ds(r, chunks, stride=parts + 1), :] = sum_ref[pl.ds(r, chunks, stride=parts), :]
    grad_ref[pl.ds(parts, chunks, stride=parts + 1), :] = jnp.broadcast_to(loss_ref[0:1], (chunks, head))


VMEM = pl.BlockSpec(memory_space=pltpu.VMEM)
PARAMS = pltpu.CompilerParams(vmem_limit_bytes=20 * 1024 * 1024)


def spread(a, axis, groups=None, ways=None):
    ways = ways or lax.axis_size(axis)
    copies = jnp.broadcast_to(a[None], (ways, *a.shape))
    return lax.all_to_all(copies, axis, 0, 0, tiled=True, axis_index_groups=groups)


def shards(nx, ny, queries, keys, values, w_query, w_key):
    rows, groups, per, head = queries.shape
    n_ctx, n_kvh = lax.axis_size("ctx"), lax.axis_size("kvh")
    scale = head**-0.5
    count = float(rows * n_ctx * groups * n_kvh * per)
    at = lambda x, y, c: (x * ny + y) * CORES + c
    every = [(x, y, c) for x in range(nx) for y in range(ny) for c in range(CORES)]
    y_groups = [[at(x, y, c) for y in range(ny)] for x in range(nx) for c in range(CORES)]
    x_groups = [[at(x, y, c) for x in range(nx)] for y in range(ny) for c in range(CORES)]
    swap = [(at(x, y, c), at(x, y, 1 - c)) for x, y, c in every]
    n, feats, keys_n = rows * per, 2 * head, ny * rows
    f32 = lambda *shape: jax.ShapeDtypeStruct(shape, F32)
    bf16 = lambda *shape: jax.ShapeDtypeStruct(shape, BF16)

    def call(body, outs, args, scratch=(), flops=1, name=None):
        return pl.pallas_call(
            body,
            out_shape=outs,
            in_specs=[VMEM] * len(args),
            out_specs=jax.tree.map(lambda _: VMEM, outs),
            scratch_shapes=[pltpu.VMEM(shape, F32) for shape in scratch],
            compiler_params=PARAMS,
            cost_estimate=pl.CostEstimate(
                flops=flops * 1_000_000_000, bytes_accessed=2_000_000, transcendentals=flops * 300_000
            ),
            name=name,
        )(*args)

    q = queries.reshape(n, head)
    k, v = keys.reshape(rows, head), values.reshape(rows, head)
    same = spread(jnp.stack([k, v]), "ctx", y_groups, ny)
    later = [
        lax.ppermute(q, "ctx", [(at(x, y, c), at(x - s, y, c)) for x, y, c in every if x >= s])
        for s in range(1, nx)
    ]
    own = call(
        prepare,
        (f32(n, feats), f32(feats, n), f32(head, n), f32(feats, rows), f32(head, rows), f32(n, feats)),
        (q, k, v, w_query, w_key), flops=2, name="prepare",
    )
    same, later, (fq, fqt, sigq, fkd, sigd, near) = lax.optimization_barrier((same, later, own))
    other = lax.ppermute(same, "ctx", swap)
    state, full, sig0 = call(
        functools.partial(same_core, ny),
        (f32(feats, feats), f32(feats, feats), f32(head, keys_n)), (same, w_key), flops=2, name="same_core",
    )
    m, accl, state, sig1, pay = call(
        functools.partial(forward, nx, ny, scale),
        (f32(n, 1), f32(n, feats), f32(feats, feats), f32(head, keys_n), bf16(nx, n + feats + 16, head)),
        (q, *later, same, other, w_key, state, full),
        scratch=((n, 1), (n, feats)), flops=6, name="forward",
    )
    got = lax.all_to_all(pay, "ctx", 0, 0, tiled=True, axis_index_groups=x_groups)
    out, dnum, dden, state, back, pay, loss = call(
        functools.partial(merge, nx, ny, scale, count),
        (bf16(n, head), f32(n, head), f32(n, head), f32(feats, feats), f32(feats, feats), bf16(nx, feats + 16, head), f32(8, head)),
        (m, accl, state, got, fq, fqt, near),
        scratch=((n, 1), (n, feats)), flops=2, name="merge",
    )
    got = lax.all_to_all(pay, "ctx", 0, 0, tiled=True, axis_index_groups=x_groups)
    grads = call(
        near_grads, f32(feats, head), (q, k, v, dnum, dden, state, fqt, sigq, fkd, sigd), flops=2, name="near_grads",
    )
    parts = feats // n_ctx
    grads = call(
        functools.partial(backward, nx, ny),
        f32(n_ctx * (parts + 1), head),
        (same, other, sig0, sig1, back, got, grads, loss),
        scratch=((feats, feats), (feats, head)), flops=4, name="backward",
    )
    mine = lax.all_to_all(grads.reshape(n_ctx, 1, -1), "ctx", 0, 0, tiled=True).sum(0)
    mine = spread(mine, "kvh").sum(0)
    g = spread(mine[:, : parts * head], "ctx").reshape(2, head, head)
    return out.reshape(queries.shape), g[0], g[1], mine[0, parts * head]


def solution(mesh):
    n_ctx = mesh.shape["ctx"]
    ny = min(8, n_ctx // CORES)
    nx = n_ctx // (CORES * ny)
    placed = (P("ctx", "kvh", None, None), P("ctx", "kvh", None), P("ctx", "kvh", None), P(), P())
    return jax.shard_map(
        functools.partial(shards, nx, ny),
        mesh=mesh,
        in_specs=placed,
        out_specs=(P("ctx", "kvh", None, None), P(), P(), P()),
        check_vma=False,
    )
```

```python
import functools

import jax
import jax.numpy as jnp
from jax import lax
from jax.experimental import pallas as pl
from jax.experimental.pallas import tpu as pltpu
from jax.sharding import PartitionSpec as P

F32, BF16 = jnp.float32, jnp.bfloat16
NN = (((1,), (0,)), ((), ()))
NT = (((1,), (1,)), ((), ()))
LOG2E = 1.4426950408889634
CORES = 2


def dot(a, b, dims=NN):
    return lax.dot_general(a, b, dims, preferred_element_type=F32)


def halves(a):
    high = a.astype(BF16)
    return high, (a - high.astype(F32)).astype(BF16)


def dot3(a, b, dims=NN):
    ah, al = halves(a)
    bh, bl = halves(b)
    return dot(ah, bh, dims) + (dot(ah, bl, dims) + dot(al, bh, dims))


def dot2(a, b, dims=NN):
    ah, al = halves(a)
    return dot(ah, b, dims) + dot(al, b, dims)


def log1p(e):
    return jnp.where(e < 1e-3, e * (1.0 - e * (0.5 - e * (1.0 / 3.0))), jnp.log(1.0 + e))


def feature_parts(pre):
    e = jnp.exp(-jnp.abs(pre))
    t = log1p(e)
    r = 1.0 / (1.0 + e)
    return jnp.maximum(pre, 0.0) + t, jnp.maximum(-pre, 0.0) + t, jnp.where(pre >= 0.0, r, e * r)


def pair(a):
    return jnp.concatenate([a, a], 1)


def with_ones(v):
    return jnp.concatenate([v, jnp.ones_like(v)], 1)


def flat(ref, which):
    blocks, rows, head = ref.shape[0], ref.shape[2], ref.shape[3]
    return ref[:, which].reshape(blocks * rows, head)


def place(ny):
    me = lax.axis_index("ctx")
    return me // (ny * CORES), (me // CORES) % ny, me % CORES


def diagonal(n, rows):
    return lax.broadcasted_iota(jnp.int32, (n, rows), 1) <= (
        lax.broadcasted_iota(jnp.int32, (n, rows), 0) // (n // rows)
    )


def to_rows(columns, head):
    n = columns[0].shape[0]
    lane = lax.broadcasted_iota(jnp.int32, (n, head), 1)
    wide = jnp.zeros((n, head), F32)
    for i, c in enumerate(columns):
        wide = jnp.where(lane == i, c, wide)
    rows = wide.T[:8]
    return jnp.concatenate([rows[:, k : k + head] for k in range(0, n, head)], 0)


def to_columns(pages, head):
    rows = [
        jnp.concatenate([page[k : k + 8] for k in range(0, page.shape[0], 8)], 1) for page in pages
    ]
    rows += [rows[0]] * (head // 8 - len(rows))
    return jnp.concatenate(rows, 0).T


def own_features(q, k, wq, wk):
    wqt = jnp.concatenate(halves(wq.T), 1)
    w2 = jnp.concatenate(halves(wk.T), 1)
    sp, sm, sig_q = feature_parts(dot(wqt, pair(q), NT))
    fq_t = jnp.concatenate([sp, sm], 0)
    sp, sm, sig_k = feature_parts(dot(w2, pair(k), NT))
    return fq_t, sig_q, jnp.concatenate([sp, sm], 0), sig_k


def prepare(q_ref, k_ref, v_ref, wq_ref, wk_ref, fq_ref, near_ref):
    q, k, v = q_ref[...], k_ref[...], v_ref[...]
    fq_t, _, fk_t, _ = own_features(q, k, wq_ref[...], wk_ref[...])
    fq = fq_t.T
    fq_ref[...] = fq
    attn = jnp.where(diagonal(q.shape[0], k.shape[0]), dot3(fq, fk_t), 0.0)
    near_ref[...] = dot2(attn, with_ones(v))


def add_states(keys, vals, w2, seen, part, whole):
    rows = part.shape[0] // 2
    sp, sm, _ = feature_parts(dot(w2, pair(keys), NT))
    both = jnp.concatenate([sp, sm], 0)
    for b in range(keys.shape[0] // rows):
        high, low = halves(both[:, b * rows : (b + 1) * rows])
        values1 = with_ones(vals[b * rows : (b + 1) * rows])
        state = dot(jnp.concatenate([high, low], 1), jnp.concatenate([values1, values1], 0))
        whole += state
        part += state * (b < seen).astype(F32)
    return part, whole


def same_core(ny, same_ref, wk_ref, state_ref, full_ref):
    _, y, _ = place(ny)
    w2 = jnp.concatenate(halves(wk_ref[...].T), 1)
    zero = jnp.zeros(state_ref.shape, F32)
    state_ref[...], full_ref[...] = add_states(flat(same_ref, 0), flat(same_ref, 1), w2, y, zero, zero)


def teach(q, keys0, values0, keys1, values1, scale, masks=None):
    scores0, scores1 = dot(q, keys0, NT), dot(q, keys1, NT)
    if masks is not None:
        scores0 = jnp.where(masks[0], scores0, -1e30)
        scores1 = jnp.where(masks[1], scores1, -1e30)
    best = jnp.maximum(scores0.max(-1, keepdims=True), scores1.max(-1, keepdims=True))
    best = best.astype(BF16).astype(F32)
    c = scale * LOG2E
    return best, dot(jnp.exp2((scores0 - best) * c).astype(BF16), values0) + dot(
        jnp.exp2((scores1 - best) * c).astype(BF16), values1
    )


def own_teacher(ny, scale, q_ref, same_ref, other_ref, accl_ref):
    _, y, core = place(ny)
    n, rows = q_ref.shape[0], same_ref.shape[2]
    col = lax.broadcasted_iota(jnp.int32, (n, ny * rows), 1)
    row = lax.broadcasted_iota(jnp.int32, (n, ny * rows), 0) // (n // rows)
    best, accl = teach(
        q_ref[...],
        flat(same_ref, 0), with_ones(flat(same_ref, 1)),
        flat(other_ref, 0), with_ones(flat(other_ref, 1)),
        scale, (col <= row + y * rows, col < (y + core) * rows),
    )
    lane = lax.broadcasted_iota(jnp.int32, accl.shape, 1)
    accl_ref[...] = jnp.where(lane == accl.shape[1] - 1, best, accl)


def forward(nx, ny, scale, *refs):
    later = refs[: nx - 1]
    same_ref, other_ref, wk_ref, state_in, full_in, pay_ref = refs[nx - 1 :]
    x, y, core = place(ny)
    head = same_ref.shape[3]
    n = later[0].shape[0]
    w2 = jnp.concatenate(halves(wk_ref[...].T), 1)
    keys0, values0 = flat(same_ref, 0), with_ones(flat(same_ref, 1))
    keys1, values1 = flat(other_ref, 0), with_ones(flat(other_ref, 1))
    state, full = add_states(keys1, flat(other_ref, 1), w2, y + core, state_in[...], full_in[...])
    feats_n = full.shape[0]
    full_high = full[:, :head].astype(BF16)
    norm = full[:, head : head + 1]
    norm_high = norm.astype(BF16).astype(F32)
    for s in range(1, nx):

        @pl.when(x + s < nx)
        def _(s=s):
            best, accl = teach(later[s - 1][...], keys0, values0, keys1, values1, scale)
            to = x + s
            total = accl[:, head : head + 1]
            high = total.astype(BF16).astype(F32)
            pay_ref[to, :n] = accl[:, :head].astype(BF16)
            pay_ref[to, n : n + feats_n] = full_high
            pay_ref[to, n + feats_n :] = to_rows(
                [best, high, total - high, norm_high, norm - norm_high], head
            ).astype(BF16)

    for d in range(nx):

        @pl.when(d < x)
        def _(d=d):
            pay_ref[d] = jnp.zeros(pay_ref.shape[1:], BF16)

    high, low = halves(state[:, :head])
    norm = state[:, head : head + 1]
    norm_high = norm.astype(BF16).astype(F32)
    zero = jnp.zeros_like(norm)
    pay_ref[x, :feats_n] = low
    pay_ref[x, n : n + feats_n] = high
    pay_ref[x, n + feats_n :] = to_rows([zero, zero, zero, norm_high, norm - norm_high], head).astype(BF16)


def merge(
    nx, ny, scale, count,
    accl_in, got_ref, fq_ref, near_ref,
    out_ref, dnum_ref, dden_ref, state_ref, back_ref, pay_ref, loss_ref,
):
    x, _, _ = place(ny)
    n, feats_n = fq_ref.shape
    head = out_ref.shape[1]
    c = scale * LOG2E
    columns = to_columns([got_ref[d, n + feats_n :].astype(F32) for d in range(nx)], head)
    bests = [accl_in[:, 2 * head - 1 :]]
    for d in range(nx):
        bests.append(jnp.where(d < x, columns[:, 8 * d : 8 * d + 1], -1e30))
    best = functools.reduce(jnp.maximum, bests)
    factor = jnp.exp2((bests[0] - best) * c)
    accl = accl_in[...] * factor
    acc, total = accl[:, :head], accl[:, head : head + 1]
    state, norm = got_ref[x, :feats_n].astype(F32), jnp.zeros((feats_n, 1), F32)
    for d in range(nx):
        factor = jnp.where(d < x, jnp.exp2((bests[d + 1] - best) * c), 0.0)
        acc += got_ref[d, :n].astype(F32) * factor
        total += (columns[:, 8 * d + 1 : 8 * d + 2] + columns[:, 8 * d + 2 : 8 * d + 3]) * factor
        state += got_ref[d, n : n + feats_n].astype(F32)
        norm += columns[:, 8 * d + 3 : 8 * d + 4] + columns[:, 8 * d + 4 : 8 * d + 5]
    state = jnp.concatenate([state, jnp.broadcast_to(norm, state.shape)], 1)
    state_ref[...] = state
    targets = (acc / total).astype(BF16).astype(F32)
    fq = fq_ref[...]
    numden = dot3(fq, state) + near_ref[...]
    den = numden[:, head:]
    outs = numden[:, :head] / den
    out_ref[...] = outs.astype(BF16)
    diff = outs - targets
    loss_ref[...] = jnp.full(loss_ref.shape, jnp.sum(diff * diff) / count, F32)
    grad_out = diff * (2.0 / count)
    d_num = grad_out / den
    d_den = -jnp.sum(grad_out * outs, -1, keepdims=True) / den
    dnum_ref[...] = d_num
    dden_ref[...] = d_den
    back = dot3(fq.T, jnp.concatenate([d_num, d_den], 1))
    back_ref[...] = back
    norm = back[:, head : head + 1]
    nh = norm.astype(BF16).astype(F32)
    rows = to_rows([nh, norm - nh], head).astype(BF16)
    for d in range(nx):
        pay_ref[d, :feats_n] = back[:, :head].astype(BF16)
        pay_ref[d, feats_n:] = rows


def near_grads(q_ref, k_ref, v_ref, wq_ref, wk_ref, dnum_ref, dden_ref, state_ref, grads_ref):
    q, kd, vd = q_ref[...], k_ref[...], v_ref[...]
    head, rows = kd.shape[1], kd.shape[0]
    d_num, d_den = dnum_ref[...], dden_ref[...]
    fq_t, sig_q, fk_t, sig_d = own_features(q, kd, wq_ref[...], wk_ref[...])
    d_attn = jnp.where(diagonal(q.shape[0], rows), dot2(d_num, vd, NT) + d_den[:, :rows], 0.0)
    lane = lax.broadcasted_iota(jnp.int32, d_den.shape, 1)
    d_aug = jnp.concatenate([d_num, jnp.where(lane == 0, d_den, 0.0)], 1)
    d_fq = dot3(state_ref[...], d_aug, NT) + dot3(fk_t, d_attn, NT)
    d_pre = d_fq[:head] * sig_q - d_fq[head:] * (1.0 - sig_q)
    grads_ref[:head] = dot2(d_pre, q)
    d_fk = dot3(fq_t, d_attn)
    d_pre = d_fk[:head] * sig_d - d_fk[head:] * (1.0 - sig_d)
    grads_ref[head:] = dot2(d_pre, kd)


def backward(
    nx, ny,
    same_ref, other_ref, wk_ref, back_in, got_ref, near_ref, loss_ref,
    grad_ref, sum_ref,
):
    x, y, core = place(ny)
    rows, head = same_ref.shape[2], same_ref.shape[3]
    keys_n = ny * rows
    feats_n = back_in.shape[0]
    columns = to_columns([got_ref[d, feats_n:].astype(F32) for d in range(nx)], head)
    after, norm = jnp.zeros((feats_n, head), F32), jnp.zeros((feats_n, 1), F32)
    for d in range(nx):
        counts = (d > x).astype(F32)
        after += got_ref[d, :feats_n].astype(F32) * counts
        norm += (columns[:, 8 * d : 8 * d + 1] + columns[:, 8 * d + 1 : 8 * d + 2]) * counts

    def both(state, norm):
        mats = jnp.concatenate([state[:head] + state[head:], state[head:]], 0)
        norms = jnp.concatenate([norm[:head] + norm[head:], norm[head:]], 0)
        return jnp.concatenate(halves(mats), 1), norms

    own2, own_n = both(back_in[:, :head], back_in[:, head : head + 1])
    after2, after_n = both(after, norm)
    two = jnp.concatenate([own2, after2], 0)
    key = lax.broadcasted_iota(jnp.int32, (1, keys_n), 1)
    w2 = jnp.concatenate(halves(wk_ref[...].T), 1)
    total = near_ref[head:]
    for half, ref in enumerate((same_ref, other_ref)):
        z = dot(two, pair(flat(ref, 1)), NT)
        d = jnp.where(key < (y + half * core) * rows, z[: 2 * head] + own_n, 0.0) + (z[2 * head :] + after_n)
        _, _, sig = feature_parts(dot(w2, pair(flat(ref, 0)), NT))
        total += dot2(sig * d[:head] - d[head:], flat(ref, 0))
    sum_ref[:head] = near_ref[:head].T
    sum_ref[head:] = total.T
    chunks = grad_ref.shape[0] - 2 * head
    parts = 2 * head // chunks
    for r in range(parts):
        grad_ref[pl.ds(r, chunks, stride=parts + 1), :] = sum_ref[pl.ds(r, chunks, stride=parts), :]
    grad_ref[pl.ds(parts, chunks, stride=parts + 1), :] = jnp.broadcast_to(loss_ref[0:1], (chunks, head))


VMEM = pl.BlockSpec(memory_space=pltpu.VMEM)
PARAMS = pltpu.CompilerParams(vmem_limit_bytes=20 * 1024 * 1024)


def spread(a, axis):
    copies = jnp.broadcast_to(a[None], (lax.axis_size(axis), *a.shape))
    return lax.all_to_all(copies, axis, 0, 0, tiled=True)


def shards(nx, ny, queries, keys, values, w_query, w_key):
    rows, groups, per, head = queries.shape
    n_ctx, n_kvh = lax.axis_size("ctx"), lax.axis_size("kvh")
    scale = head**-0.5
    count = float(rows * n_ctx * groups * n_kvh * per)
    at = lambda x, y, c: (x * ny + y) * CORES + c
    every = [(x, y, c) for x in range(nx) for y in range(ny) for c in range(CORES)]
    y_groups = [[at(x, y, c) for y in range(ny)] for x in range(nx) for c in range(CORES)]
    x_groups = [[at(x, y, c) for x in range(nx)] for y in range(ny) for c in range(CORES)]
    swap = [(at(x, y, c), at(x, y, 1 - c)) for x, y, c in every]
    n, feats, keys_n = rows * per, 2 * head, ny * rows
    f32 = lambda *shape: jax.ShapeDtypeStruct(shape, F32)
    bf16 = lambda *shape: jax.ShapeDtypeStruct(shape, BF16)

    def call(body, outs, args, scratch=(), flops=1, name=None):
        return pl.pallas_call(
            body,
            out_shape=outs,
            in_specs=[VMEM] * len(args),
            out_specs=jax.tree.map(lambda _: VMEM, outs),
            scratch_shapes=list(scratch),
            compiler_params=PARAMS,
            cost_estimate=pl.CostEstimate(
                flops=flops * 1_000_000_000, bytes_accessed=20_000_000, transcendentals=flops * 300_000
            ),
            name=name,
        )(*args)

    q = queries.reshape(n, head)
    k, v = keys.reshape(rows, head), values.reshape(rows, head)
    kvs = jnp.broadcast_to(jnp.stack([k, v])[None], (ny, 2, rows, head))
    same = lax.all_to_all(kvs, "ctx", 0, 0, tiled=True, axis_index_groups=y_groups)
    later = [
        lax.ppermute(q, "ctx", [(at(x, y, c), at(x - s, y, c)) for x, y, c in every if x >= s])
        for s in range(1, nx)
    ]
    own = call(
        prepare,
        (f32(n, feats), f32(n, feats)), (q, k, v, w_query, w_key), flops=2, name="prepare",
    )
    same, later, (fq, near) = lax.optimization_barrier((same, later, own))
    other = lax.ppermute(same, "ctx", swap)
    state, full = call(
        functools.partial(same_core, ny),
        (f32(feats, feats), f32(feats, feats)), (same, w_key), flops=2, name="same_core",
    )
    pay = call(
        functools.partial(forward, nx, ny, scale),
        bf16(nx, n + feats + 16, head),
        (*later, same, other, w_key, state, full), flops=6, name="forward",
    )
    got = lax.all_to_all(pay, "ctx", 0, 0, tiled=True, axis_index_groups=x_groups)
    accl = call(
        functools.partial(own_teacher, ny, scale), f32(n, feats), (q, same, other), flops=2, name="own_teacher",
    )
    out, dnum, dden, state, back, pay, loss = call(
        functools.partial(merge, nx, ny, scale, count),
        (bf16(n, head), f32(n, head), f32(n, head), f32(feats, feats), f32(feats, feats), bf16(nx, feats + 16, head), f32(8, head)),
        (accl, got, fq, near), flops=2, name="merge",
    )
    got = lax.all_to_all(pay, "ctx", 0, 0, tiled=True, axis_index_groups=x_groups)
    grads = call(
        near_grads, f32(feats, head), (q, k, v, w_query, w_key, dnum, dden, state), flops=2, name="near_grads",
    )
    parts = feats // n_ctx
    grads = call(
        functools.partial(backward, nx, ny),
        f32(n_ctx * (parts + 1), head),
        (same, other, w_key, back, got, grads, loss),
        scratch=(pltpu.VMEM((feats, head), F32),), flops=4, name="backward",
    )
    mine = lax.all_to_all(grads.reshape(n_ctx, 1, -1), "ctx", 0, 0, tiled=True).sum(0)
    mine = spread(mine, "kvh").sum(0)
    g = spread(mine[:, : parts * head], "ctx").reshape(2, head, head)
    return out.reshape(queries.shape), g[0], g[1], mine[0, parts * head]


def solution(mesh):
    n_ctx = mesh.shape["ctx"]
    ny = min(8, n_ctx // CORES)
    nx = n_ctx // (CORES * ny)
    placed = (P("ctx", "kvh", None, None), P("ctx", "kvh", None), P("ctx", "kvh", None), P(), P())
    return jax.shard_map(
        functools.partial(shards, nx, ny),
        mesh=mesh,
        in_specs=placed,
        out_specs=(P("ctx", "kvh", None, None), P(), P(), P()),
        check_vma=False,
    )
```

```python
import functools

import jax
import jax.numpy as jnp
from jax import lax
from jax.experimental import pallas as pl
from jax.experimental.pallas import tpu as pltpu
from jax.sharding import PartitionSpec as P

F32, BF16 = jnp.float32, jnp.bfloat16
NN = (((1,), (0,)), ((), ()))
NT = (((1,), (1,)), ((), ()))
LOG2E = 1.4426950408889634
CORES = 2


def dot(a, b, dims=NN):
    return lax.dot_general(a, b, dims, preferred_element_type=F32)


def halves(a):
    high = a.astype(BF16)
    return high, (a - high.astype(F32)).astype(BF16)


def dot3(a, b, dims=NN):
    ah, al = halves(a)
    bh, bl = halves(b)
    return dot(ah, bh, dims) + (dot(ah, bl, dims) + dot(al, bh, dims))


def dot2(a, b, dims=NN):
    ah, al = halves(a)
    return dot(ah, b, dims) + dot(al, b, dims)


def log1p(e):
    return jnp.where(e < 1e-3, e * (1.0 - e * (0.5 - e * (1.0 / 3.0))), jnp.log(1.0 + e))


def feature_parts(pre):
    e = jnp.exp(-jnp.abs(pre))
    t = log1p(e)
    r = 1.0 / (1.0 + e)
    return jnp.maximum(pre, 0.0) + t, jnp.maximum(-pre, 0.0) + t, jnp.where(pre >= 0.0, r, e * r)


def pair(a):
    return jnp.concatenate([a, a], 1)


def with_ones(v):
    return jnp.concatenate([v, jnp.ones_like(v)], 1)


def flat(ref, which):
    blocks, rows, head = ref.shape[0], ref.shape[2], ref.shape[3]
    return ref[:, which].reshape(blocks * rows, head)


def place(ny):
    me = lax.axis_index("ctx")
    return me // (ny * CORES), (me // CORES) % ny, me % CORES


def diagonal(n, rows):
    return lax.broadcasted_iota(jnp.int32, (n, rows), 1) <= (
        lax.broadcasted_iota(jnp.int32, (n, rows), 0) // (n // rows)
    )


def to_rows(pages, head):
    n = pages[0][0].shape[0]
    lane = lax.broadcasted_iota(jnp.int32, (n, head), 1)
    wide = jnp.zeros((n, head), F32)
    for p, columns in enumerate(pages):
        for i, c in enumerate(columns):
            wide = jnp.where(lane == 8 * p + i, c, wide)
    rows = wide.T
    return [
        jnp.concatenate([rows[8 * p : 8 * p + 8, k : k + head] for k in range(0, n, head)], 0).astype(BF16)
        for p in range(len(pages))
    ]


def to_columns(pages, head):
    rows = [
        jnp.concatenate([page[k : k + 8] for k in range(0, page.shape[0], 8)], 1) for page in pages
    ]
    rows += [rows[0]] * (head // 8 - len(rows))
    return jnp.concatenate(rows, 0).T


def copies(k_ref, v_ref, out_ref, sems):
    moves = [
        pltpu.make_async_copy(ref, out_ref.at[d, i], sems.at[d, i])
        for d in range(out_ref.shape[0])
        for i, ref in enumerate((k_ref, v_ref))
    ]
    for move in moves:
        move.start()
    for move in moves:
        move.wait()


def own_features(q, k, wq, wk):
    wqt = jnp.concatenate(halves(wq.T), 1)
    w2 = jnp.concatenate(halves(wk.T), 1)
    sp, sm, sig_q = feature_parts(dot(wqt, pair(q), NT))
    fq_t = jnp.concatenate([sp, sm], 0)
    sp, sm, sig_k = feature_parts(dot(w2, pair(k), NT))
    return fq_t, sig_q, jnp.concatenate([sp, sm], 0), sig_k


def prepare(q_ref, k_ref, v_ref, wq_ref, wk_ref, fq_ref, near_ref):
    q, k, v = q_ref[...], k_ref[...], v_ref[...]
    fq_t, _, fk_t, _ = own_features(q, k, wq_ref[...], wk_ref[...])
    fq = fq_t.T
    fq_ref[...] = fq
    attn = jnp.where(diagonal(q.shape[0], k.shape[0]), dot3(fq, fk_t), 0.0)
    near_ref[...] = dot2(attn, with_ones(v))


def add_states(keys, vals, w2, seen, part, whole):
    rows = part.shape[0] // 2
    sp, sm, _ = feature_parts(dot(w2, pair(keys), NT))
    both = jnp.concatenate([sp, sm], 0)
    for b in range(keys.shape[0] // rows):
        high, low = halves(both[:, b * rows : (b + 1) * rows])
        values1 = with_ones(vals[b * rows : (b + 1) * rows])
        state = dot(jnp.concatenate([high, low], 1), jnp.concatenate([values1, values1], 0))
        whole += state
        part += state * (b < seen).astype(F32)
    return part, whole


def teach(q, keys0, values0, keys1, values1, scale, masks=None):
    scores0, scores1 = dot(q, keys0, NT), dot(q, keys1, NT)
    if masks is not None:
        scores0 = jnp.where(masks[0], scores0, -1e30)
        scores1 = jnp.where(masks[1], scores1, -1e30)
    best = jnp.maximum(scores0.max(-1, keepdims=True), scores1.max(-1, keepdims=True))
    best = best.astype(BF16).astype(F32)
    c = scale * LOG2E
    return best, dot(jnp.exp2((scores0 - best) * c).astype(BF16), values0) + dot(
        jnp.exp2((scores1 - best) * c).astype(BF16), values1
    )


def own_teacher(ny, scale, q_ref, same_ref, other_ref, accl_ref):
    _, y, core = place(ny)
    n, rows = q_ref.shape[0], same_ref.shape[2]
    col = lax.broadcasted_iota(jnp.int32, (n, ny * rows), 1)
    row = lax.broadcasted_iota(jnp.int32, (n, ny * rows), 0) // (n // rows)
    best, accl = teach(
        q_ref[...],
        flat(same_ref, 0), with_ones(flat(same_ref, 1)),
        flat(other_ref, 0), with_ones(flat(other_ref, 1)),
        scale, (col <= row + y * rows, col < (y + core) * rows),
    )
    lane = lax.broadcasted_iota(jnp.int32, accl.shape, 1)
    accl_ref[...] = jnp.where(lane == accl.shape[1] - 1, best, accl)


def partial_softmax(q, keys, values1, c):
    scores = dot(q, keys, NT)
    best = scores.max(-1, keepdims=True).astype(BF16).astype(F32)
    return best, dot(jnp.exp2((scores - best) * c).astype(BF16), values1)


def same_core(nx, ny, scale, *refs):
    later = refs[: nx - 1]
    same_ref, wk_ref, state_ref, full_ref, accl_ref = refs[nx - 1 :]
    _, y, _ = place(ny)
    w2 = jnp.concatenate(halves(wk_ref[...].T), 1)
    zero = jnp.zeros(state_ref.shape, F32)
    keys, vals = flat(same_ref, 0), flat(same_ref, 1)
    state_ref[...], full_ref[...] = add_states(keys, vals, w2, y, zero, zero)
    lane = lax.broadcasted_iota(jnp.int32, accl_ref.shape[1:], 1)
    for s in range(nx - 1):
        best, accl = partial_softmax(later[s][...], keys, with_ones(vals), scale * LOG2E)
        accl_ref[s] = jnp.where(lane == accl.shape[1] - 1, best, accl)


def forward(nx, ny, scale, *refs):
    later = refs[: nx - 1]
    other_ref, wk_ref, state_in, full_in, accl_in, pay_ref = refs[nx - 1 :]
    x, y, core = place(ny)
    head = other_ref.shape[3]
    n = later[0].shape[0]
    c = scale * LOG2E
    w2 = jnp.concatenate(halves(wk_ref[...].T), 1)
    keys, vals = flat(other_ref, 0), flat(other_ref, 1)
    values1 = with_ones(vals)
    state, full = add_states(keys, vals, w2, y + core, state_in[...], full_in[...])
    feats_n = full.shape[0]
    full_high = full[:, :head].astype(BF16)

    def two(column):
        high = column.astype(BF16).astype(F32)
        return [high, column - high]

    high, low = halves(state[:, :head])
    pay_ref[x, :feats_n] = low
    pay_ref[x, n : n + feats_n] = high
    zero = jnp.zeros((n, 1), F32)
    columns = [[zero, zero, zero, *two(state[:, head : head + 1])]]
    sums = []
    for s in range(nx - 1):
        best, accl = partial_softmax(later[s][...], keys, values1, c)
        before = accl_in[s]
        old = before[:, 2 * head - 1 :]
        new = jnp.maximum(old, best)
        mine, other = jnp.exp2((old - new) * c), jnp.exp2((best - new) * c)
        sums.append((before[:, :head] * mine + accl[:, :head] * other).astype(BF16))
        total = before[:, head : head + 1] * mine + accl[:, head : head + 1] * other
        columns.append([new, *two(total), *two(full[:, head : head + 1])])
    rows = to_rows(columns, head)
    pay_ref[x, n + feats_n :] = rows[0]
    for s in range(1, nx):

        @pl.when(x + s < nx)
        def _(s=s):
            pay_ref[x + s, :n] = sums[s - 1]
            pay_ref[x + s, n : n + feats_n] = full_high
            pay_ref[x + s, n + feats_n :] = rows[s]

    for d in range(nx):

        @pl.when(d < x)
        def _(d=d):
            pay_ref[d] = jnp.zeros(pay_ref.shape[1:], BF16)


def merge(
    nx, ny, scale, count,
    accl_in, got_ref, fq_ref, near_ref,
    out_ref, dnum_ref, dden_ref, state_ref, back_ref, pay_ref, loss_ref,
):
    x, _, _ = place(ny)
    n, feats_n = fq_ref.shape
    head = out_ref.shape[1]
    c = scale * LOG2E
    columns = to_columns([got_ref[d, n + feats_n :].astype(F32) for d in range(nx)], head)
    bests = [accl_in[:, 2 * head - 1 :]]
    for d in range(nx):
        bests.append(jnp.where(d < x, columns[:, 8 * d : 8 * d + 1], -1e30))
    best = functools.reduce(jnp.maximum, bests)
    factor = jnp.exp2((bests[0] - best) * c)
    accl = accl_in[...] * factor
    acc, total = accl[:, :head], accl[:, head : head + 1]
    state, norm = got_ref[x, :feats_n].astype(F32), jnp.zeros((feats_n, 1), F32)
    for d in range(nx):
        factor = jnp.where(d < x, jnp.exp2((bests[d + 1] - best) * c), 0.0)
        acc += got_ref[d, :n].astype(F32) * factor
        total += (columns[:, 8 * d + 1 : 8 * d + 2] + columns[:, 8 * d + 2 : 8 * d + 3]) * factor
        state += got_ref[d, n : n + feats_n].astype(F32)
        norm += columns[:, 8 * d + 3 : 8 * d + 4] + columns[:, 8 * d + 4 : 8 * d + 5]
    state = jnp.concatenate([state, jnp.broadcast_to(norm, state.shape)], 1)
    state_ref[...] = state
    targets = (acc / total).astype(BF16).astype(F32)
    fq = fq_ref[...]
    numden = dot3(fq, state) + near_ref[...]
    den = numden[:, head:]
    outs = numden[:, :head] / den
    out_ref[...] = outs.astype(BF16)
    diff = outs - targets
    loss_ref[...] = jnp.full(loss_ref.shape, jnp.sum(diff * diff) / count, F32)
    grad_out = diff * (2.0 / count)
    d_num = grad_out / den
    d_den = -jnp.sum(grad_out * outs, -1, keepdims=True) / den
    dnum_ref[...] = d_num
    dden_ref[...] = d_den
    back = dot3(fq.T, jnp.concatenate([d_num, d_den], 1))
    back_ref[...] = back
    norm = back[:, head : head + 1]
    nh = norm.astype(BF16).astype(F32)
    (rows,) = to_rows([[nh, norm - nh]], head)
    for d in range(nx):
        pay_ref[d, :feats_n] = back[:, :head].astype(BF16)
        pay_ref[d, feats_n:] = rows


def near_grads(q_ref, k_ref, v_ref, wq_ref, wk_ref, dnum_ref, dden_ref, state_ref, grads_ref):
    q, kd, vd = q_ref[...], k_ref[...], v_ref[...]
    head, rows = kd.shape[1], kd.shape[0]
    d_num, d_den = dnum_ref[...], dden_ref[...]
    fq_t, sig_q, fk_t, sig_d = own_features(q, kd, wq_ref[...], wk_ref[...])
    d_attn = jnp.where(diagonal(q.shape[0], rows), dot2(d_num, vd, NT) + d_den[:, :rows], 0.0)
    lane = lax.broadcasted_iota(jnp.int32, d_den.shape, 1)
    d_aug = jnp.concatenate([d_num, jnp.where(lane == 0, d_den, 0.0)], 1)
    d_fq = dot3(state_ref[...], d_aug, NT) + dot3(fk_t, d_attn, NT)
    d_pre = d_fq[:head] * sig_q - d_fq[head:] * (1.0 - sig_q)
    grads_ref[:head] = dot2(d_pre, q)
    d_fk = dot3(fq_t, d_attn)
    d_pre = d_fk[:head] * sig_d - d_fk[head:] * (1.0 - sig_d)
    grads_ref[head:] = dot2(d_pre, kd)


def backward(
    nx, ny,
    same_ref, other_ref, wk_ref, back_in, got_ref, near_ref, loss_ref,
    grad_ref, sum_ref,
):
    x, y, core = place(ny)
    rows, head = same_ref.shape[2], same_ref.shape[3]
    keys_n = ny * rows
    feats_n = back_in.shape[0]
    columns = to_columns([got_ref[d, feats_n:].astype(F32) for d in range(nx)], head)
    after, norm = jnp.zeros((feats_n, head), F32), jnp.zeros((feats_n, 1), F32)
    for d in range(nx):
        counts = (d > x).astype(F32)
        after += got_ref[d, :feats_n].astype(F32) * counts
        norm += (columns[:, 8 * d : 8 * d + 1] + columns[:, 8 * d + 1 : 8 * d + 2]) * counts

    def both(state, norm):
        mats = jnp.concatenate([state[:head] + state[head:], state[head:]], 0)
        norms = jnp.concatenate([norm[:head] + norm[head:], norm[head:]], 0)
        return jnp.concatenate(halves(mats), 1), norms

    own2, own_n = both(back_in[:, :head], back_in[:, head : head + 1])
    after2, after_n = both(after, norm)
    two = jnp.concatenate([own2, after2], 0)
    key = lax.broadcasted_iota(jnp.int32, (1, keys_n), 1)
    w2 = jnp.concatenate(halves(wk_ref[...].T), 1)
    total = near_ref[head:]
    for half, ref in enumerate((same_ref, other_ref)):
        z = dot(two, pair(flat(ref, 1)), NT)
        d = jnp.where(key < (y + half * core) * rows, z[: 2 * head] + own_n, 0.0) + (z[2 * head :] + after_n)
        _, _, sig = feature_parts(dot(w2, pair(flat(ref, 0)), NT))
        total += dot2(sig * d[:head] - d[head:], flat(ref, 0))
    sum_ref[:head] = near_ref[:head].T
    sum_ref[head:] = total.T
    chunks = grad_ref.shape[0] - 2 * head
    parts = 2 * head // chunks
    for r in range(parts):
        grad_ref[pl.ds(r, chunks, stride=parts + 1), :] = sum_ref[pl.ds(r, chunks, stride=parts), :]
    grad_ref[pl.ds(parts, chunks, stride=parts + 1), :] = jnp.broadcast_to(loss_ref[0:1], (chunks, head))


VMEM = pl.BlockSpec(memory_space=pltpu.VMEM)
PARAMS = pltpu.CompilerParams(vmem_limit_bytes=20 * 1024 * 1024)


def spread(a, axis):
    copies = jnp.broadcast_to(a[None], (lax.axis_size(axis), *a.shape))
    return lax.all_to_all(copies, axis, 0, 0, tiled=True)


def shards(nx, ny, queries, keys, values, w_query, w_key):
    rows, groups, per, head = queries.shape
    n_ctx, n_kvh = lax.axis_size("ctx"), lax.axis_size("kvh")
    scale = head**-0.5
    count = float(rows * n_ctx * groups * n_kvh * per)
    at = lambda x, y, c: (x * ny + y) * CORES + c
    every = [(x, y, c) for x in range(nx) for y in range(ny) for c in range(CORES)]
    y_groups = [[at(x, y, c) for y in range(ny)] for x in range(nx) for c in range(CORES)]
    x_groups = [[at(x, y, c) for x in range(nx)] for y in range(ny) for c in range(CORES)]
    swap = [(at(x, y, c), at(x, y, 1 - c)) for x, y, c in every]
    n, feats, keys_n = rows * per, 2 * head, ny * rows
    f32 = lambda *shape: jax.ShapeDtypeStruct(shape, F32)
    bf16 = lambda *shape: jax.ShapeDtypeStruct(shape, BF16)

    def call(body, outs, args, scratch=(), flops=1, name=None):
        return pl.pallas_call(
            body,
            out_shape=outs,
            in_specs=[VMEM] * len(args),
            out_specs=jax.tree.map(lambda _: VMEM, outs),
            scratch_shapes=list(scratch),
            compiler_params=PARAMS,
            cost_estimate=pl.CostEstimate(
                flops=flops * 1_000_000_000, bytes_accessed=20_000_000, transcendentals=flops * 300_000
            ),
            name=name,
        )(*args)

    q = queries.reshape(n, head)
    k, v = keys.reshape(rows, head), values.reshape(rows, head)
    kvs = pl.pallas_call(
        copies,
        out_shape=bf16(ny, 2, rows, head),
        in_specs=[pl.BlockSpec(memory_space=pl.ANY)] * 2,
        out_specs=pl.BlockSpec(memory_space=pl.ANY),
        scratch_shapes=[pltpu.SemaphoreType.DMA((ny, 2))],
        compiler_params=pltpu.CompilerParams(vmem_limit_bytes=60 * 1024 * 1024),
        name="copies",
    )(k, v)
    same = lax.all_to_all(kvs, "ctx", 0, 0, tiled=True, axis_index_groups=y_groups)
    later = [
        lax.ppermute(q, "ctx", [(at(x, y, c), at(x - s, y, c)) for x, y, c in every if x >= s])
        for s in range(1, nx)
    ]
    own = call(
        prepare,
        (f32(n, feats), f32(n, feats)), (q, k, v, w_query, w_key), flops=2, name="prepare",
    )
    same, later, (fq, near) = lax.optimization_barrier((same, later, own))
    other = lax.ppermute(same, "ctx", swap)
    state, full, sums = call(
        functools.partial(same_core, nx, ny, scale),
        (f32(feats, feats), f32(feats, feats), f32(nx - 1, n, feats)), (*later, same, w_key), flops=3, name="same_core",
    )
    pay = call(
        functools.partial(forward, nx, ny, scale),
        bf16(nx, n + feats + 16, head),
        (*later, other, w_key, state, full, sums), flops=4, name="forward",
    )
    got = lax.all_to_all(pay, "ctx", 0, 0, tiled=True, axis_index_groups=x_groups)
    accl = call(
        functools.partial(own_teacher, ny, scale), f32(n, feats), (q, same, other), flops=2, name="own_teacher",
    )
    out, dnum, dden, state, back, pay, loss = call(
        functools.partial(merge, nx, ny, scale, count),
        (bf16(n, head), f32(n, head), f32(n, head), f32(feats, feats), f32(feats, feats), bf16(nx, feats + 16, head), f32(8, head)),
        (accl, got, fq, near), flops=2, name="merge",
    )
    got = lax.all_to_all(pay, "ctx", 0, 0, tiled=True, axis_index_groups=x_groups)
    grads = call(
        near_grads, f32(feats, head), (q, k, v, w_query, w_key, dnum, dden, state), flops=2, name="near_grads",
    )
    parts = feats // n_ctx
    grads = call(
        functools.partial(backward, nx, ny),
        f32(n_ctx * (parts + 1), head),
        (same, other, w_key, back, got, grads, loss),
        scratch=(pltpu.VMEM((feats, head), F32),), flops=4, name="backward",
    )
    mine = lax.all_to_all(grads.reshape(n_ctx, 1, -1), "ctx", 0, 0, tiled=True).sum(0)
    mine = spread(mine, "kvh").sum(0)
    g = spread(mine[:, : parts * head], "ctx").reshape(2, head, head)
    return out.reshape(queries.shape), g[0], g[1], mine[0, parts * head]


def solution(mesh):
    n_ctx = mesh.shape["ctx"]
    ny = min(8, n_ctx // CORES)
    nx = n_ctx // (CORES * ny)
    placed = (P("ctx", "kvh", None, None), P("ctx", "kvh", None), P("ctx", "kvh", None), P(), P())
    return jax.shard_map(
        functools.partial(shards, nx, ny),
        mesh=mesh,
        in_specs=placed,
        out_specs=(P("ctx", "kvh", None, None), P(), P(), P()),
        check_vma=False,
    )
```

```python
import functools

import jax
import jax.numpy as jnp
from jax import lax
from jax.experimental import pallas as pl
from jax.experimental.pallas import tpu as pltpu
from jax.sharding import PartitionSpec as P

F32, BF16 = jnp.float32, jnp.bfloat16
NN = (((1,), (0,)), ((), ()))
NT = (((1,), (1,)), ((), ()))
LOG2E = 1.4426950408889634
CORES = 2


def dot(a, b, dims=NN):
    return lax.dot_general(a, b, dims, preferred_element_type=F32)


def halves(a):
    high = a.astype(BF16)
    return high, (a - high.astype(F32)).astype(BF16)


def dot3(a, b, dims=NN):
    ah, al = halves(a)
    bh, bl = halves(b)
    return dot(ah, bh, dims) + (dot(ah, bl, dims) + dot(al, bh, dims))


def dot2(a, b, dims=NN):
    ah, al = halves(a)
    return dot(ah, b, dims) + dot(al, b, dims)


def log1p(e):
    return jnp.where(e < 1e-3, e * (1.0 - e * (0.5 - e * (1.0 / 3.0))), jnp.log(1.0 + e))


def feature_parts(pre):
    e = jnp.exp(-jnp.abs(pre))
    t = log1p(e)
    r = 1.0 / (1.0 + e)
    return jnp.maximum(pre, 0.0) + t, jnp.maximum(-pre, 0.0) + t, jnp.where(pre >= 0.0, r, e * r)


def pair(a):
    return jnp.concatenate([a, a], 1)


def with_ones(v):
    return jnp.concatenate([v, jnp.ones_like(v)], 1)


def flat(ref, which):
    blocks, rows, head = ref.shape[0], ref.shape[2], ref.shape[3]
    return ref[:, which].reshape(blocks * rows, head)


def place(ny):
    me = lax.axis_index("ctx")
    return me // (ny * CORES), (me // CORES) % ny, me % CORES


def diagonal(n, rows):
    return lax.broadcasted_iota(jnp.int32, (n, rows), 1) <= (
        lax.broadcasted_iota(jnp.int32, (n, rows), 0) // (n // rows)
    )


def to_rows(pages, head):
    n = pages[0][0].shape[0]
    lane = lax.broadcasted_iota(jnp.int32, (n, head), 1)
    wide = jnp.zeros((n, head), F32)
    for p, columns in enumerate(pages):
        for i, c in enumerate(columns):
            wide = jnp.where(lane == 8 * p + i, c, wide)
    rows = wide.T
    return [
        jnp.concatenate([rows[8 * p : 8 * p + 8, k : k + head] for k in range(0, n, head)], 0).astype(BF16)
        for p in range(len(pages))
    ]


def row_numbers(page):
    return jnp.concatenate([page[k : k + 8] for k in range(0, page.shape[0], 8)], 1).astype(F32)


def to_columns(rows, head):
    return jnp.concatenate(rows + [jnp.zeros((head - len(rows), rows[0].shape[1]), F32)], 0).T


def copies(k_ref, v_ref, out_ref):
    for d in range(out_ref.shape[0]):
        out_ref[d, 0] = k_ref[...]
        out_ref[d, 1] = v_ref[...]


def own_features(q, k, wq, wk):
    wqt = jnp.concatenate(halves(wq.T), 1)
    w2 = jnp.concatenate(halves(wk.T), 1)
    sp, sm, sig_q = feature_parts(dot(wqt, pair(q), NT))
    fq_t = jnp.concatenate([sp, sm], 0)
    sp, sm, sig_k = feature_parts(dot(w2, pair(k), NT))
    return fq_t, sig_q, jnp.concatenate([sp, sm], 0), sig_k


def prepare(q_ref, k_ref, v_ref, wq_ref, wk_ref, fq_ref, near_ref):
    q, k, v = q_ref[...], k_ref[...], v_ref[...]
    fq_t, _, fk_t, _ = own_features(q, k, wq_ref[...], wk_ref[...])
    fq = fq_t.T
    fq_ref[...] = fq
    attn = jnp.where(diagonal(q.shape[0], k.shape[0]), dot3(fq, fk_t), 0.0)
    near_ref[...] = dot2(attn, with_ones(v))


def add_states(keys, vals, w2, seen, part, whole):
    rows = part.shape[0] // 2
    sp, sm, _ = feature_parts(dot(w2, pair(keys), NT))
    both = jnp.concatenate([sp, sm], 0)
    for b in range(keys.shape[0] // rows):
        high, low = halves(both[:, b * rows : (b + 1) * rows])
        values1 = with_ones(vals[b * rows : (b + 1) * rows])
        state = dot(jnp.concatenate([high, low], 1), jnp.concatenate([values1, values1], 0))
        whole += state
        part += state * (b < seen).astype(F32)
    return part, whole


def teach(q, keys0, values0, keys1, values1, scale, masks=None):
    scores0, scores1 = dot(q, keys0, NT), dot(q, keys1, NT)
    if masks is not None:
        scores0 = jnp.where(masks[0], scores0, -1e30)
        scores1 = jnp.where(masks[1], scores1, -1e30)
    best = jnp.maximum(scores0.max(-1, keepdims=True), scores1.max(-1, keepdims=True))
    best = best.astype(BF16).astype(F32)
    c = scale * LOG2E
    return best, dot(jnp.exp2((scores0 - best) * c).astype(BF16), values0) + dot(
        jnp.exp2((scores1 - best) * c).astype(BF16), values1
    )


def own_teacher(ny, scale, q_ref, same_ref, other_ref, acc_ref, stats_ref):
    _, y, core = place(ny)
    n, rows = q_ref.shape[0], same_ref.shape[2]
    col = lax.broadcasted_iota(jnp.int32, (n, ny * rows), 1)
    row = lax.broadcasted_iota(jnp.int32, (n, ny * rows), 0) // (n // rows)
    best, accl = teach(
        q_ref[...],
        flat(same_ref, 0), with_ones(flat(same_ref, 1)),
        flat(other_ref, 0), with_ones(flat(other_ref, 1)),
        scale, (col <= row + y * rows, col < (y + core) * rows),
    )
    head = accl.shape[1] // 2
    acc_ref[...] = accl[:, :head]
    lane = lax.broadcasted_iota(jnp.int32, (n, head), 1)
    stats_ref[...] = jnp.where(lane == 0, best, accl[:, head:]).T[:8]


def partial_softmax(q, keys, values1, c):
    scores = dot(q, keys, NT)
    best = scores.max(-1, keepdims=True).astype(BF16).astype(F32)
    return best, dot(jnp.exp2((scores - best) * c).astype(BF16), values1)


def same_core(nx, ny, scale, *refs):
    later = refs[: nx - 1]
    same_ref, wk_ref, state_ref, full_ref, accl_ref = refs[nx - 1 :]
    _, y, _ = place(ny)
    w2 = jnp.concatenate(halves(wk_ref[...].T), 1)
    zero = jnp.zeros(state_ref.shape, F32)
    keys, vals = flat(same_ref, 0), flat(same_ref, 1)
    state_ref[...], full_ref[...] = add_states(keys, vals, w2, y, zero, zero)
    lane = lax.broadcasted_iota(jnp.int32, accl_ref.shape[1:], 1)
    for s in range(nx - 1):
        best, accl = partial_softmax(later[s][...], keys, with_ones(vals), scale * LOG2E)
        accl_ref[s] = jnp.where(lane == accl.shape[1] - 1, best, accl)


def forward(nx, ny, scale, *refs):
    later = refs[: nx - 1]
    other_ref, wk_ref, state_in, full_in, accl_in, pay_ref = refs[nx - 1 :]
    x, y, core = place(ny)
    head = other_ref.shape[3]
    n = later[0].shape[0]
    c = scale * LOG2E
    w2 = jnp.concatenate(halves(wk_ref[...].T), 1)
    keys, vals = flat(other_ref, 0), flat(other_ref, 1)
    values1 = with_ones(vals)
    state, full = add_states(keys, vals, w2, y + core, state_in[...], full_in[...])
    feats_n = full.shape[0]
    full_high = full[:, :head].astype(BF16)

    def two(column):
        high = column.astype(BF16).astype(F32)
        return [high, column - high]

    high, low = halves(state[:, :head])
    pay_ref[x, :feats_n] = low
    pay_ref[x, n : n + feats_n] = high
    zero = jnp.zeros((n, 1), F32)
    columns = [[zero, zero, zero, *two(state[:, head : head + 1])]]
    sums = []
    for s in range(nx - 1):
        best, accl = partial_softmax(later[s][...], keys, values1, c)
        before = accl_in[s]
        old = before[:, 2 * head - 1 :]
        new = jnp.maximum(old, best)
        mine, other = jnp.exp2((old - new) * c), jnp.exp2((best - new) * c)
        sums.append((before[:, :head] * mine + accl[:, :head] * other).astype(BF16))
        total = before[:, head : head + 1] * mine + accl[:, head : head + 1] * other
        columns.append([new, *two(total), *two(full[:, head : head + 1])])
    rows = to_rows(columns, head)
    pay_ref[x, n + feats_n :] = rows[0]
    for s in range(1, nx):

        @pl.when(x + s < nx)
        def _(s=s):
            pay_ref[x + s, :n] = sums[s - 1]
            pay_ref[x + s, n : n + feats_n] = full_high
            pay_ref[x + s, n + feats_n :] = rows[s]

    for d in range(nx):

        @pl.when(d < x)
        def _(d=d):
            pay_ref[d] = jnp.zeros(pay_ref.shape[1:], BF16)


def merge(
    nx, ny, scale, count,
    acc_in, stats_in, got_ref, fq_ref, near_ref,
    out_ref, dnum_ref, dden_ref, state_ref, back_ref, pay_ref, loss_ref,
):
    x, _, _ = place(ny)
    n, feats_n = fq_ref.shape
    head = out_ref.shape[1]
    c = scale * LOG2E
    pages = [row_numbers(got_ref[d, n + feats_n :]) for d in range(nx)]
    own = stats_in[0:1]
    bests = [jnp.where(d < x, pages[d][0:1], -1e30) for d in range(nx)]
    best = functools.reduce(jnp.maximum, bests, own)
    factors = [jnp.exp2((own - best) * c)]
    total = stats_in[1:2] * factors[0]
    norm = jnp.zeros_like(total)
    for d in range(nx):
        factors.append(jnp.where(d < x, jnp.exp2((bests[d] - best) * c), 0.0))
        total += (pages[d][1:2] + pages[d][2:3]) * factors[d + 1]
        norm += pages[d][3:4] + pages[d][4:5]
    columns = to_columns([f / total for f in factors] + [norm], head)
    targets = acc_in[...] * columns[:, 0:1]
    state = got_ref[x, :feats_n].astype(F32)
    for d in range(nx):
        targets += got_ref[d, :n].astype(F32) * columns[:, d + 1 : d + 2]
        state += got_ref[d, n : n + feats_n].astype(F32)
    targets = targets.astype(BF16).astype(F32)
    norm = columns[:, nx + 1 : nx + 2]
    state = jnp.concatenate([state, jnp.broadcast_to(norm, state.shape)], 1)
    state_ref[...] = state
    fq = fq_ref[...]
    numden = dot3(fq, state) + near_ref[...]
    den = numden[:, head:]
    outs = numden[:, :head] / den
    out_ref[...] = outs.astype(BF16)
    diff = outs - targets
    loss_ref[...] = jnp.full(loss_ref.shape, jnp.sum(diff * diff) / count, F32)
    grad_out = diff * (2.0 / count)
    d_num = grad_out / den
    d_den = -jnp.sum(grad_out * outs, -1, keepdims=True) / den
    dnum_ref[...] = d_num
    dden_ref[...] = d_den
    back = dot3(fq.T, jnp.concatenate([d_num, d_den], 1))
    back_ref[...] = back
    norm = back[:, head : head + 1]
    nh = norm.astype(BF16).astype(F32)
    (rows,) = to_rows([[nh, norm - nh]], head)
    for d in range(nx):
        pay_ref[d, :feats_n] = back[:, :head].astype(BF16)
        pay_ref[d, feats_n:] = rows


def near_grads(q_ref, k_ref, v_ref, wq_ref, wk_ref, dnum_ref, dden_ref, state_ref, grads_ref):
    q, kd, vd = q_ref[...], k_ref[...], v_ref[...]
    head, rows = kd.shape[1], kd.shape[0]
    d_num, d_den = dnum_ref[...], dden_ref[...]
    fq_t, sig_q, fk_t, sig_d = own_features(q, kd, wq_ref[...], wk_ref[...])
    d_attn = jnp.where(diagonal(q.shape[0], rows), dot2(d_num, vd, NT) + d_den[:, :rows], 0.0)
    lane = lax.broadcasted_iota(jnp.int32, d_den.shape, 1)
    d_aug = jnp.concatenate([d_num, jnp.where(lane == 0, d_den, 0.0)], 1)
    d_fq = dot3(state_ref[...], d_aug, NT) + dot3(fk_t, d_attn, NT)
    d_pre = d_fq[:head] * sig_q - d_fq[head:] * (1.0 - sig_q)
    grads_ref[:head] = dot2(d_pre, q)
    d_fk = dot3(fq_t, d_attn)
    d_pre = d_fk[:head] * sig_d - d_fk[head:] * (1.0 - sig_d)
    grads_ref[head:] = dot2(d_pre, kd)


def backward(
    nx, ny,
    same_ref, other_ref, wk_ref, back_in, got_ref, near_ref, loss_ref,
    grad_ref, sum_ref,
):
    x, y, core = place(ny)
    rows, head = same_ref.shape[2], same_ref.shape[3]
    keys_n = ny * rows
    feats_n = back_in.shape[0]
    after, norm = jnp.zeros((feats_n, head), F32), jnp.zeros((1, feats_n), F32)
    for d in range(nx):
        counts = (d > x).astype(F32)
        after += got_ref[d, :feats_n].astype(F32) * counts
        page = row_numbers(got_ref[d, feats_n:])
        norm += (page[0:1] + page[1:2]) * counts
    norm = to_columns([norm], head)[:, 0:1]

    def both(state, norm):
        mats = jnp.concatenate([state[:head] + state[head:], state[head:]], 0)
        norms = jnp.concatenate([norm[:head] + norm[head:], norm[head:]], 0)
        return jnp.concatenate(halves(mats), 1), norms

    own2, own_n = both(back_in[:, :head], back_in[:, head : head + 1])
    after2, after_n = both(after, norm)
    two = jnp.concatenate([own2, after2], 0)
    key = lax.broadcasted_iota(jnp.int32, (1, keys_n), 1)
    w2 = jnp.concatenate(halves(wk_ref[...].T), 1)
    total = near_ref[head:]
    for half, ref in enumerate((same_ref, other_ref)):
        z = dot(two, pair(flat(ref, 1)), NT)
        d = jnp.where(key < (y + half * core) * rows, z[: 2 * head] + own_n, 0.0) + (z[2 * head :] + after_n)
        _, _, sig = feature_parts(dot(w2, pair(flat(ref, 0)), NT))
        total += dot2(sig * d[:head] - d[head:], flat(ref, 0))
    sum_ref[:head] = near_ref[:head].T
    sum_ref[head:] = total.T
    chunks = grad_ref.shape[0] - 2 * head
    parts = 2 * head // chunks
    for r in range(parts):
        grad_ref[pl.ds(r, chunks, stride=parts + 1), :] = sum_ref[pl.ds(r, chunks, stride=parts), :]
    grad_ref[pl.ds(parts, chunks, stride=parts + 1), :] = jnp.broadcast_to(loss_ref[0:1], (chunks, head))


VMEM = pl.BlockSpec(memory_space=pltpu.VMEM)


def spread(a, axis):
    copies = jnp.broadcast_to(a[None], (lax.axis_size(axis), *a.shape))
    return lax.all_to_all(copies, axis, 0, 0, tiled=True)


def shards(nx, ny, queries, keys, values, w_query, w_key):
    rows, groups, per, head = queries.shape
    n_ctx, n_kvh = lax.axis_size("ctx"), lax.axis_size("kvh")
    scale = head**-0.5
    count = float(rows * n_ctx * groups * n_kvh * per)
    at = lambda x, y, c: (x * ny + y) * CORES + c
    every = [(x, y, c) for x in range(nx) for y in range(ny) for c in range(CORES)]
    y_groups = [[at(x, y, c) for y in range(ny)] for x in range(nx) for c in range(CORES)]
    x_groups = [[at(x, y, c) for x in range(nx)] for y in range(ny) for c in range(CORES)]
    swap = [(at(x, y, c), at(x, y, 1 - c)) for x, y, c in every]
    n, feats, keys_n = rows * per, 2 * head, ny * rows
    f32 = lambda *shape: jax.ShapeDtypeStruct(shape, F32)
    bf16 = lambda *shape: jax.ShapeDtypeStruct(shape, BF16)

    def call(body, outs, args, scratch=(), flops=1, name=None, vmem=20):
        return pl.pallas_call(
            body,
            out_shape=outs,
            in_specs=[VMEM] * len(args),
            out_specs=jax.tree.map(lambda _: VMEM, outs),
            scratch_shapes=list(scratch),
            compiler_params=pltpu.CompilerParams(vmem_limit_bytes=vmem * 1024 * 1024),
            cost_estimate=pl.CostEstimate(
                flops=flops * 1_000_000_000, bytes_accessed=20_000_000, transcendentals=flops * 300_000
            ),
            name=name,
        )(*args)

    q = queries.reshape(n, head)
    k, v = keys.reshape(rows, head), values.reshape(rows, head)
    kvs = call(copies, bf16(ny, 2, rows, head), (k, v), name="copies", vmem=60)
    same = lax.all_to_all(kvs, "ctx", 0, 0, tiled=True, axis_index_groups=y_groups)
    later = [
        lax.ppermute(q, "ctx", [(at(x, y, c), at(x - s, y, c)) for x, y, c in every if x >= s])
        for s in range(1, nx)
    ]
    own = call(
        prepare,
        (f32(n, feats), f32(n, feats)), (q, k, v, w_query, w_key), flops=2, name="prepare",
    )
    same, later, (fq, near) = lax.optimization_barrier((same, later, own))
    other = lax.ppermute(same, "ctx", swap)
    state, full, sums = call(
        functools.partial(same_core, nx, ny, scale),
        (f32(feats, feats), f32(feats, feats), f32(nx - 1, n, feats)), (*later, same, w_key), flops=3, name="same_core",
    )
    pay = call(
        functools.partial(forward, nx, ny, scale),
        bf16(nx, n + feats + 16, head),
        (*later, other, w_key, state, full, sums), flops=4, name="forward",
    )
    got = lax.all_to_all(pay, "ctx", 0, 0, tiled=True, axis_index_groups=x_groups)
    acc, stats = call(
        functools.partial(own_teacher, ny, scale), (f32(n, head), f32(8, n)), (q, same, other), flops=2, name="own_teacher",
    )
    out, dnum, dden, state, back, pay, loss = call(
        functools.partial(merge, nx, ny, scale, count),
        (bf16(n, head), f32(n, head), f32(n, head), f32(feats, feats), f32(feats, feats), bf16(nx, feats + 16, head), f32(8, head)),
        (acc, stats, got, fq, near), flops=2, name="merge",
    )
    got = lax.all_to_all(pay, "ctx", 0, 0, tiled=True, axis_index_groups=x_groups)
    grads = call(
        near_grads, f32(feats, head), (q, k, v, w_query, w_key, dnum, dden, state), flops=2, name="near_grads",
    )
    parts = feats // n_ctx
    grads = call(
        functools.partial(backward, nx, ny),
        f32(n_ctx * (parts + 1), head),
        (same, other, w_key, back, got, grads, loss),
        scratch=(pltpu.VMEM((feats, head), F32),), flops=4, name="backward",
    )
    mine = lax.all_to_all(grads.reshape(n_ctx, 1, -1), "ctx", 0, 0, tiled=True).sum(0)
    mine = spread(mine, "kvh").sum(0)
    g = spread(mine[:, : parts * head], "ctx").reshape(2, head, head)
    return out.reshape(queries.shape), g[0], g[1], mine[0, parts * head]


def solution(mesh):
    n_ctx = mesh.shape["ctx"]
    ny = min(8, n_ctx // CORES)
    nx = n_ctx // (CORES * ny)
    placed = (P("ctx", "kvh", None, None), P("ctx", "kvh", None), P("ctx", "kvh", None), P(), P())
    return jax.shard_map(
        functools.partial(shards, nx, ny),
        mesh=mesh,
        in_specs=placed,
        out_specs=(P("ctx", "kvh", None, None), P(), P(), P()),
        check_vma=False,
    )
```

```python
import functools

import jax
import jax.numpy as jnp
from jax import lax
from jax.experimental import pallas as pl
from jax.experimental.pallas import tpu as pltpu
from jax.sharding import PartitionSpec as P

F32, BF16 = jnp.float32, jnp.bfloat16
NN = (((1,), (0,)), ((), ()))
NT = (((1,), (1,)), ((), ()))
LOG2E = 1.4426950408889634
CORES = 2


def dot(a, b, dims=NN):
    return lax.dot_general(a, b, dims, preferred_element_type=F32)


def halves(a):
    high = a.astype(BF16)
    return high, (a - high.astype(F32)).astype(BF16)


def dot3(a, b, dims=NN):
    ah, al = halves(a)
    bh, bl = halves(b)
    return dot(ah, bh, dims) + (dot(ah, bl, dims) + dot(al, bh, dims))


def dot2(a, b, dims=NN):
    ah, al = halves(a)
    return dot(ah, b, dims) + dot(al, b, dims)


def log1p(e):
    return jnp.where(e < 1e-3, e * (1.0 - e * (0.5 - e * (1.0 / 3.0))), jnp.log(1.0 + e))


def feature_parts(pre):
    e = jnp.exp(-jnp.abs(pre))
    t = log1p(e)
    r = 1.0 / (1.0 + e)
    return jnp.maximum(pre, 0.0) + t, jnp.maximum(-pre, 0.0) + t, jnp.where(pre >= 0.0, r, e * r)


def pair(a):
    return jnp.concatenate([a, a], 1)


def with_ones(v):
    return jnp.concatenate([v, jnp.ones_like(v)], 1)


def flat(ref, which):
    blocks, rows, head = ref.shape[0], ref.shape[2], ref.shape[3]
    return ref[:, which].reshape(blocks * rows, head)


def place(ny):
    me = lax.axis_index("ctx")
    return me // (ny * CORES), (me // CORES) % ny, me % CORES


def diagonal(n, rows):
    return lax.broadcasted_iota(jnp.int32, (n, rows), 1) <= (
        lax.broadcasted_iota(jnp.int32, (n, rows), 0) // (n // rows)
    )


def to_rows(pages, head):
    n = pages[0][0].shape[0]
    lane = lax.broadcasted_iota(jnp.int32, (n, head), 1)
    wide = jnp.zeros((n, head), F32)
    for p, columns in enumerate(pages):
        for i, c in enumerate(columns):
            wide = jnp.where(lane == 8 * p + i, c, wide)
    rows = wide.T
    return [
        jnp.concatenate([rows[8 * p : 8 * p + 8, k : k + head] for k in range(0, n, head)], 0).astype(BF16)
        for p in range(len(pages))
    ]


def row_numbers(page):
    return jnp.concatenate([page[k : k + 8] for k in range(0, page.shape[0], 8)], 1).astype(F32)


def to_columns(rows, head):
    return jnp.concatenate(rows + [jnp.zeros((head - len(rows), rows[0].shape[1]), F32)], 0).T


def copies(k_ref, v_ref, out_ref):
    for d in range(out_ref.shape[0]):
        out_ref[d, 0] = k_ref[...]
        out_ref[d, 1] = v_ref[...]


def own_features(q, k, wq, wk):
    wqt = jnp.concatenate(halves(wq.T), 1)
    w2 = jnp.concatenate(halves(wk.T), 1)
    sp, sm, sig_q = feature_parts(dot(wqt, pair(q), NT))
    fq_t = jnp.concatenate([sp, sm], 0)
    sp, sm, sig_k = feature_parts(dot(w2, pair(k), NT))
    return fq_t, sig_q, jnp.concatenate([sp, sm], 0), sig_k


def prepare(q_ref, k_ref, v_ref, wq_ref, wk_ref, fq_ref, near_ref):
    q, k, v = q_ref[...], k_ref[...], v_ref[...]
    fq_t, _, fk_t, _ = own_features(q, k, wq_ref[...], wk_ref[...])
    fq = fq_t.T
    fq_ref[...] = fq
    attn = jnp.where(diagonal(q.shape[0], k.shape[0]), dot3(fq, fk_t), 0.0)
    near_ref[...] = dot2(attn, with_ones(v))


def add_states(keys, vals, w2, seen, part, whole):
    rows = part.shape[0] // 2
    sp, sm, _ = feature_parts(dot(w2, pair(keys), NT))
    both = jnp.concatenate([sp, sm], 0)
    for b in range(keys.shape[0] // rows):
        high, low = halves(both[:, b * rows : (b + 1) * rows])
        values1 = with_ones(vals[b * rows : (b + 1) * rows])
        state = dot(jnp.concatenate([high, low], 1), jnp.concatenate([values1, values1], 0))
        whole += state
        part += state * (b < seen).astype(F32)
    return part, whole


def teach(q, keys0, values0, keys1, values1, scale, masks=None):
    scores0, scores1 = dot(q, keys0, NT), dot(q, keys1, NT)
    if masks is not None:
        scores0 = jnp.where(masks[0], scores0, -1e30)
        scores1 = jnp.where(masks[1], scores1, -1e30)
    best = jnp.maximum(scores0.max(-1, keepdims=True), scores1.max(-1, keepdims=True))
    best = best.astype(BF16).astype(F32)
    c = scale * LOG2E
    return best, dot(jnp.exp2((scores0 - best) * c).astype(BF16), values0) + dot(
        jnp.exp2((scores1 - best) * c).astype(BF16), values1
    )


def own_teacher(ny, scale, q_ref, same_ref, other_ref, acc_ref, stats_ref):
    _, y, core = place(ny)
    n, rows = q_ref.shape[0], same_ref.shape[2]
    col = lax.broadcasted_iota(jnp.int32, (n, ny * rows), 1)
    row = lax.broadcasted_iota(jnp.int32, (n, ny * rows), 0) // (n // rows)
    best, accl = teach(
        q_ref[...],
        flat(same_ref, 0), with_ones(flat(same_ref, 1)),
        flat(other_ref, 0), with_ones(flat(other_ref, 1)),
        scale, (col <= row + y * rows, col < (y + core) * rows),
    )
    head = accl.shape[1] // 2
    acc_ref[...] = accl[:, :head]
    lane = lax.broadcasted_iota(jnp.int32, (n, head), 1)
    stats_ref[...] = jnp.where(lane == 0, best, accl[:, head:]).T[:8]


def partial_softmax(q, keys, values1, c):
    scores = dot(q, keys, NT)
    best = scores.max(-1, keepdims=True).astype(BF16).astype(F32)
    return best, dot(jnp.exp2((scores - best) * c).astype(BF16), values1)


def same_core(nx, ny, scale, *refs):
    later = refs[: nx - 1]
    same_ref, wk_ref, state_ref, full_ref, accl_ref = refs[nx - 1 :]
    _, y, _ = place(ny)
    w2 = jnp.concatenate(halves(wk_ref[...].T), 1)
    zero = jnp.zeros(state_ref.shape, F32)
    keys, vals = flat(same_ref, 0), flat(same_ref, 1)
    state_ref[...], full_ref[...] = add_states(keys, vals, w2, y, zero, zero)
    lane = lax.broadcasted_iota(jnp.int32, accl_ref.shape[1:], 1)
    for s in range(nx - 1):
        best, accl = partial_softmax(later[s][...], keys, with_ones(vals), scale * LOG2E)
        accl_ref[s] = jnp.where(lane == accl.shape[1] - 1, best, accl)


def forward(nx, ny, scale, *refs):
    later = refs[: nx - 1]
    other_ref, wk_ref, state_in, full_in, accl_in, pay_ref = refs[nx - 1 :]
    x, y, core = place(ny)
    head = other_ref.shape[3]
    n = later[0].shape[0]
    c = scale * LOG2E
    w2 = jnp.concatenate(halves(wk_ref[...].T), 1)
    keys, vals = flat(other_ref, 0), flat(other_ref, 1)
    values1 = with_ones(vals)
    state, full = add_states(keys, vals, w2, y + core, state_in[...], full_in[...])
    feats_n = full.shape[0]
    full_high = full[:, :head].astype(BF16)

    def two(column):
        high = column.astype(BF16).astype(F32)
        return [high, column - high]

    high, low = halves(state[:, :head])
    pay_ref[x, :feats_n] = low
    pay_ref[x, n : n + feats_n] = high
    zero = jnp.zeros((n, 1), F32)
    columns = [[zero, zero, zero, *two(state[:, head : head + 1])]]
    sums = []
    for s in range(nx - 1):
        best, accl = partial_softmax(later[s][...], keys, values1, c)
        before = accl_in[s]
        old = before[:, 2 * head - 1 :]
        new = jnp.maximum(old, best)
        mine, other = jnp.exp2((old - new) * c), jnp.exp2((best - new) * c)
        sums.append((before[:, :head] * mine + accl[:, :head] * other).astype(BF16))
        total = before[:, head : head + 1] * mine + accl[:, head : head + 1] * other
        columns.append([new, *two(total), *two(full[:, head : head + 1])])
    rows = to_rows(columns, head)
    pay_ref[x, n + feats_n :] = rows[0]
    for s in range(1, nx):

        @pl.when(x + s < nx)
        def _(s=s):
            pay_ref[x + s, :n] = sums[s - 1]
            pay_ref[x + s, n : n + feats_n] = full_high
            pay_ref[x + s, n + feats_n :] = rows[s]

    for d in range(nx):

        @pl.when(d < x)
        def _(d=d):
            pay_ref[d] = jnp.zeros(pay_ref.shape[1:], BF16)


def merge(
    nx, ny, scale, count,
    acc_in, stats_in, got_ref, fq_ref, near_ref,
    out_ref, dnum_ref, dden_ref, state_ref, back_ref, pay_ref, loss_ref,
):
    x, _, _ = place(ny)
    n, feats_n = fq_ref.shape
    head = out_ref.shape[1]
    c = scale * LOG2E
    pages = [row_numbers(got_ref[d, n + feats_n :]) for d in range(nx)]
    own = stats_in[0:1]
    bests = [jnp.where(d < x, pages[d][0:1], -1e30) for d in range(nx)]
    best = functools.reduce(jnp.maximum, bests, own)
    factors = [jnp.exp2((own - best) * c)]
    total = stats_in[1:2] * factors[0]
    norm = jnp.zeros_like(total)
    for d in range(nx):
        factors.append(jnp.where(d < x, jnp.exp2((bests[d] - best) * c), 0.0))
        total += (pages[d][1:2] + pages[d][2:3]) * factors[d + 1]
        norm += pages[d][3:4] + pages[d][4:5]
    columns = to_columns([f / total for f in factors] + [norm], head)
    targets = acc_in[...] * columns[:, 0:1]
    state = got_ref[x, :feats_n].astype(F32)
    for d in range(nx):
        targets += got_ref[d, :n].astype(F32) * columns[:, d + 1 : d + 2]
        state += got_ref[d, n : n + feats_n].astype(F32)
    targets = targets.astype(BF16).astype(F32)
    norm = columns[:, nx + 1 : nx + 2]
    state = jnp.concatenate([state, jnp.broadcast_to(norm, state.shape)], 1)
    state_ref[...] = state
    fq = fq_ref[...]
    numden = dot3(fq, state) + near_ref[...]
    den = numden[:, head:]
    outs = numden[:, :head] / den
    out_ref[...] = outs.astype(BF16)
    diff = outs - targets
    loss_ref[...] = jnp.full(loss_ref.shape, jnp.sum(diff * diff) / count, F32)
    grad_out = diff * (2.0 / count)
    d_num = grad_out / den
    d_den = -jnp.sum(grad_out * outs, -1, keepdims=True) / den
    dnum_ref[...] = d_num
    dden_ref[...] = d_den
    back = dot3(fq.T, jnp.concatenate([d_num, d_den], 1))
    back_ref[...] = back
    norm = back[:, head : head + 1]
    nh = norm.astype(BF16).astype(F32)
    (rows,) = to_rows([[nh, norm - nh]], head)
    for d in range(nx):
        pay_ref[d, :feats_n] = back[:, :head].astype(BF16)
        pay_ref[d, feats_n:] = rows


def near_grads(q_ref, k_ref, v_ref, wq_ref, wk_ref, dnum_ref, dden_ref, state_ref, grads_ref):
    q, kd, vd = q_ref[...], k_ref[...], v_ref[...]
    head, rows = kd.shape[1], kd.shape[0]
    d_num, d_den = dnum_ref[...], dden_ref[...]
    fq_t, sig_q, fk_t, sig_d = own_features(q, kd, wq_ref[...], wk_ref[...])
    d_attn = jnp.where(diagonal(q.shape[0], rows), dot2(d_num, vd, NT) + d_den[:, :rows], 0.0)
    lane = lax.broadcasted_iota(jnp.int32, d_den.shape, 1)
    d_aug = jnp.concatenate([d_num, jnp.where(lane == 0, d_den, 0.0)], 1)
    d_fq = dot3(state_ref[...], d_aug, NT) + dot3(fk_t, d_attn, NT)
    d_pre = d_fq[:head] * sig_q - d_fq[head:] * (1.0 - sig_q)
    grads_ref[:head] = dot2(d_pre, q)
    d_fk = dot3(fq_t, d_attn)
    d_pre = d_fk[:head] * sig_d - d_fk[head:] * (1.0 - sig_d)
    grads_ref[head:] = dot2(d_pre, kd)


def backward(
    nx, ny,
    same_ref, other_ref, wk_ref, back_in, got_ref, near_ref, loss_ref,
    grad_ref, sum_ref,
):
    x, y, core = place(ny)
    rows, head = same_ref.shape[2], same_ref.shape[3]
    keys_n = ny * rows
    feats_n = back_in.shape[0]
    after, norm = jnp.zeros((feats_n, head), F32), jnp.zeros((1, feats_n), F32)
    for d in range(nx):
        counts = (d > x).astype(F32)
        after += got_ref[d, :feats_n].astype(F32) * counts
        page = row_numbers(got_ref[d, feats_n:])
        norm += (page[0:1] + page[1:2]) * counts
    norm = to_columns([norm], head)[:, 0:1]

    def both(state, norm):
        mats = jnp.concatenate([state[:head] + state[head:], state[head:]], 0)
        norms = jnp.concatenate([norm[:head] + norm[head:], norm[head:]], 0)
        return jnp.concatenate(halves(mats), 1), norms

    own2, own_n = both(back_in[:, :head], back_in[:, head : head + 1])
    after2, after_n = both(after, norm)
    two = jnp.concatenate([own2, after2], 0)
    key = lax.broadcasted_iota(jnp.int32, (1, keys_n), 1)
    w2 = jnp.concatenate(halves(wk_ref[...].T), 1)
    total = near_ref[head:]
    for half, ref in enumerate((same_ref, other_ref)):
        z = dot(two, pair(flat(ref, 1)), NT)
        d = jnp.where(key < (y + half * core) * rows, z[: 2 * head] + own_n, 0.0) + (z[2 * head :] + after_n)
        _, _, sig = feature_parts(dot(w2, pair(flat(ref, 0)), NT))
        total += dot2(sig * d[:head] - d[head:], flat(ref, 0))
    sum_ref[:head] = near_ref[:head].T
    sum_ref[head:] = total.T
    chunks = grad_ref.shape[0] - 2 * head
    parts = 2 * head // chunks
    for r in range(parts):
        grad_ref[pl.ds(r, chunks, stride=parts + 1), :] = sum_ref[pl.ds(r, chunks, stride=parts), :]
    grad_ref[pl.ds(parts, chunks, stride=parts + 1), :] = jnp.broadcast_to(loss_ref[0:1], (chunks, head))


VMEM = pl.BlockSpec(memory_space=pltpu.VMEM)


def spread(a, axes, groups):
    copies = jnp.broadcast_to(a[None], (len(groups[0]), *a.shape))
    return lax.all_to_all(copies, axes, 0, 0, tiled=True, axis_index_groups=groups)


def shards(nx, ny, queries, keys, values, w_query, w_key):
    rows, groups, per, head = queries.shape
    n_ctx, n_kvh = lax.axis_size("ctx"), lax.axis_size("kvh")
    scale = head**-0.5
    count = float(rows * n_ctx * groups * n_kvh * per)
    at = lambda x, y, c: (x * ny + y) * CORES + c
    every = [(x, y, c) for x in range(nx) for y in range(ny) for c in range(CORES)]
    y_groups = [[at(x, y, c) for y in range(ny)] for x in range(nx) for c in range(CORES)]
    x_groups = [[at(x, y, c) for x in range(nx)] for y in range(ny) for c in range(CORES)]
    swap = [(at(x, y, c), at(x, y, 1 - c)) for x, y, c in every]
    n, feats, keys_n = rows * per, 2 * head, ny * rows
    f32 = lambda *shape: jax.ShapeDtypeStruct(shape, F32)
    bf16 = lambda *shape: jax.ShapeDtypeStruct(shape, BF16)

    def call(body, outs, args, scratch=(), flops=1, name=None, vmem=20):
        return pl.pallas_call(
            body,
            out_shape=outs,
            in_specs=[VMEM] * len(args),
            out_specs=jax.tree.map(lambda _: VMEM, outs),
            scratch_shapes=list(scratch),
            compiler_params=pltpu.CompilerParams(vmem_limit_bytes=vmem * 1024 * 1024),
            cost_estimate=pl.CostEstimate(
                flops=flops * 1_000_000_000, bytes_accessed=20_000_000, transcendentals=flops * 300_000
            ),
            name=name,
        )(*args)

    q = queries.reshape(n, head)
    k, v = keys.reshape(rows, head), values.reshape(rows, head)
    kvs = call(copies, bf16(ny, 2, rows, head), (k, v), name="copies", vmem=60)
    same = lax.all_to_all(kvs, "ctx", 0, 0, tiled=True, axis_index_groups=y_groups)
    later = [
        lax.ppermute(q, "ctx", [(at(x, y, c), at(x - s, y, c)) for x, y, c in every if x >= s])
        for s in range(1, nx)
    ]
    own = call(
        prepare,
        (f32(n, feats), f32(n, feats)), (q, k, v, w_query, w_key), flops=2, name="prepare",
    )
    same, later, (fq, near) = lax.optimization_barrier((same, later, own))
    other = lax.ppermute(same, "ctx", swap)
    state, full, sums = call(
        functools.partial(same_core, nx, ny, scale),
        (f32(feats, feats), f32(feats, feats), f32(nx - 1, n, feats)), (*later, same, w_key), flops=3, name="same_core",
    )
    pay = call(
        functools.partial(forward, nx, ny, scale),
        bf16(nx, n + feats + 16, head),
        (*later, other, w_key, state, full, sums), flops=4, name="forward",
    )
    got = lax.all_to_all(pay, "ctx", 0, 0, tiled=True, axis_index_groups=x_groups)
    acc, stats = call(
        functools.partial(own_teacher, ny, scale), (f32(n, head), f32(8, n)), (q, same, other), flops=2, name="own_teacher",
    )
    out, dnum, dden, state, back, pay, loss = call(
        functools.partial(merge, nx, ny, scale, count),
        (bf16(n, head), f32(n, head), f32(n, head), f32(feats, feats), f32(feats, feats), bf16(nx, feats + 16, head), f32(8, head)),
        (acc, stats, got, fq, near), flops=2, name="merge",
    )
    got = lax.all_to_all(pay, "ctx", 0, 0, tiled=True, axis_index_groups=x_groups)
    grads = call(
        near_grads, f32(feats, head), (q, k, v, w_query, w_key, dnum, dden, state), flops=2, name="near_grads",
    )
    both_axes = ("ctx", "kvh")
    chips = nx * ny
    chip_groups = [
        [at(x, y, c) * n_kvh + z for x in range(nx) for y in range(ny)] for c in range(CORES) for z in range(n_kvh)
    ]
    rest_groups = [
        [at(x, y, c) * n_kvh + z for c in range(CORES) for z in range(n_kvh)] for x in range(nx) for y in range(ny)
    ]
    parts = feats // chips
    grads = call(
        functools.partial(backward, nx, ny),
        f32(chips * (parts + 1), head),
        (same, other, w_key, back, got, grads, loss),
        scratch=(pltpu.VMEM((feats, head), F32),), flops=4, name="backward",
    )
    mine = lax.all_to_all(
        grads.reshape(chips, 1, -1), both_axes, 0, 0, tiled=True, axis_index_groups=chip_groups
    ).sum(0)
    mine = spread(mine, both_axes, rest_groups).sum(0)
    g = spread(mine[0, : parts * head].reshape(parts, head), both_axes, chip_groups).reshape(2, head, head)
    return out.reshape(queries.shape), g[0], g[1], mine[0, parts * head]


def solution(mesh):
    n_ctx = mesh.shape["ctx"]
    ny = min(8, n_ctx // CORES)
    nx = n_ctx // (CORES * ny)
    placed = (P("ctx", "kvh", None, None), P("ctx", "kvh", None), P("ctx", "kvh", None), P(), P())
    return jax.shard_map(
        functools.partial(shards, nx, ny),
        mesh=mesh,
        in_specs=placed,
        out_specs=(P("ctx", "kvh", None, None), P(), P(), P()),
        check_vma=False,
    )
```

```python
import functools

import jax
import jax.numpy as jnp
from jax import lax
from jax.experimental import pallas as pl
from jax.experimental.pallas import tpu as pltpu
from jax.sharding import PartitionSpec as P

F32, BF16 = jnp.float32, jnp.bfloat16
NN = (((1,), (0,)), ((), ()))
NT = (((1,), (1,)), ((), ()))
LOG2E = 1.4426950408889634
CORES = 2


def dot(a, b, dims=NN):
    return lax.dot_general(a, b, dims, preferred_element_type=F32)


def halves(a):
    high = a.astype(BF16)
    return high, (a - high.astype(F32)).astype(BF16)


def dot3(a, b, dims=NN):
    ah, al = halves(a)
    bh, bl = halves(b)
    return dot(ah, bh, dims) + (dot(ah, bl, dims) + dot(al, bh, dims))


def dot2(a, b, dims=NN):
    ah, al = halves(a)
    return dot(ah, b, dims) + dot(al, b, dims)


def log1p(e):
    return jnp.where(e < 1e-3, e * (1.0 - e * (0.5 - e * (1.0 / 3.0))), jnp.log(1.0 + e))


def feature_parts(pre):
    e = jnp.exp(-jnp.abs(pre))
    t = log1p(e)
    r = 1.0 / (1.0 + e)
    return jnp.maximum(pre, 0.0) + t, jnp.maximum(-pre, 0.0) + t, jnp.where(pre >= 0.0, r, e * r)


def pair(a):
    return jnp.concatenate([a, a], 1)


def with_ones(v):
    return jnp.concatenate([v, jnp.ones_like(v)], 1)


def flat(ref, which):
    blocks, rows, head = ref.shape[0], ref.shape[2], ref.shape[3]
    return ref[:, which].reshape(blocks * rows, head)


def place(ny):
    me = lax.axis_index("ctx")
    return me // (ny * CORES), (me // CORES) % ny, me % CORES


def diagonal(n, rows):
    return lax.broadcasted_iota(jnp.int32, (n, rows), 1) <= (
        lax.broadcasted_iota(jnp.int32, (n, rows), 0) // (n // rows)
    )


def to_rows(pages, head):
    n = pages[0][0].shape[0]
    lane = lax.broadcasted_iota(jnp.int32, (n, head), 1)
    wide = jnp.zeros((n, head), F32)
    for p, columns in enumerate(pages):
        for i, c in enumerate(columns):
            wide = jnp.where(lane == 8 * p + i, c, wide)
    rows = wide.T
    return [
        jnp.concatenate([rows[8 * p : 8 * p + 8, k : k + head] for k in range(0, n, head)], 0).astype(BF16)
        for p in range(len(pages))
    ]


def row_numbers(page):
    return jnp.concatenate([page[k : k + 8] for k in range(0, page.shape[0], 8)], 1).astype(F32)


def to_columns(rows, head):
    return jnp.concatenate(rows + [jnp.zeros((head - len(rows), rows[0].shape[1]), F32)], 0).T


def copies(k_ref, v_ref, out_ref):
    for d in range(out_ref.shape[0]):
        out_ref[d, 0] = k_ref[...]
        out_ref[d, 1] = v_ref[...]


def own_features(q, k, wq, wk):
    wqt = jnp.concatenate(halves(wq.T), 1)
    w2 = jnp.concatenate(halves(wk.T), 1)
    sp, sm, sig_q = feature_parts(dot(wqt, pair(q), NT))
    fq_t = jnp.concatenate([sp, sm], 0)
    sp, sm, sig_k = feature_parts(dot(w2, pair(k), NT))
    return fq_t, sig_q, jnp.concatenate([sp, sm], 0), sig_k


def prepare(q_ref, k_ref, v_ref, wq_ref, wk_ref, fq_ref, near_ref):
    q, k, v = q_ref[...], k_ref[...], v_ref[...]
    fq_t, _, fk_t, _ = own_features(q, k, wq_ref[...], wk_ref[...])
    fq = fq_t.T
    fq_ref[...] = fq
    attn = jnp.where(diagonal(q.shape[0], k.shape[0]), dot3(fq, fk_t), 0.0)
    near_ref[...] = dot2(attn, with_ones(v))


def add_states(keys, vals, w2, seen, part, whole):
    rows = part.shape[0] // 2
    sp, sm, _ = feature_parts(dot(w2, pair(keys), NT))
    both = jnp.concatenate([sp, sm], 0)
    for b in range(keys.shape[0] // rows):
        high, low = halves(both[:, b * rows : (b + 1) * rows])
        values1 = with_ones(vals[b * rows : (b + 1) * rows])
        state = dot(jnp.concatenate([high, low], 1), jnp.concatenate([values1, values1], 0))
        whole += state
        part += state * (b < seen).astype(F32)
    return part, whole


def teach(q, keys0, values0, keys1, values1, scale, masks=None):
    scores0, scores1 = dot(q, keys0, NT), dot(q, keys1, NT)
    if masks is not None:
        scores0 = jnp.where(masks[0], scores0, -1e30)
        scores1 = jnp.where(masks[1], scores1, -1e30)
    best = jnp.maximum(scores0.max(-1, keepdims=True), scores1.max(-1, keepdims=True))
    best = best.astype(BF16).astype(F32)
    c = scale * LOG2E
    return best, dot(jnp.exp2((scores0 - best) * c).astype(BF16), values0) + dot(
        jnp.exp2((scores1 - best) * c).astype(BF16), values1
    )


def own_teacher(q, same, other, y, core, rows, scale, acc_ref, stats_ref):
    n, keys_n = q.shape[0], same[0].shape[0]
    col = lax.broadcasted_iota(jnp.int32, (n, keys_n), 1)
    row = lax.broadcasted_iota(jnp.int32, (n, keys_n), 0) // (n // rows)
    best, accl = teach(q, *same, *other, scale, (col <= row + y * rows, col < (y + core) * rows))
    head = accl.shape[1] // 2
    acc_ref[...] = accl[:, :head]
    lane = lax.broadcasted_iota(jnp.int32, (n, head), 1)
    stats_ref[...] = jnp.where(lane == 0, best, accl[:, head:]).T[:8]


def partial_softmax(q, keys, values1, c):
    scores = dot(q, keys, NT)
    best = scores.max(-1, keepdims=True).astype(BF16).astype(F32)
    return best, dot(jnp.exp2((scores - best) * c).astype(BF16), values1)


def same_core(nx, ny, scale, *refs):
    later = refs[: nx - 1]
    same_ref, wk_ref, state_ref, full_ref, accl_ref = refs[nx - 1 :]
    _, y, _ = place(ny)
    w2 = jnp.concatenate(halves(wk_ref[...].T), 1)
    zero = jnp.zeros(state_ref.shape, F32)
    keys, vals = flat(same_ref, 0), flat(same_ref, 1)
    state_ref[...], full_ref[...] = add_states(keys, vals, w2, y, zero, zero)
    lane = lax.broadcasted_iota(jnp.int32, accl_ref.shape[1:], 1)
    for s in range(nx - 1):
        best, accl = partial_softmax(later[s][...], keys, with_ones(vals), scale * LOG2E)
        accl_ref[s] = jnp.where(lane == accl.shape[1] - 1, best, accl)


def forward(nx, ny, scale, *refs):
    later = refs[: nx - 1]
    q_ref, same_ref, other_ref, wk_ref, state_in, full_in, accl_in, pay_ref, acc_ref, stats_ref = refs[nx - 1 :]
    x, y, core = place(ny)
    head = other_ref.shape[3]
    n = later[0].shape[0]
    c = scale * LOG2E
    w2 = jnp.concatenate(halves(wk_ref[...].T), 1)
    keys, vals = flat(other_ref, 0), flat(other_ref, 1)
    values1 = with_ones(vals)
    state, full = add_states(keys, vals, w2, y + core, state_in[...], full_in[...])
    feats_n = full.shape[0]
    full_high = full[:, :head].astype(BF16)

    own_teacher(
        q_ref[...], (flat(same_ref, 0), with_ones(flat(same_ref, 1))), (keys, values1),
        y, core, other_ref.shape[2], scale, acc_ref, stats_ref,
    )

    def two(column):
        high = column.astype(BF16).astype(F32)
        return [high, column - high]

    high, low = halves(state[:, :head])
    pay_ref[x, :feats_n] = low
    pay_ref[x, n : n + feats_n] = high
    zero = jnp.zeros((n, 1), F32)
    columns = [[zero, zero, zero, *two(state[:, head : head + 1])]]
    sums = []
    for s in range(nx - 1):
        best, accl = partial_softmax(later[s][...], keys, values1, c)
        before = accl_in[s]
        old = before[:, 2 * head - 1 :]
        new = jnp.maximum(old, best)
        mine, other = jnp.exp2((old - new) * c), jnp.exp2((best - new) * c)
        sums.append((before[:, :head] * mine + accl[:, :head] * other).astype(BF16))
        total = before[:, head : head + 1] * mine + accl[:, head : head + 1] * other
        columns.append([new, *two(total), *two(full[:, head : head + 1])])
    rows = to_rows(columns, head)
    pay_ref[x, n + feats_n :] = rows[0]
    for s in range(1, nx):

        @pl.when(x + s < nx)
        def _(s=s):
            pay_ref[x + s, :n] = sums[s - 1]
            pay_ref[x + s, n : n + feats_n] = full_high
            pay_ref[x + s, n + feats_n :] = rows[s]

    for d in range(nx):

        @pl.when(d < x)
        def _(d=d):
            pay_ref[d] = jnp.zeros(pay_ref.shape[1:], BF16)


def merge(
    nx, ny, scale, count,
    acc_in, stats_in, got_ref, fq_ref, near_ref,
    out_ref, dnum_ref, dden_ref, state_ref, back_ref, pay_ref, loss_ref,
):
    x, _, _ = place(ny)
    n, feats_n = fq_ref.shape
    head = out_ref.shape[1]
    c = scale * LOG2E
    pages = [row_numbers(got_ref[d, n + feats_n :]) for d in range(nx)]
    own = stats_in[0:1]
    bests = [jnp.where(d < x, pages[d][0:1], -1e30) for d in range(nx)]
    best = functools.reduce(jnp.maximum, bests, own)
    factors = [jnp.exp2((own - best) * c)]
    total = stats_in[1:2] * factors[0]
    norm = jnp.zeros_like(total)
    for d in range(nx):
        factors.append(jnp.where(d < x, jnp.exp2((bests[d] - best) * c), 0.0))
        total += (pages[d][1:2] + pages[d][2:3]) * factors[d + 1]
        norm += pages[d][3:4] + pages[d][4:5]
    columns = to_columns([f / total for f in factors] + [norm], head)
    targets = acc_in[...] * columns[:, 0:1]
    state = got_ref[x, :feats_n].astype(F32)
    for d in range(nx):
        targets += got_ref[d, :n].astype(F32) * columns[:, d + 1 : d + 2]
        state += got_ref[d, n : n + feats_n].astype(F32)
    targets = targets.astype(BF16).astype(F32)
    norm = columns[:, nx + 1 : nx + 2]
    state = jnp.concatenate([state, jnp.broadcast_to(norm, state.shape)], 1)
    state_ref[...] = state
    fq = fq_ref[...]
    numden = dot3(fq, state) + near_ref[...]
    den = numden[:, head:]
    outs = numden[:, :head] / den
    out_ref[...] = outs.astype(BF16)
    diff = outs - targets
    loss_ref[...] = jnp.full(loss_ref.shape, jnp.sum(diff * diff) / count, F32)
    grad_out = diff * (2.0 / count)
    d_num = grad_out / den
    d_den = -jnp.sum(grad_out * outs, -1, keepdims=True) / den
    dnum_ref[...] = d_num
    dden_ref[...] = d_den
    back = dot3(fq.T, jnp.concatenate([d_num, d_den], 1))
    back_ref[...] = back
    norm = back[:, head : head + 1]
    nh = norm.astype(BF16).astype(F32)
    (rows,) = to_rows([[nh, norm - nh]], head)
    for d in range(nx):
        pay_ref[d, :feats_n] = back[:, :head].astype(BF16)
        pay_ref[d, feats_n:] = rows


def near_grads(q_ref, k_ref, v_ref, wq_ref, wk_ref, dnum_ref, dden_ref, state_ref, grads_ref):
    q, kd, vd = q_ref[...], k_ref[...], v_ref[...]
    head, rows = kd.shape[1], kd.shape[0]
    d_num, d_den = dnum_ref[...], dden_ref[...]
    fq_t, sig_q, fk_t, sig_d = own_features(q, kd, wq_ref[...], wk_ref[...])
    d_attn = jnp.where(diagonal(q.shape[0], rows), dot2(d_num, vd, NT) + d_den[:, :rows], 0.0)
    lane = lax.broadcasted_iota(jnp.int32, d_den.shape, 1)
    d_aug = jnp.concatenate([d_num, jnp.where(lane == 0, d_den, 0.0)], 1)
    d_fq = dot3(state_ref[...], d_aug, NT) + dot3(fk_t, d_attn, NT)
    d_pre = d_fq[:head] * sig_q - d_fq[head:] * (1.0 - sig_q)
    grads_ref[:head] = dot2(d_pre, q)
    d_fk = dot3(fq_t, d_attn)
    d_pre = d_fk[:head] * sig_d - d_fk[head:] * (1.0 - sig_d)
    grads_ref[head:] = dot2(d_pre, kd)


def backward(
    nx, ny,
    same_ref, other_ref, wk_ref, back_in, got_ref, near_ref, loss_ref,
    grad_ref, sum_ref,
):
    x, y, core = place(ny)
    rows, head = same_ref.shape[2], same_ref.shape[3]
    keys_n = ny * rows
    feats_n = back_in.shape[0]
    after, norm = jnp.zeros((feats_n, head), F32), jnp.zeros((1, feats_n), F32)
    for d in range(nx):
        counts = (d > x).astype(F32)
        after += got_ref[d, :feats_n].astype(F32) * counts
        page = row_numbers(got_ref[d, feats_n:])
        norm += (page[0:1] + page[1:2]) * counts
    norm = to_columns([norm], head)[:, 0:1]

    def both(state, norm):
        mats = jnp.concatenate([state[:head] + state[head:], state[head:]], 0)
        norms = jnp.concatenate([norm[:head] + norm[head:], norm[head:]], 0)
        return jnp.concatenate(halves(mats), 1), norms

    own2, own_n = both(back_in[:, :head], back_in[:, head : head + 1])
    after2, after_n = both(after, norm)
    two = jnp.concatenate([own2, after2], 0)
    key = lax.broadcasted_iota(jnp.int32, (1, keys_n), 1)
    w2 = jnp.concatenate(halves(wk_ref[...].T), 1)
    total = near_ref[head:]
    for half, ref in enumerate((same_ref, other_ref)):
        z = dot(two, pair(flat(ref, 1)), NT)
        d = jnp.where(key < (y + half * core) * rows, z[: 2 * head] + own_n, 0.0) + (z[2 * head :] + after_n)
        _, _, sig = feature_parts(dot(w2, pair(flat(ref, 0)), NT))
        total += dot2(sig * d[:head] - d[head:], flat(ref, 0))
    sum_ref[:head] = near_ref[:head].T
    sum_ref[head:] = total.T
    chunks = grad_ref.shape[0] - 2 * head
    parts = 2 * head // chunks
    for r in range(parts):
        grad_ref[pl.ds(r, chunks, stride=parts + 1), :] = sum_ref[pl.ds(r, chunks, stride=parts), :]
    grad_ref[pl.ds(parts, chunks, stride=parts + 1), :] = jnp.broadcast_to(loss_ref[0:1], (chunks, head))


VMEM = pl.BlockSpec(memory_space=pltpu.VMEM)


def spread(a, axes, groups):
    copies = jnp.broadcast_to(a[None], (len(groups[0]), *a.shape))
    return lax.all_to_all(copies, axes, 0, 0, tiled=True, axis_index_groups=groups)


def shards(nx, ny, queries, keys, values, w_query, w_key):
    rows, groups, per, head = queries.shape
    n_ctx, n_kvh = lax.axis_size("ctx"), lax.axis_size("kvh")
    scale = head**-0.5
    count = float(rows * n_ctx * groups * n_kvh * per)
    at = lambda x, y, c: (x * ny + y) * CORES + c
    every = [(x, y, c) for x in range(nx) for y in range(ny) for c in range(CORES)]
    y_groups = [[at(x, y, c) for y in range(ny)] for x in range(nx) for c in range(CORES)]
    x_groups = [[at(x, y, c) for x in range(nx)] for y in range(ny) for c in range(CORES)]
    swap = [(at(x, y, c), at(x, y, 1 - c)) for x, y, c in every]
    n, feats, keys_n = rows * per, 2 * head, ny * rows
    f32 = lambda *shape: jax.ShapeDtypeStruct(shape, F32)
    bf16 = lambda *shape: jax.ShapeDtypeStruct(shape, BF16)

    def call(body, outs, args, scratch=(), flops=1, name=None, vmem=20):
        return pl.pallas_call(
            body,
            out_shape=outs,
            in_specs=[VMEM] * len(args),
            out_specs=jax.tree.map(lambda _: VMEM, outs),
            scratch_shapes=list(scratch),
            compiler_params=pltpu.CompilerParams(vmem_limit_bytes=vmem * 1024 * 1024),
            cost_estimate=pl.CostEstimate(
                flops=flops * 1_000_000_000, bytes_accessed=20_000_000, transcendentals=flops * 300_000
            ),
            name=name,
        )(*args)

    q = queries.reshape(n, head)
    k, v = keys.reshape(rows, head), values.reshape(rows, head)
    kvs = call(copies, bf16(ny, 2, rows, head), (k, v), name="copies", vmem=60)
    same = lax.all_to_all(kvs, "ctx", 0, 0, tiled=True, axis_index_groups=y_groups)
    later = [
        lax.ppermute(q, "ctx", [(at(x, y, c), at(x - s, y, c)) for x, y, c in every if x >= s])
        for s in range(1, nx)
    ]
    own = call(
        prepare,
        (f32(n, feats), f32(n, feats)), (q, k, v, w_query, w_key), flops=2, name="prepare",
    )
    same, later, (fq, near) = lax.optimization_barrier((same, later, own))
    other = lax.ppermute(same, "ctx", swap)
    state, full, sums = call(
        functools.partial(same_core, nx, ny, scale),
        (f32(feats, feats), f32(feats, feats), f32(nx - 1, n, feats)), (*later, same, w_key), flops=3, name="same_core",
    )
    pay, acc, stats = call(
        functools.partial(forward, nx, ny, scale),
        (bf16(nx, n + feats + 16, head), f32(n, head), f32(8, n)),
        (*later, q, same, other, w_key, state, full, sums), flops=6, name="forward",
    )
    got = lax.all_to_all(pay, "ctx", 0, 0, tiled=True, axis_index_groups=x_groups)
    out, dnum, dden, state, back, pay, loss = call(
        functools.partial(merge, nx, ny, scale, count),
        (bf16(n, head), f32(n, head), f32(n, head), f32(feats, feats), f32(feats, feats), bf16(nx, feats + 16, head), f32(8, head)),
        (acc, stats, got, fq, near), flops=2, name="merge",
    )
    got = lax.all_to_all(pay, "ctx", 0, 0, tiled=True, axis_index_groups=x_groups)
    grads = call(
        near_grads, f32(feats, head), (q, k, v, w_query, w_key, dnum, dden, state), flops=2, name="near_grads",
    )
    both_axes = ("ctx", "kvh")
    chips = nx * ny
    chip_groups = [
        [at(x, y, c) * n_kvh + z for x in range(nx) for y in range(ny)] for c in range(CORES) for z in range(n_kvh)
    ]
    rest_groups = [
        [at(x, y, c) * n_kvh + z for c in range(CORES) for z in range(n_kvh)] for x in range(nx) for y in range(ny)
    ]
    parts = feats // chips
    grads = call(
        functools.partial(backward, nx, ny),
        f32(chips * (parts + 1), head),
        (same, other, w_key, back, got, grads, loss),
        scratch=(pltpu.VMEM((feats, head), F32),), flops=4, name="backward",
    )
    mine = lax.all_to_all(
        grads.reshape(chips, 1, -1), both_axes, 0, 0, tiled=True, axis_index_groups=chip_groups
    ).sum(0)
    mine = spread(mine, both_axes, rest_groups).sum(0)
    g = spread(mine[0, : parts * head].reshape(parts, head), both_axes, chip_groups).reshape(2, head, head)
    return out.reshape(queries.shape), g[0], g[1], mine[0, parts * head]


def solution(mesh):
    n_ctx = mesh.shape["ctx"]
    ny = min(8, n_ctx // CORES)
    nx = n_ctx // (CORES * ny)
    placed = (P("ctx", "kvh", None, None), P("ctx", "kvh", None), P("ctx", "kvh", None), P(), P())
    return jax.shard_map(
        functools.partial(shards, nx, ny),
        mesh=mesh,
        in_specs=placed,
        out_specs=(P("ctx", "kvh", None, None), P(), P(), P()),
        check_vma=False,
    )
```

```python
import functools

import jax
import jax.numpy as jnp
from jax import lax
from jax.experimental import pallas as pl
from jax.experimental.pallas import tpu as pltpu
from jax.sharding import PartitionSpec as P

F32, BF16 = jnp.float32, jnp.bfloat16
NN = (((1,), (0,)), ((), ()))
NT = (((1,), (1,)), ((), ()))
LOG2E = 1.4426950408889634
CORES = 2


def dot(a, b, dims=NN):
    return lax.dot_general(a, b, dims, preferred_element_type=F32)


def halves(a):
    high = a.astype(BF16)
    return high, (a - high.astype(F32)).astype(BF16)


def dot3(a, b, dims=NN):
    ah, al = halves(a)
    bh, bl = halves(b)
    return dot(ah, bh, dims) + (dot(ah, bl, dims) + dot(al, bh, dims))


def dot2(a, b, dims=NN):
    ah, al = halves(a)
    return dot(ah, b, dims) + dot(al, b, dims)


def log1p(e):
    return jnp.where(e < 1e-3, e * (1.0 - e * (0.5 - e * (1.0 / 3.0))), jnp.log(1.0 + e))


def feature_parts(pre):
    e = jnp.exp(-jnp.abs(pre))
    t = log1p(e)
    r = 1.0 / (1.0 + e)
    return jnp.maximum(pre, 0.0) + t, jnp.maximum(-pre, 0.0) + t, jnp.where(pre >= 0.0, r, e * r)


def pair(a):
    return jnp.concatenate([a, a], 1)


def with_ones(v):
    return jnp.concatenate([v, jnp.ones_like(v)], 1)


def flat(ref, which):
    blocks, rows, head = ref.shape[0], ref.shape[2], ref.shape[3]
    return ref[:, which].reshape(blocks * rows, head)


def place(ny):
    me = lax.axis_index("ctx")
    return me // (ny * CORES), (me // CORES) % ny, me % CORES


def diagonal(n, rows):
    return lax.broadcasted_iota(jnp.int32, (n, rows), 1) <= (
        lax.broadcasted_iota(jnp.int32, (n, rows), 0) // (n // rows)
    )


def to_rows(pages, head):
    n = pages[0][0].shape[0]
    lane = lax.broadcasted_iota(jnp.int32, (n, head), 1)
    wide = jnp.zeros((n, head), F32)
    for p, columns in enumerate(pages):
        for i, c in enumerate(columns):
            wide = jnp.where(lane == 8 * p + i, c, wide)
    rows = wide.T
    return [
        jnp.concatenate([rows[8 * p : 8 * p + 8, k : k + head] for k in range(0, n, head)], 0).astype(BF16)
        for p in range(len(pages))
    ]


def row_numbers(page):
    return jnp.concatenate([page[k : k + 8] for k in range(0, page.shape[0], 8)], 1).astype(F32)


def to_columns(rows, head):
    return jnp.concatenate(rows + [jnp.zeros((head - len(rows), rows[0].shape[1]), F32)], 0).T


def copies(k_ref, v_ref, out_ref):
    for d in range(out_ref.shape[0]):
        out_ref[d, 0] = k_ref[...]
        out_ref[d, 1] = v_ref[...]


def own_features(q, k, wq, wk):
    wqt = jnp.concatenate(halves(wq.T), 1)
    w2 = jnp.concatenate(halves(wk.T), 1)
    sp, sm, sig_q = feature_parts(dot(wqt, pair(q), NT))
    fq_t = jnp.concatenate([sp, sm], 0)
    sp, sm, sig_k = feature_parts(dot(w2, pair(k), NT))
    return fq_t, sig_q, jnp.concatenate([sp, sm], 0), sig_k


def prepare(q_ref, k_ref, v_ref, wq_ref, wk_ref, fq_ref, near_ref):
    q, k, v = q_ref[...], k_ref[...], v_ref[...]
    fq_t, _, fk_t, _ = own_features(q, k, wq_ref[...], wk_ref[...])
    fq = fq_t.T
    fq_ref[...] = fq
    attn = jnp.where(diagonal(q.shape[0], k.shape[0]), dot3(fq, fk_t), 0.0)
    near_ref[...] = dot2(attn, with_ones(v))


def add_states(keys, vals, w2, seen, part, whole):
    rows = part.shape[0] // 2
    sp, sm, _ = feature_parts(dot(w2, pair(keys), NT))
    both = jnp.concatenate([sp, sm], 0)
    for b in range(keys.shape[0] // rows):
        high, low = halves(both[:, b * rows : (b + 1) * rows])
        values1 = with_ones(vals[b * rows : (b + 1) * rows])
        state = dot(jnp.concatenate([high, low], 1), jnp.concatenate([values1, values1], 0))
        whole += state
        part += state * (b < seen).astype(F32)
    return part, whole


def teach(q, keys0, values0, keys1, values1, scale, masks=None):
    scores0, scores1 = dot(q, keys0, NT), dot(q, keys1, NT)
    if masks is not None:
        scores0 = jnp.where(masks[0], scores0, -1e30)
        scores1 = jnp.where(masks[1], scores1, -1e30)
    best = jnp.maximum(scores0.max(-1, keepdims=True), scores1.max(-1, keepdims=True))
    best = best.astype(BF16).astype(F32)
    c = scale * LOG2E
    return best, dot(jnp.exp2((scores0 - best) * c).astype(BF16), values0) + dot(
        jnp.exp2((scores1 - best) * c).astype(BF16), values1
    )


def own_teacher(q, same, other, y, core, rows, scale, acc_ref, stats_ref):
    n, keys_n = q.shape[0], same[0].shape[0]
    col = lax.broadcasted_iota(jnp.int32, (n, keys_n), 1)
    row = lax.broadcasted_iota(jnp.int32, (n, keys_n), 0) // (n // rows)
    best, accl = teach(q, *same, *other, scale, (col <= row + y * rows, col < (y + core) * rows))
    head = accl.shape[1] // 2
    acc_ref[...] = accl[:, :head]
    lane = lax.broadcasted_iota(jnp.int32, (n, head), 1)
    stats_ref[...] = jnp.where(lane == 0, best, accl[:, head:]).T[:8]


def partial_softmax(q, keys, values1, c):
    scores = dot(q, keys, NT)
    best = scores.max(-1, keepdims=True).astype(BF16).astype(F32)
    return best, dot(jnp.exp2((scores - best) * c).astype(BF16), values1)


def same_core(nx, ny, scale, *refs):
    later = refs[: nx - 1]
    same_ref, wk_ref, state_ref, full_ref, accl_ref = refs[nx - 1 :]
    _, y, _ = place(ny)
    w2 = jnp.concatenate(halves(wk_ref[...].T), 1)
    zero = jnp.zeros(state_ref.shape, F32)
    keys, vals = flat(same_ref, 0), flat(same_ref, 1)
    state_ref[...], full_ref[...] = add_states(keys, vals, w2, y, zero, zero)
    lane = lax.broadcasted_iota(jnp.int32, accl_ref.shape[1:], 1)
    for s in range(nx - 1):
        best, accl = partial_softmax(later[s][...], keys, with_ones(vals), scale * LOG2E)
        accl_ref[s] = jnp.where(lane == accl.shape[1] - 1, best, accl)


def forward(nx, ny, scale, *refs):
    later = refs[: nx - 1]
    q_ref, same_ref, other_ref, wk_ref, state_in, full_in, accl_in, pay_ref, acc_ref, stats_ref = refs[nx - 1 :]
    x, y, core = place(ny)
    head = other_ref.shape[3]
    n = later[0].shape[0]
    c = scale * LOG2E
    w2 = jnp.concatenate(halves(wk_ref[...].T), 1)
    keys, vals = flat(other_ref, 0), flat(other_ref, 1)
    values1 = with_ones(vals)
    state, full = add_states(keys, vals, w2, y + core, state_in[...], full_in[...])
    feats_n = full.shape[0]
    full_high = full[:, :head].astype(BF16)

    own_teacher(
        q_ref[...], (flat(same_ref, 0), with_ones(flat(same_ref, 1))), (keys, values1),
        y, core, other_ref.shape[2], scale, acc_ref, stats_ref,
    )

    def two(column):
        high = column.astype(BF16).astype(F32)
        return [high, column - high]

    high, low = halves(state[:, :head])
    pay_ref[x, :feats_n] = low
    pay_ref[x, n : n + feats_n] = high
    zero = jnp.zeros((n, 1), F32)
    columns = [[zero, zero, zero, *two(state[:, head : head + 1])]]
    sums = []
    for s in range(nx - 1):
        best, accl = partial_softmax(later[s][...], keys, values1, c)
        before = accl_in[s]
        old = before[:, 2 * head - 1 :]
        new = jnp.maximum(old, best)
        mine, other = jnp.exp2((old - new) * c), jnp.exp2((best - new) * c)
        sums.append((before[:, :head] * mine + accl[:, :head] * other).astype(BF16))
        total = before[:, head : head + 1] * mine + accl[:, head : head + 1] * other
        columns.append([new, *two(total), *two(full[:, head : head + 1])])
    rows = to_rows(columns, head)
    pay_ref[x, n + feats_n :] = rows[0]
    for s in range(1, nx):

        @pl.when(x + s < nx)
        def _(s=s):
            pay_ref[x + s, :n] = sums[s - 1]
            pay_ref[x + s, n : n + feats_n] = full_high
            pay_ref[x + s, n + feats_n :] = rows[s]

    for d in range(nx):

        @pl.when(d < x)
        def _(d=d):
            pay_ref[d] = jnp.zeros(pay_ref.shape[1:], BF16)


def merge(
    nx, ny, scale, count,
    acc_in, stats_in, got_ref, fq_ref, near_ref,
    out_ref, dnum_ref, dden_ref, state_ref, back_ref, pay_ref, loss_ref,
):
    x, _, _ = place(ny)
    n, feats_n = fq_ref.shape
    head = out_ref.shape[1]
    c = scale * LOG2E
    pages = [row_numbers(got_ref[d, n + feats_n :]) for d in range(nx)]
    own = stats_in[0:1]
    bests = [jnp.where(d < x, pages[d][0:1], -1e30) for d in range(nx)]
    best = functools.reduce(jnp.maximum, bests, own)
    factors = [jnp.exp2((own - best) * c)]
    total = stats_in[1:2] * factors[0]
    norm = jnp.zeros_like(total)
    for d in range(nx):
        factors.append(jnp.where(d < x, jnp.exp2((bests[d] - best) * c), 0.0))
        total += (pages[d][1:2] + pages[d][2:3]) * factors[d + 1]
        norm += pages[d][3:4] + pages[d][4:5]
    columns = to_columns([f / total for f in factors] + [norm], head)
    targets = acc_in[...] * columns[:, 0:1]
    state = got_ref[x, :feats_n].astype(F32)
    for d in range(nx):
        targets += got_ref[d, :n].astype(F32) * columns[:, d + 1 : d + 2]
        state += got_ref[d, n : n + feats_n].astype(F32)
    targets = targets.astype(BF16).astype(F32)
    norm = columns[:, nx + 1 : nx + 2]
    state = jnp.concatenate([state, jnp.broadcast_to(norm, state.shape)], 1)
    state_ref[...] = state
    fq = fq_ref[...]
    numden = dot3(fq, state) + near_ref[...]
    den = numden[:, head:]
    outs = numden[:, :head] / den
    out_ref[...] = outs.astype(BF16)
    diff = outs - targets
    loss_ref[...] = jnp.full(loss_ref.shape, jnp.sum(diff * diff) / count, F32)
    grad_out = diff * (2.0 / count)
    d_num = grad_out / den
    d_den = -jnp.sum(grad_out * outs, -1, keepdims=True) / den
    dnum_ref[...] = d_num
    dden_ref[...] = d_den
    back = dot3(fq.T, jnp.concatenate([d_num, d_den], 1))
    back_ref[...] = back
    norm = back[:, head : head + 1]
    nh = norm.astype(BF16).astype(F32)
    (rows,) = to_rows([[nh, norm - nh]], head)
    for d in range(nx):
        pay_ref[d, :feats_n] = back[:, :head].astype(BF16)
        pay_ref[d, feats_n:] = rows


def near_grads(q, kd, vd, wq, wk, d_num, d_den, state):
    head, rows = kd.shape[1], kd.shape[0]
    fq_t, sig_q, fk_t, sig_d = own_features(q, kd, wq, wk)
    d_attn = jnp.where(diagonal(q.shape[0], rows), dot2(d_num, vd, NT) + d_den[:, :rows], 0.0)
    lane = lax.broadcasted_iota(jnp.int32, d_den.shape, 1)
    d_aug = jnp.concatenate([d_num, jnp.where(lane == 0, d_den, 0.0)], 1)
    d_fq = dot3(state, d_aug, NT) + dot3(fk_t, d_attn, NT)
    d_pre = d_fq[:head] * sig_q - d_fq[head:] * (1.0 - sig_q)
    grad_q = dot2(d_pre, q)
    d_fk = dot3(fq_t, d_attn)
    d_pre = d_fk[:head] * sig_d - d_fk[head:] * (1.0 - sig_d)
    return grad_q, dot2(d_pre, kd)


def backward(
    nx, ny,
    same_ref, other_ref, q_ref, k_ref, v_ref, wq_ref, wk_ref, dnum_ref, dden_ref, state_ref, back_in, got_ref, loss_ref,
    grad_ref, sum_ref,
):
    x, y, core = place(ny)
    rows, head = same_ref.shape[2], same_ref.shape[3]
    keys_n = ny * rows
    feats_n = back_in.shape[0]
    after, norm = jnp.zeros((feats_n, head), F32), jnp.zeros((1, feats_n), F32)
    for d in range(nx):
        counts = (d > x).astype(F32)
        after += got_ref[d, :feats_n].astype(F32) * counts
        page = row_numbers(got_ref[d, feats_n:])
        norm += (page[0:1] + page[1:2]) * counts
    norm = to_columns([norm], head)[:, 0:1]

    def both(state, norm):
        mats = jnp.concatenate([state[:head] + state[head:], state[head:]], 0)
        norms = jnp.concatenate([norm[:head] + norm[head:], norm[head:]], 0)
        return jnp.concatenate(halves(mats), 1), norms

    own2, own_n = both(back_in[:, :head], back_in[:, head : head + 1])
    after2, after_n = both(after, norm)
    two = jnp.concatenate([own2, after2], 0)
    key = lax.broadcasted_iota(jnp.int32, (1, keys_n), 1)
    w2 = jnp.concatenate(halves(wk_ref[...].T), 1)
    grad_q, total = near_grads(
        q_ref[...], k_ref[...], v_ref[...], wq_ref[...], wk_ref[...], dnum_ref[...], dden_ref[...], state_ref[...]
    )
    for half, ref in enumerate((same_ref, other_ref)):
        z = dot(two, pair(flat(ref, 1)), NT)
        d = jnp.where(key < (y + half * core) * rows, z[: 2 * head] + own_n, 0.0) + (z[2 * head :] + after_n)
        _, _, sig = feature_parts(dot(w2, pair(flat(ref, 0)), NT))
        total += dot2(sig * d[:head] - d[head:], flat(ref, 0))
    sum_ref[:head] = grad_q.T
    sum_ref[head:] = total.T
    chunks = grad_ref.shape[0] - 2 * head
    parts = 2 * head // chunks
    for r in range(parts):
        grad_ref[pl.ds(r, chunks, stride=parts + 1), :] = sum_ref[pl.ds(r, chunks, stride=parts), :]
    grad_ref[pl.ds(parts, chunks, stride=parts + 1), :] = jnp.broadcast_to(loss_ref[0:1], (chunks, head))


VMEM = pl.BlockSpec(memory_space=pltpu.VMEM)


def spread(a, axes, groups):
    copies = jnp.broadcast_to(a[None], (len(groups[0]), *a.shape))
    return lax.all_to_all(copies, axes, 0, 0, tiled=True, axis_index_groups=groups)


def shards(nx, ny, queries, keys, values, w_query, w_key):
    rows, groups, per, head = queries.shape
    n_ctx, n_kvh = lax.axis_size("ctx"), lax.axis_size("kvh")
    scale = head**-0.5
    count = float(rows * n_ctx * groups * n_kvh * per)
    at = lambda x, y, c: (x * ny + y) * CORES + c
    every = [(x, y, c) for x in range(nx) for y in range(ny) for c in range(CORES)]
    y_groups = [[at(x, y, c) for y in range(ny)] for x in range(nx) for c in range(CORES)]
    x_groups = [[at(x, y, c) for x in range(nx)] for y in range(ny) for c in range(CORES)]
    swap = [(at(x, y, c), at(x, y, 1 - c)) for x, y, c in every]
    n, feats, keys_n = rows * per, 2 * head, ny * rows
    f32 = lambda *shape: jax.ShapeDtypeStruct(shape, F32)
    bf16 = lambda *shape: jax.ShapeDtypeStruct(shape, BF16)

    def call(body, outs, args, scratch=(), flops=1, name=None, vmem=20):
        return pl.pallas_call(
            body,
            out_shape=outs,
            in_specs=[VMEM] * len(args),
            out_specs=jax.tree.map(lambda _: VMEM, outs),
            scratch_shapes=list(scratch),
            compiler_params=pltpu.CompilerParams(vmem_limit_bytes=vmem * 1024 * 1024),
            cost_estimate=pl.CostEstimate(
                flops=flops * 1_000_000_000, bytes_accessed=20_000_000, transcendentals=flops * 300_000
            ),
            name=name,
        )(*args)

    q = queries.reshape(n, head)
    k, v = keys.reshape(rows, head), values.reshape(rows, head)
    kvs = call(copies, bf16(ny, 2, rows, head), (k, v), name="copies", vmem=60)
    same = lax.all_to_all(kvs, "ctx", 0, 0, tiled=True, axis_index_groups=y_groups)
    later = [
        lax.ppermute(q, "ctx", [(at(x, y, c), at(x - s, y, c)) for x, y, c in every if x >= s])
        for s in range(1, nx)
    ]
    own = call(
        prepare,
        (f32(n, feats), f32(n, feats)), (q, k, v, w_query, w_key), flops=2, name="prepare",
    )
    same, later, (fq, near) = lax.optimization_barrier((same, later, own))
    other = lax.ppermute(same, "ctx", swap)
    state, full, sums = call(
        functools.partial(same_core, nx, ny, scale),
        (f32(feats, feats), f32(feats, feats), f32(nx - 1, n, feats)), (*later, same, w_key), flops=3, name="same_core",
    )
    pay, acc, stats = call(
        functools.partial(forward, nx, ny, scale),
        (bf16(nx, n + feats + 16, head), f32(n, head), f32(8, n)),
        (*later, q, same, other, w_key, state, full, sums), flops=6, name="forward",
    )
    got = lax.all_to_all(pay, "ctx", 0, 0, tiled=True, axis_index_groups=x_groups)
    out, dnum, dden, state, back, pay, loss = call(
        functools.partial(merge, nx, ny, scale, count),
        (bf16(n, head), f32(n, head), f32(n, head), f32(feats, feats), f32(feats, feats), bf16(nx, feats + 16, head), f32(8, head)),
        (acc, stats, got, fq, near), flops=2, name="merge",
    )
    got = lax.all_to_all(pay, "ctx", 0, 0, tiled=True, axis_index_groups=x_groups)
    both_axes = ("ctx", "kvh")
    chips = nx * ny
    chip_groups = [
        [at(x, y, c) * n_kvh + z for x in range(nx) for y in range(ny)] for c in range(CORES) for z in range(n_kvh)
    ]
    rest_groups = [
        [at(x, y, c) * n_kvh + z for c in range(CORES) for z in range(n_kvh)] for x in range(nx) for y in range(ny)
    ]
    parts = feats // chips
    grads = call(
        functools.partial(backward, nx, ny),
        f32(chips * (parts + 1), head),
        (same, other, q, k, v, w_query, w_key, dnum, dden, state, back, got, loss),
        scratch=(pltpu.VMEM((feats, head), F32),), flops=4, name="backward",
    )
    mine = lax.all_to_all(
        grads.reshape(chips, 1, -1), both_axes, 0, 0, tiled=True, axis_index_groups=chip_groups
    ).sum(0)
    mine = spread(mine, both_axes, rest_groups).sum(0)
    g = spread(mine[0, : parts * head].reshape(parts, head), both_axes, chip_groups).reshape(2, head, head)
    return out.reshape(queries.shape), g[0], g[1], mine[0, parts * head]


def solution(mesh):
    n_ctx = mesh.shape["ctx"]
    ny = min(8, n_ctx // CORES)
    nx = n_ctx // (CORES * ny)
    placed = (P("ctx", "kvh", None, None), P("ctx", "kvh", None), P("ctx", "kvh", None), P(), P())
    return jax.shard_map(
        functools.partial(shards, nx, ny),
        mesh=mesh,
        in_specs=placed,
        out_specs=(P("ctx", "kvh", None, None), P(), P(), P()),
        check_vma=False,
    )
```

```python
import functools

import jax
import jax.numpy as jnp
from jax import lax
from jax.experimental import pallas as pl
from jax.experimental.pallas import tpu as pltpu
from jax.sharding import PartitionSpec as P

F32, BF16 = jnp.float32, jnp.bfloat16
NN = (((1,), (0,)), ((), ()))
NT = (((1,), (1,)), ((), ()))
LOG2E = 1.4426950408889634
CORES = 2


def dot(a, b, dims=NN):
    return lax.dot_general(a, b, dims, preferred_element_type=F32)


def halves(a):
    high = a.astype(BF16)
    return high, (a - high.astype(F32)).astype(BF16)


def dot3(a, b, dims=NN):
    ah, al = halves(a)
    bh, bl = halves(b)
    return dot(ah, bh, dims) + (dot(ah, bl, dims) + dot(al, bh, dims))


def dot2(a, b, dims=NN):
    ah, al = halves(a)
    return dot(ah, b, dims) + dot(al, b, dims)


def log1p(e):
    return jnp.where(e < 1e-3, e * (1.0 - e * (0.5 - e * (1.0 / 3.0))), jnp.log(1.0 + e))


def feature_parts(pre):
    e = jnp.exp(-jnp.abs(pre))
    t = log1p(e)
    r = 1.0 / (1.0 + e)
    return jnp.maximum(pre, 0.0) + t, jnp.maximum(-pre, 0.0) + t, jnp.where(pre >= 0.0, r, e * r)


def pair(a):
    return jnp.concatenate([a, a], 1)


def with_ones(v):
    return jnp.concatenate([v, jnp.ones_like(v)], 1)


def flat(ref, which):
    blocks, rows, head = ref.shape[0], ref.shape[2], ref.shape[3]
    return ref[:, which].reshape(blocks * rows, head)


def place(ny):
    me = lax.axis_index("ctx")
    return me // (ny * CORES), (me // CORES) % ny, me % CORES


def diagonal(n, rows):
    return lax.broadcasted_iota(jnp.int32, (n, rows), 1) <= (
        lax.broadcasted_iota(jnp.int32, (n, rows), 0) // (n // rows)
    )


def to_rows(pages, head):
    n = pages[0][0].shape[0]
    lane = lax.broadcasted_iota(jnp.int32, (n, head), 1)
    wide = jnp.zeros((n, head), F32)
    for p, columns in enumerate(pages):
        for i, c in enumerate(columns):
            wide = jnp.where(lane == 8 * p + i, c, wide)
    rows = wide.T
    return [
        jnp.concatenate([rows[8 * p : 8 * p + 8, k : k + head] for k in range(0, n, head)], 0).astype(BF16)
        for p in range(len(pages))
    ]


def row_numbers(page):
    return jnp.concatenate([page[k : k + 8] for k in range(0, page.shape[0], 8)], 1).astype(F32)


def to_columns(rows, head):
    return jnp.concatenate(rows + [jnp.zeros((head - len(rows), rows[0].shape[1]), F32)], 0).T


def copies(k_ref, v_ref, out_ref):
    for d in range(out_ref.shape[0]):
        out_ref[d, 0] = k_ref[...]
        out_ref[d, 1] = v_ref[...]


def own_features(q, k, wq, wk):
    wqt = jnp.concatenate(halves(wq.T), 1)
    w2 = jnp.concatenate(halves(wk.T), 1)
    sp, sm, sig_q = feature_parts(dot(wqt, pair(q), NT))
    fq_t = jnp.concatenate([sp, sm], 0)
    sp, sm, sig_k = feature_parts(dot(w2, pair(k), NT))
    return fq_t, sig_q, jnp.concatenate([sp, sm], 0), sig_k


def prepare(q_ref, k_ref, v_ref, wq_ref, wk_ref, fq_ref, near_ref):
    q, k, v = q_ref[...], k_ref[...], v_ref[...]
    fq_t, _, fk_t, _ = own_features(q, k, wq_ref[...], wk_ref[...])
    fq = fq_t.T
    fq_ref[...] = fq
    attn = jnp.where(diagonal(q.shape[0], k.shape[0]), dot3(fq, fk_t), 0.0)
    near_ref[...] = dot2(attn, with_ones(v))


def add_states(keys, vals, w2, seen, part, whole):
    rows = part.shape[0] // 2
    sp, sm, _ = feature_parts(dot(w2, pair(keys), NT))
    both = jnp.concatenate([sp, sm], 0)
    for b in range(keys.shape[0] // rows):
        high, low = halves(both[:, b * rows : (b + 1) * rows])
        values1 = with_ones(vals[b * rows : (b + 1) * rows])
        state = dot(jnp.concatenate([high, low], 1), jnp.concatenate([values1, values1], 0))
        whole += state
        part += state * (b < seen).astype(F32)
    return part, whole


def teach(q, keys0, values0, keys1, values1, scale, masks=None):
    scores0, scores1 = dot(q, keys0, NT), dot(q, keys1, NT)
    if masks is not None:
        scores0 = jnp.where(masks[0], scores0, -1e30)
        scores1 = jnp.where(masks[1], scores1, -1e30)
    best = jnp.maximum(scores0.max(-1, keepdims=True), scores1.max(-1, keepdims=True))
    best = best.astype(BF16).astype(F32)
    c = scale * LOG2E
    return best, dot(jnp.exp2((scores0 - best) * c).astype(BF16), values0) + dot(
        jnp.exp2((scores1 - best) * c).astype(BF16), values1
    )


def own_teacher(q, same, other, y, core, rows, scale, acc_ref, stats_ref):
    n, keys_n = q.shape[0], same[0].shape[0]
    col = lax.broadcasted_iota(jnp.int32, (n, keys_n), 1)
    row = lax.broadcasted_iota(jnp.int32, (n, keys_n), 0) // (n // rows)
    best, accl = teach(q, *same, *other, scale, (col <= row + y * rows, col < (y + core) * rows))
    head = accl.shape[1] // 2
    acc_ref[...] = accl[:, :head]
    lane = lax.broadcasted_iota(jnp.int32, (n, head), 1)
    stats_ref[...] = jnp.where(lane == 0, best, accl[:, head:]).T[:8]


def partial_softmax(q, keys, values1, c):
    scores = dot(q, keys, NT)
    best = scores.max(-1, keepdims=True).astype(BF16).astype(F32)
    return best, dot(jnp.exp2((scores - best) * c).astype(BF16), values1)


def same_core(nx, ny, scale, *refs):
    later = refs[: nx - 1]
    same_ref, wk_ref, state_ref, full_ref, accl_ref = refs[nx - 1 :]
    _, y, _ = place(ny)
    w2 = jnp.concatenate(halves(wk_ref[...].T), 1)
    zero = jnp.zeros(state_ref.shape, F32)
    keys, vals = flat(same_ref, 0), flat(same_ref, 1)
    state_ref[...], full_ref[...] = add_states(keys, vals, w2, y, zero, zero)
    lane = lax.broadcasted_iota(jnp.int32, accl_ref.shape[1:], 1)
    for s in range(nx - 1):
        best, accl = partial_softmax(later[s][...], keys, with_ones(vals), scale * LOG2E)
        accl_ref[s] = jnp.where(lane == accl.shape[1] - 1, best, accl)


def forward(nx, ny, scale, *refs):
    later = refs[: nx - 1]
    q_ref, same_ref, other_ref, wk_ref, state_in, full_in, accl_in, acc_ref, stats_ref, own_ref, *page_refs = refs[nx - 1 :]
    x, y, core = place(ny)
    head = other_ref.shape[3]
    n = later[0].shape[0]
    c = scale * LOG2E
    w2 = jnp.concatenate(halves(wk_ref[...].T), 1)
    keys, vals = flat(other_ref, 0), flat(other_ref, 1)
    values1 = with_ones(vals)
    state, full = add_states(keys, vals, w2, y + core, state_in[...], full_in[...])
    feats_n = full.shape[0]
    full_high = full[:, :head].astype(BF16)

    own_teacher(
        q_ref[...], (flat(same_ref, 0), with_ones(flat(same_ref, 1))), (keys, values1),
        y, core, other_ref.shape[2], scale, acc_ref, stats_ref,
    )

    def two(column):
        high = column.astype(BF16).astype(F32)
        return [high, column - high]

    high, low = halves(state[:, :head])
    own_ref[:feats_n] = low
    own_ref[n : n + feats_n] = high
    zero = jnp.zeros((n, 1), F32)
    columns = [[zero, zero, zero, *two(state[:, head : head + 1])]]
    sums = []
    for s in range(nx - 1):
        best, accl = partial_softmax(later[s][...], keys, values1, c)
        before = accl_in[s]
        old = before[:, 2 * head - 1 :]
        new = jnp.maximum(old, best)
        mine, other = jnp.exp2((old - new) * c), jnp.exp2((best - new) * c)
        sums.append((before[:, :head] * mine + accl[:, :head] * other).astype(BF16))
        total = before[:, head : head + 1] * mine + accl[:, head : head + 1] * other
        columns.append([new, *two(total), *two(full[:, head : head + 1])])
    rows = to_rows(columns, head)
    own_ref[n + feats_n :] = rows[0]
    for s in range(1, nx):
        page_refs[s - 1][:n] = sums[s - 1]
        page_refs[s - 1][n : n + feats_n] = full_high
        page_refs[s - 1][n + feats_n :] = rows[s]


def merge(nx, ny, scale, count, *refs):
    got = refs[:nx]
    (
        acc_in, stats_in, fq_ref, near_ref,
        out_ref, dnum_ref, dden_ref, state_ref, back_ref, pay_ref, loss_ref,
    ) = refs[nx:]
    x, _, _ = place(ny)
    n, feats_n = fq_ref.shape
    head = out_ref.shape[1]
    c = scale * LOG2E
    pages = [row_numbers(page[n + feats_n :]) for page in got]
    own = stats_in[0:1]
    bests = [jnp.where(s <= x, pages[s][0:1], -1e30) for s in range(1, nx)]
    best = functools.reduce(jnp.maximum, bests, own)
    factors = [jnp.exp2((own - best) * c)]
    total = stats_in[1:2] * factors[0]
    norm = pages[0][3:4] + pages[0][4:5]
    for s in range(1, nx):
        factors.append(jnp.where(s <= x, jnp.exp2((bests[s - 1] - best) * c), 0.0))
        total += (pages[s][1:2] + pages[s][2:3]) * factors[s]
        norm += pages[s][3:4] + pages[s][4:5]
    columns = to_columns([f / total for f in factors] + [norm], head)
    targets = acc_in[...] * columns[:, 0:1]
    state = got[0][:feats_n].astype(F32) + got[0][n : n + feats_n].astype(F32)
    for s in range(1, nx):
        targets += got[s][:n].astype(F32) * columns[:, s : s + 1]
        state += got[s][n : n + feats_n].astype(F32)
    targets = targets.astype(BF16).astype(F32)
    norm = columns[:, nx : nx + 1]
    state = jnp.concatenate([state, jnp.broadcast_to(norm, state.shape)], 1)
    state_ref[...] = state
    fq = fq_ref[...]
    numden = dot3(fq, state) + near_ref[...]
    den = numden[:, head:]
    outs = numden[:, :head] / den
    out_ref[...] = outs.astype(BF16)
    diff = outs - targets
    loss_ref[...] = jnp.full(loss_ref.shape, jnp.sum(diff * diff) / count, F32)
    grad_out = diff * (2.0 / count)
    d_num = grad_out / den
    d_den = -jnp.sum(grad_out * outs, -1, keepdims=True) / den
    dnum_ref[...] = d_num
    dden_ref[...] = d_den
    back = dot3(fq.T, jnp.concatenate([d_num, d_den], 1))
    back_ref[...] = back
    norm = back[:, head : head + 1]
    nh = norm.astype(BF16).astype(F32)
    (rows,) = to_rows([[nh, norm - nh]], head)
    for d in range(nx):
        pay_ref[d, :feats_n] = back[:, :head].astype(BF16)
        pay_ref[d, feats_n:] = rows


def near_grads(q_ref, k_ref, v_ref, wq_ref, wk_ref, dnum_ref, dden_ref, state_ref, grads_ref):
    q, kd, vd = q_ref[...], k_ref[...], v_ref[...]
    head, rows = kd.shape[1], kd.shape[0]
    d_num, d_den = dnum_ref[...], dden_ref[...]
    fq_t, sig_q, fk_t, sig_d = own_features(q, kd, wq_ref[...], wk_ref[...])
    d_attn = jnp.where(diagonal(q.shape[0], rows), dot2(d_num, vd, NT) + d_den[:, :rows], 0.0)
    lane = lax.broadcasted_iota(jnp.int32, d_den.shape, 1)
    d_aug = jnp.concatenate([d_num, jnp.where(lane == 0, d_den, 0.0)], 1)
    d_fq = dot3(state_ref[...], d_aug, NT) + dot3(fk_t, d_attn, NT)
    d_pre = d_fq[:head] * sig_q - d_fq[head:] * (1.0 - sig_q)
    grads_ref[:head] = dot2(d_pre, q)
    d_fk = dot3(fq_t, d_attn)
    d_pre = d_fk[:head] * sig_d - d_fk[head:] * (1.0 - sig_d)
    grads_ref[head:] = dot2(d_pre, kd)


def backward(
    nx, ny,
    same_ref, other_ref, wk_ref, back_in, got_ref, near_ref, loss_ref,
    grad_ref, sum_ref,
):
    x, y, core = place(ny)
    rows, head = same_ref.shape[2], same_ref.shape[3]
    keys_n = ny * rows
    feats_n = back_in.shape[0]
    after, norm = jnp.zeros((feats_n, head), F32), jnp.zeros((1, feats_n), F32)
    for d in range(nx):
        counts = (d > x).astype(F32)
        after += got_ref[d, :feats_n].astype(F32) * counts
        page = row_numbers(got_ref[d, feats_n:])
        norm += (page[0:1] + page[1:2]) * counts
    norm = to_columns([norm], head)[:, 0:1]

    def both(state, norm):
        mats = jnp.concatenate([state[:head] + state[head:], state[head:]], 0)
        norms = jnp.concatenate([norm[:head] + norm[head:], norm[head:]], 0)
        return jnp.concatenate(halves(mats), 1), norms

    own2, own_n = both(back_in[:, :head], back_in[:, head : head + 1])
    after2, after_n = both(after, norm)
    two = jnp.concatenate([own2, after2], 0)
    key = lax.broadcasted_iota(jnp.int32, (1, keys_n), 1)
    w2 = jnp.concatenate(halves(wk_ref[...].T), 1)
    total = near_ref[head:]
    for half, ref in enumerate((same_ref, other_ref)):
        z = dot(two, pair(flat(ref, 1)), NT)
        d = jnp.where(key < (y + half * core) * rows, z[: 2 * head] + own_n, 0.0) + (z[2 * head :] + after_n)
        _, _, sig = feature_parts(dot(w2, pair(flat(ref, 0)), NT))
        total += dot2(sig * d[:head] - d[head:], flat(ref, 0))
    sum_ref[:head] = near_ref[:head].T
    sum_ref[head:] = total.T
    chunks = grad_ref.shape[0] - 2 * head
    parts = 2 * head // chunks
    for r in range(parts):
        grad_ref[pl.ds(r, chunks, stride=parts + 1), :] = sum_ref[pl.ds(r, chunks, stride=parts), :]
    grad_ref[pl.ds(parts, chunks, stride=parts + 1), :] = jnp.broadcast_to(loss_ref[0:1], (chunks, head))


VMEM = pl.BlockSpec(memory_space=pltpu.VMEM)


def spread(a, axes, groups):
    copies = jnp.broadcast_to(a[None], (len(groups[0]), *a.shape))
    return lax.all_to_all(copies, axes, 0, 0, tiled=True, axis_index_groups=groups)


def shards(nx, ny, queries, keys, values, w_query, w_key):
    rows, groups, per, head = queries.shape
    n_ctx, n_kvh = lax.axis_size("ctx"), lax.axis_size("kvh")
    scale = head**-0.5
    count = float(rows * n_ctx * groups * n_kvh * per)
    at = lambda x, y, c: (x * ny + y) * CORES + c
    every = [(x, y, c) for x in range(nx) for y in range(ny) for c in range(CORES)]
    y_groups = [[at(x, y, c) for y in range(ny)] for x in range(nx) for c in range(CORES)]
    x_groups = [[at(x, y, c) for x in range(nx)] for y in range(ny) for c in range(CORES)]
    swap = [(at(x, y, c), at(x, y, 1 - c)) for x, y, c in every]
    n, feats, keys_n = rows * per, 2 * head, ny * rows
    f32 = lambda *shape: jax.ShapeDtypeStruct(shape, F32)
    bf16 = lambda *shape: jax.ShapeDtypeStruct(shape, BF16)

    def call(body, outs, args, scratch=(), flops=1, name=None, vmem=20):
        return pl.pallas_call(
            body,
            out_shape=outs,
            in_specs=[VMEM] * len(args),
            out_specs=jax.tree.map(lambda _: VMEM, outs),
            scratch_shapes=list(scratch),
            compiler_params=pltpu.CompilerParams(vmem_limit_bytes=vmem * 1024 * 1024),
            cost_estimate=pl.CostEstimate(
                flops=flops * 1_000_000_000, bytes_accessed=20_000_000, transcendentals=flops * 300_000
            ),
            name=name,
        )(*args)

    q = queries.reshape(n, head)
    k, v = keys.reshape(rows, head), values.reshape(rows, head)
    kvs = call(copies, bf16(ny, 2, rows, head), (k, v), name="copies", vmem=60)
    same = lax.all_to_all(kvs, "ctx", 0, 0, tiled=True, axis_index_groups=y_groups)
    later = [
        lax.ppermute(q, "ctx", [(at(x, y, c), at(x - s, y, c)) for x, y, c in every if x >= s])
        for s in range(1, nx)
    ]
    own = call(
        prepare,
        (f32(n, feats), f32(n, feats)), (q, k, v, w_query, w_key), flops=2, name="prepare",
    )
    same, later, (fq, near) = lax.optimization_barrier((same, later, own))
    other = lax.ppermute(same, "ctx", swap)
    state, full, sums = call(
        functools.partial(same_core, nx, ny, scale),
        (f32(feats, feats), f32(feats, feats), f32(nx - 1, n, feats)), (*later, same, w_key), flops=3, name="same_core",
    )
    acc, stats, mine, *pages = call(
        functools.partial(forward, nx, ny, scale),
        (f32(n, head), f32(8, n), *[bf16(n + feats + 16, head)] * nx),
        (*later, q, same, other, w_key, state, full, sums), flops=6, name="forward",
    )
    got = [mine] + [
        lax.ppermute(a, "ctx", [(at(x, y, c), at(x + s, y, c)) for x, y, c in every if x + s < nx])
        for s, a in enumerate(pages, 1)
    ]
    out, dnum, dden, state, back, pay, loss = call(
        functools.partial(merge, nx, ny, scale, count),
        (bf16(n, head), f32(n, head), f32(n, head), f32(feats, feats), f32(feats, feats), bf16(nx, feats + 16, head), f32(8, head)),
        (*got, acc, stats, fq, near), flops=2, name="merge",
    )
    got = lax.all_to_all(pay, "ctx", 0, 0, tiled=True, axis_index_groups=x_groups)
    grads = call(
        near_grads, f32(feats, head), (q, k, v, w_query, w_key, dnum, dden, state), flops=2, name="near_grads",
    )
    both_axes = ("ctx", "kvh")
    chips = nx * ny
    chip_groups = [
        [at(x, y, c) * n_kvh + z for x in range(nx) for y in range(ny)] for c in range(CORES) for z in range(n_kvh)
    ]
    rest_groups = [
        [at(x, y, c) * n_kvh + z for c in range(CORES) for z in range(n_kvh)] for x in range(nx) for y in range(ny)
    ]
    parts = feats // chips
    grads = call(
        functools.partial(backward, nx, ny),
        f32(chips * (parts + 1), head),
        (same, other, w_key, back, got, grads, loss),
        scratch=(pltpu.VMEM((feats, head), F32),), flops=4, name="backward",
    )
    mine = lax.all_to_all(
        grads.reshape(chips, 1, -1), both_axes, 0, 0, tiled=True, axis_index_groups=chip_groups
    ).sum(0)
    mine = spread(mine, both_axes, rest_groups).sum(0)
    g = spread(mine[0, : parts * head].reshape(parts, head), both_axes, chip_groups).reshape(2, head, head)
    return out.reshape(queries.shape), g[0], g[1], mine[0, parts * head]


def solution(mesh):
    n_ctx = mesh.shape["ctx"]
    ny = min(8, n_ctx // CORES)
    nx = n_ctx // (CORES * ny)
    placed = (P("ctx", "kvh", None, None), P("ctx", "kvh", None), P("ctx", "kvh", None), P(), P())
    return jax.shard_map(
        functools.partial(shards, nx, ny),
        mesh=mesh,
        in_specs=placed,
        out_specs=(P("ctx", "kvh", None, None), P(), P(), P()),
        check_vma=False,
    )
```

```python
import functools

import jax
import jax.numpy as jnp
from jax import lax
from jax.experimental import pallas as pl
from jax.experimental.pallas import tpu as pltpu
from jax.sharding import PartitionSpec as P

F32, BF16 = jnp.float32, jnp.bfloat16
NN = (((1,), (0,)), ((), ()))
NT = (((1,), (1,)), ((), ()))
LOG2E = 1.4426950408889634
CORES = 2


def dot(a, b, dims=NN):
    return lax.dot_general(a, b, dims, preferred_element_type=F32)


def halves(a):
    high = a.astype(BF16)
    return high, (a - high.astype(F32)).astype(BF16)


def dot3(a, b, dims=NN):
    ah, al = halves(a)
    bh, bl = halves(b)
    return dot(ah, bh, dims) + (dot(ah, bl, dims) + dot(al, bh, dims))


def dot2(a, b, dims=NN):
    ah, al = halves(a)
    return dot(ah, b, dims) + dot(al, b, dims)


def log1p(e):
    return jnp.where(e < 1e-3, e * (1.0 - e * (0.5 - e * (1.0 / 3.0))), jnp.log(1.0 + e))


def feature_parts(pre):
    e = jnp.exp(-jnp.abs(pre))
    t = log1p(e)
    r = 1.0 / (1.0 + e)
    return jnp.maximum(pre, 0.0) + t, jnp.maximum(-pre, 0.0) + t, jnp.where(pre >= 0.0, r, e * r)


def pair(a):
    return jnp.concatenate([a, a], 1)


def with_ones(v):
    return jnp.concatenate([v, jnp.ones_like(v)], 1)


def flat(ref, which):
    blocks, rows, head = ref.shape[0], ref.shape[2], ref.shape[3]
    return ref[:, which].reshape(blocks * rows, head)


def place(ny):
    me = lax.axis_index("ctx")
    return me // (ny * CORES), (me // CORES) % ny, me % CORES


def diagonal(n, rows):
    return lax.broadcasted_iota(jnp.int32, (n, rows), 1) <= (
        lax.broadcasted_iota(jnp.int32, (n, rows), 0) // (n // rows)
    )


def to_rows(pages, head):
    n = pages[0][0].shape[0]
    lane = lax.broadcasted_iota(jnp.int32, (n, head), 1)
    wide = jnp.zeros((n, head), F32)
    for p, columns in enumerate(pages):
        for i, c in enumerate(columns):
            wide = jnp.where(lane == 8 * p + i, c, wide)
    rows = wide.T
    return [
        jnp.concatenate([rows[8 * p : 8 * p + 8, k : k + head] for k in range(0, n, head)], 0).astype(BF16)
        for p in range(len(pages))
    ]


def row_numbers(page):
    return jnp.concatenate([page[k : k + 8] for k in range(0, page.shape[0], 8)], 1).astype(F32)


def to_columns(rows, head):
    return jnp.concatenate(rows + [jnp.zeros((head - len(rows), rows[0].shape[1]), F32)], 0).T


def copies(k_ref, v_ref, out_ref, sems):
    moves = [
        pltpu.make_async_copy(ref, out_ref.at[d, i], sems.at[d, i])
        for d in range(out_ref.shape[0])
        for i, ref in enumerate((k_ref, v_ref))
    ]
    for move in moves:
        move.start()
    for move in moves:
        move.wait()


def own_features(q, k, wq, wk):
    wqt = jnp.concatenate(halves(wq.T), 1)
    w2 = jnp.concatenate(halves(wk.T), 1)
    sp, sm, sig_q = feature_parts(dot(wqt, pair(q), NT))
    fq_t = jnp.concatenate([sp, sm], 0)
    sp, sm, sig_k = feature_parts(dot(w2, pair(k), NT))
    return fq_t, sig_q, jnp.concatenate([sp, sm], 0), sig_k


def prepare(q_ref, k_ref, v_ref, wq_ref, wk_ref, fq_ref, near_ref):
    q, k, v = q_ref[...], k_ref[...], v_ref[...]
    fq_t, _, fk_t, _ = own_features(q, k, wq_ref[...], wk_ref[...])
    fq = fq_t.T
    fq_ref[...] = fq
    attn = jnp.where(diagonal(q.shape[0], k.shape[0]), dot3(fq, fk_t), 0.0)
    near_ref[...] = dot2(attn, with_ones(v))


def add_states(keys, vals, w2, seen, part, whole):
    rows = part.shape[0] // 2
    sp, sm, _ = feature_parts(dot(w2, pair(keys), NT))
    both = jnp.concatenate([sp, sm], 0)
    for b in range(keys.shape[0] // rows):
        high, low = halves(both[:, b * rows : (b + 1) * rows])
        values1 = with_ones(vals[b * rows : (b + 1) * rows])
        state = dot(jnp.concatenate([high, low], 1), jnp.concatenate([values1, values1], 0))
        whole += state
        part += state * (b < seen).astype(F32)
    return part, whole


def teach(q, keys0, values0, keys1, values1, scale, masks=None):
    scores0, scores1 = dot(q, keys0, NT), dot(q, keys1, NT)
    if masks is not None:
        scores0 = jnp.where(masks[0], scores0, -1e30)
        scores1 = jnp.where(masks[1], scores1, -1e30)
    best = jnp.maximum(scores0.max(-1, keepdims=True), scores1.max(-1, keepdims=True))
    best = best.astype(BF16).astype(F32)
    c = scale * LOG2E
    return best, dot(jnp.exp2((scores0 - best) * c).astype(BF16), values0) + dot(
        jnp.exp2((scores1 - best) * c).astype(BF16), values1
    )


def own_teacher(q, same, other, y, core, rows, scale, acc_ref, stats_ref):
    n, keys_n = q.shape[0], same[0].shape[0]
    col = lax.broadcasted_iota(jnp.int32, (n, keys_n), 1)
    row = lax.broadcasted_iota(jnp.int32, (n, keys_n), 0) // (n // rows)
    best, accl = teach(q, *same, *other, scale, (col <= row + y * rows, col < (y + core) * rows))
    head = accl.shape[1] // 2
    acc_ref[...] = accl[:, :head]
    lane = lax.broadcasted_iota(jnp.int32, (n, head), 1)
    stats_ref[...] = jnp.where(lane == 0, best, accl[:, head:]).T[:8]


def partial_softmax(q, keys, values1, c):
    scores = dot(q, keys, NT)
    best = scores.max(-1, keepdims=True).astype(BF16).astype(F32)
    return best, dot(jnp.exp2((scores - best) * c).astype(BF16), values1)


def same_core(nx, ny, scale, *refs):
    later = refs[: nx - 1]
    same_ref, wk_ref, state_ref, full_ref, accl_ref = refs[nx - 1 :]
    _, y, _ = place(ny)
    w2 = jnp.concatenate(halves(wk_ref[...].T), 1)
    zero = jnp.zeros(state_ref.shape, F32)
    keys, vals = flat(same_ref, 0), flat(same_ref, 1)
    state_ref[...], full_ref[...] = add_states(keys, vals, w2, y, zero, zero)
    lane = lax.broadcasted_iota(jnp.int32, accl_ref.shape[1:], 1)
    for s in range(nx - 1):
        best, accl = partial_softmax(later[s][...], keys, with_ones(vals), scale * LOG2E)
        accl_ref[s] = jnp.where(lane == accl.shape[1] - 1, best, accl)


def forward(nx, ny, scale, *refs):
    later = refs[: nx - 1]
    q_ref, same_ref, other_ref, wk_ref, state_in, full_in, accl_in, pay_ref, acc_ref, stats_ref = refs[nx - 1 :]
    x, y, core = place(ny)
    head = other_ref.shape[3]
    n = later[0].shape[0]
    c = scale * LOG2E
    w2 = jnp.concatenate(halves(wk_ref[...].T), 1)
    keys, vals = flat(other_ref, 0), flat(other_ref, 1)
    values1 = with_ones(vals)
    state, full = add_states(keys, vals, w2, y + core, state_in[...], full_in[...])
    feats_n = full.shape[0]
    full_high = full[:, :head].astype(BF16)

    own_teacher(
        q_ref[...], (flat(same_ref, 0), with_ones(flat(same_ref, 1))), (keys, values1),
        y, core, other_ref.shape[2], scale, acc_ref, stats_ref,
    )

    def two(column):
        high = column.astype(BF16).astype(F32)
        return [high, column - high]

    high, low = halves(state[:, :head])
    pay_ref[x, :feats_n] = low
    pay_ref[x, n : n + feats_n] = high
    zero = jnp.zeros((n, 1), F32)
    columns = [[zero, zero, zero, *two(state[:, head : head + 1])]]
    sums = []
    for s in range(nx - 1):
        best, accl = partial_softmax(later[s][...], keys, values1, c)
        before = accl_in[s]
        old = before[:, 2 * head - 1 :]
        new = jnp.maximum(old, best)
        mine, other = jnp.exp2((old - new) * c), jnp.exp2((best - new) * c)
        sums.append((before[:, :head] * mine + accl[:, :head] * other).astype(BF16))
        total = before[:, head : head + 1] * mine + accl[:, head : head + 1] * other
        columns.append([new, *two(total), *two(full[:, head : head + 1])])
    rows = to_rows(columns, head)
    pay_ref[x, n + feats_n :] = rows[0]
    for s in range(1, nx):

        @pl.when(x + s < nx)
        def _(s=s):
            pay_ref[x + s, :n] = sums[s - 1]
            pay_ref[x + s, n : n + feats_n] = full_high
            pay_ref[x + s, n + feats_n :] = rows[s]

    for d in range(nx):

        @pl.when(d < x)
        def _(d=d):
            pay_ref[d] = jnp.zeros(pay_ref.shape[1:], BF16)


def merge(
    nx, ny, scale, count,
    acc_in, stats_in, got_ref, fq_ref, near_ref,
    out_ref, dnum_ref, dden_ref, state_ref, back_ref, pay_ref, loss_ref,
):
    x, _, _ = place(ny)
    n, feats_n = fq_ref.shape
    head = out_ref.shape[1]
    c = scale * LOG2E
    pages = [row_numbers(got_ref[d, n + feats_n :]) for d in range(nx)]
    own = stats_in[0:1]
    bests = [jnp.where(d < x, pages[d][0:1], -1e30) for d in range(nx)]
    best = functools.reduce(jnp.maximum, bests, own)
    factors = [jnp.exp2((own - best) * c)]
    total = stats_in[1:2] * factors[0]
    norm = jnp.zeros_like(total)
    for d in range(nx):
        factors.append(jnp.where(d < x, jnp.exp2((bests[d] - best) * c), 0.0))
        total += (pages[d][1:2] + pages[d][2:3]) * factors[d + 1]
        norm += pages[d][3:4] + pages[d][4:5]
    columns = to_columns([f / total for f in factors] + [norm], head)
    targets = acc_in[...] * columns[:, 0:1]
    state = got_ref[x, :feats_n].astype(F32)
    for d in range(nx):
        targets += got_ref[d, :n].astype(F32) * columns[:, d + 1 : d + 2]
        state += got_ref[d, n : n + feats_n].astype(F32)
    targets = targets.astype(BF16).astype(F32)
    norm = columns[:, nx + 1 : nx + 2]
    state = jnp.concatenate([state, jnp.broadcast_to(norm, state.shape)], 1)
    state_ref[...] = state
    fq = fq_ref[...]
    numden = dot3(fq, state) + near_ref[...]
    den = numden[:, head:]
    outs = numden[:, :head] / den
    out_ref[...] = outs.astype(BF16)
    diff = outs - targets
    loss_ref[...] = jnp.full(loss_ref.shape, jnp.sum(diff * diff) / count, F32)
    grad_out = diff * (2.0 / count)
    d_num = grad_out / den
    d_den = -jnp.sum(grad_out * outs, -1, keepdims=True) / den
    dnum_ref[...] = d_num
    dden_ref[...] = d_den
    back = dot3(fq.T, jnp.concatenate([d_num, d_den], 1))
    back_ref[...] = back
    norm = back[:, head : head + 1]
    nh = norm.astype(BF16).astype(F32)
    (rows,) = to_rows([[nh, norm - nh]], head)
    for d in range(nx):
        pay_ref[d, :feats_n] = back[:, :head].astype(BF16)
        pay_ref[d, feats_n:] = rows


def near_grads(q_ref, k_ref, v_ref, wq_ref, wk_ref, dnum_ref, dden_ref, state_ref, grads_ref):
    q, kd, vd = q_ref[...], k_ref[...], v_ref[...]
    head, rows = kd.shape[1], kd.shape[0]
    d_num, d_den = dnum_ref[...], dden_ref[...]
    fq_t, sig_q, fk_t, sig_d = own_features(q, kd, wq_ref[...], wk_ref[...])
    d_attn = jnp.where(diagonal(q.shape[0], rows), dot2(d_num, vd, NT) + d_den[:, :rows], 0.0)
    lane = lax.broadcasted_iota(jnp.int32, d_den.shape, 1)
    d_aug = jnp.concatenate([d_num, jnp.where(lane == 0, d_den, 0.0)], 1)
    d_fq = dot3(state_ref[...], d_aug, NT) + dot3(fk_t, d_attn, NT)
    d_pre = d_fq[:head] * sig_q - d_fq[head:] * (1.0 - sig_q)
    grads_ref[:head] = dot2(d_pre, q)
    d_fk = dot3(fq_t, d_attn)
    d_pre = d_fk[:head] * sig_d - d_fk[head:] * (1.0 - sig_d)
    grads_ref[head:] = dot2(d_pre, kd)


def backward(
    nx, ny,
    same_ref, other_ref, wk_ref, back_in, got_ref, near_ref, loss_ref,
    grad_ref, sum_ref,
):
    x, y, core = place(ny)
    rows, head = same_ref.shape[2], same_ref.shape[3]
    keys_n = ny * rows
    feats_n = back_in.shape[0]
    after, norm = jnp.zeros((feats_n, head), F32), jnp.zeros((1, feats_n), F32)
    for d in range(nx):
        counts = (d > x).astype(F32)
        after += got_ref[d, :feats_n].astype(F32) * counts
        page = row_numbers(got_ref[d, feats_n:])
        norm += (page[0:1] + page[1:2]) * counts
    norm = to_columns([norm], head)[:, 0:1]

    def both(state, norm):
        mats = jnp.concatenate([state[:head] + state[head:], state[head:]], 0)
        norms = jnp.concatenate([norm[:head] + norm[head:], norm[head:]], 0)
        return jnp.concatenate(halves(mats), 1), norms

    own2, own_n = both(back_in[:, :head], back_in[:, head : head + 1])
    after2, after_n = both(after, norm)
    two = jnp.concatenate([own2, after2], 0)
    key = lax.broadcasted_iota(jnp.int32, (1, keys_n), 1)
    w2 = jnp.concatenate(halves(wk_ref[...].T), 1)
    total = near_ref[head:]
    for half, ref in enumerate((same_ref, other_ref)):
        z = dot(two, pair(flat(ref, 1)), NT)
        d = jnp.where(key < (y + half * core) * rows, z[: 2 * head] + own_n, 0.0) + (z[2 * head :] + after_n)
        _, _, sig = feature_parts(dot(w2, pair(flat(ref, 0)), NT))
        total += dot2(sig * d[:head] - d[head:], flat(ref, 0))
    sum_ref[:head] = near_ref[:head].T
    sum_ref[head:] = total.T
    chunks = grad_ref.shape[0] - 2 * head
    parts = 2 * head // chunks
    for r in range(parts):
        grad_ref[pl.ds(r, chunks, stride=parts + 1), :] = sum_ref[pl.ds(r, chunks, stride=parts), :]
    grad_ref[pl.ds(parts, chunks, stride=parts + 1), :] = jnp.broadcast_to(loss_ref[0:1], (chunks, head))


VMEM = pl.BlockSpec(memory_space=pltpu.VMEM)


def spread(a, axes, groups):
    copies = jnp.broadcast_to(a[None], (len(groups[0]), *a.shape))
    return lax.all_to_all(copies, axes, 0, 0, tiled=True, axis_index_groups=groups)


def shards(nx, ny, queries, keys, values, w_query, w_key):
    rows, groups, per, head = queries.shape
    n_ctx, n_kvh = lax.axis_size("ctx"), lax.axis_size("kvh")
    scale = head**-0.5
    count = float(rows * n_ctx * groups * n_kvh * per)
    at = lambda x, y, c: (x * ny + y) * CORES + c
    every = [(x, y, c) for x in range(nx) for y in range(ny) for c in range(CORES)]
    y_groups = [[at(x, y, c) for y in range(ny)] for x in range(nx) for c in range(CORES)]
    x_groups = [[at(x, y, c) for x in range(nx)] for y in range(ny) for c in range(CORES)]
    swap = [(at(x, y, c), at(x, y, 1 - c)) for x, y, c in every]
    n, feats, keys_n = rows * per, 2 * head, ny * rows
    f32 = lambda *shape: jax.ShapeDtypeStruct(shape, F32)
    bf16 = lambda *shape: jax.ShapeDtypeStruct(shape, BF16)

    def call(body, outs, args, scratch=(), flops=1, name=None, vmem=20):
        return pl.pallas_call(
            body,
            out_shape=outs,
            in_specs=[VMEM] * len(args),
            out_specs=jax.tree.map(lambda _: VMEM, outs),
            scratch_shapes=list(scratch),
            compiler_params=pltpu.CompilerParams(vmem_limit_bytes=vmem * 1024 * 1024),
            cost_estimate=pl.CostEstimate(
                flops=flops * 1_000_000_000, bytes_accessed=20_000_000, transcendentals=flops * 300_000
            ),
            name=name,
        )(*args)

    q = queries.reshape(n, head)
    k, v = keys.reshape(rows, head), values.reshape(rows, head)
    kvs = pl.pallas_call(
        copies,
        out_shape=bf16(ny, 2, rows, head),
        in_specs=[VMEM] * 2,
        out_specs=pl.BlockSpec(memory_space=pl.ANY),
        scratch_shapes=[pltpu.SemaphoreType.DMA((ny, 2))],
        compiler_params=pltpu.CompilerParams(vmem_limit_bytes=60 * 1024 * 1024),
        name="copies",
    )(k, v)
    same = lax.all_to_all(kvs, "ctx", 0, 0, tiled=True, axis_index_groups=y_groups)
    later = [
        lax.ppermute(q, "ctx", [(at(x, y, c), at(x - s, y, c)) for x, y, c in every if x >= s])
        for s in range(1, nx)
    ]
    own = call(
        prepare,
        (f32(n, feats), f32(n, feats)), (q, k, v, w_query, w_key), flops=2, name="prepare",
    )
    same, later, (fq, near) = lax.optimization_barrier((same, later, own))
    other = lax.ppermute(same, "ctx", swap)
    state, full, sums = call(
        functools.partial(same_core, nx, ny, scale),
        (f32(feats, feats), f32(feats, feats), f32(nx - 1, n, feats)), (*later, same, w_key), flops=3, name="same_core",
    )
    pay, acc, stats = call(
        functools.partial(forward, nx, ny, scale),
        (bf16(nx, n + feats + 16, head), f32(n, head), f32(8, n)),
        (*later, q, same, other, w_key, state, full, sums), flops=6, name="forward",
    )
    got = lax.all_to_all(pay, "ctx", 0, 0, tiled=True, axis_index_groups=x_groups)
    out, dnum, dden, state, back, pay, loss = call(
        functools.partial(merge, nx, ny, scale, count),
        (bf16(n, head), f32(n, head), f32(n, head), f32(feats, feats), f32(feats, feats), bf16(nx, feats + 16, head), f32(8, head)),
        (acc, stats, got, fq, near), flops=2, name="merge",
    )
    got = lax.all_to_all(pay, "ctx", 0, 0, tiled=True, axis_index_groups=x_groups)
    grads = call(
        near_grads, f32(feats, head), (q, k, v, w_query, w_key, dnum, dden, state), flops=2, name="near_grads",
    )
    both_axes = ("ctx", "kvh")
    chips = nx * ny
    chip_groups = [
        [at(x, y, c) * n_kvh + z for x in range(nx) for y in range(ny)] for c in range(CORES) for z in range(n_kvh)
    ]
    rest_groups = [
        [at(x, y, c) * n_kvh + z for c in range(CORES) for z in range(n_kvh)] for x in range(nx) for y in range(ny)
    ]
    parts = feats // chips
    grads = call(
        functools.partial(backward, nx, ny),
        f32(chips * (parts + 1), head),
        (same, other, w_key, back, got, grads, loss),
        scratch=(pltpu.VMEM((feats, head), F32),), flops=4, name="backward",
    )
    mine = lax.all_to_all(
        grads.reshape(chips, 1, -1), both_axes, 0, 0, tiled=True, axis_index_groups=chip_groups
    ).sum(0)
    mine = spread(mine, both_axes, rest_groups).sum(0)
    mine, loss = lax.optimization_barrier((mine, mine[0, parts * head]))
    g = spread(mine[0, : parts * head].reshape(parts, head), both_axes, chip_groups).reshape(2, head, head)
    return out.reshape(queries.shape), g[0], g[1], loss


def solution(mesh):
    n_ctx = mesh.shape["ctx"]
    ny = min(8, n_ctx // CORES)
    nx = n_ctx // (CORES * ny)
    placed = (P("ctx", "kvh", None, None), P("ctx", "kvh", None), P("ctx", "kvh", None), P(), P())
    return jax.shard_map(
        functools.partial(shards, nx, ny),
        mesh=mesh,
        in_specs=placed,
        out_specs=(P("ctx", "kvh", None, None), P(), P(), P()),
        check_vma=False,
    )
```
